32 devices in a mesh: passage: 8 (over z, y), tile: 4 (over x, core).
Axes of the slice: x: 2, y: 2, z: 4, core: 2. Of those that a mesh axis runs over, the one named last changes fastest.
Arguments:
- gas: float32 [2048, 8192], P('passage', 'tile'), may hold values from -6 to 6
- gas_speed: float32 [2048, 8192], P('passage', 'tile'), may hold values from 0.2 to 0.7
- solid: float32 [2048, 8192], P('passage', 'tile'), may hold values from -6 to 6
- material: int32 [2048, 8192], P('passage', 'tile'), may hold values from 0 to 2
- face_cell: int32 [131072], P(('passage', 'tile')), may hold values from 0 to 524287
- face_owner: int32 [131072, 1], P(('passage', 'tile')), may hold values from 0 to 31; in each aligned block of 4096 rows (0 to 4095, 4096 to 8191, ...) at most 256 rows name the same one
- face_surface: int32 [131072], P(('passage', 'tile')), may hold values from 0 to 4095
- film: float32 [131072], P(('passage', 'tile')), may hold values from 0.1 to 1
- wall_previous: float32 [131072], P(('passage', 'tile')), may hold values from -6 to 6
Outputs:
- gas_next: float32 [2048, 8192], P('passage', 'tile')
- solid_next: float32 [2048, 8192], P('passage', 'tile')
- wall_temps: float32 [131072], P(('passage', 'tile'))
The draws below stay inside these ranges and needn't reach their ends.
Inputs may be any that keep to these rules, and one draw needn't show every extreme that they name: `face_owner`: among the 4096 faces of one gas tile, at most 256 name the same owner, and in some tile one owner is named by exactly 256 faces.
All inputs are finite; a program needn't handle non-finite values.
Results may differ from the reference program's by a relative error of at most 0.00002.
Values sent between devices are 32-bit elements; how exact they have to be, the bound alone decides.
No kernel may reach another device: no remote copies, remote signals or barrier semaphores. Data moves between devices by JAX's collectives and lax.ppermute only.
A program may use at most 128 MiB of HBM per device.

```python
import math
import jax
import jax.numpy as jnp
import numpy as np

FXL = 256
FZL = 2048
SYL = 256
SZL = 2048
NF = 4096
SUBSTEPS = 4
NFX = 2048
NFZ = 8192
NSY = 2048
NSZ = 8192
FACES = 131072
CAP = 256
N_PASSAGE = 8
N_TILE = 4
DEVICES = 32


def place_ends(array, own_key, low, high):
    shape = array.shape
    index_at = [jax.random.randint(jax.random.fold_in(own_key, axis), (), 0, shape[axis]) for axis in range(len(shape))]
    array = array.at[tuple(index_at)].set(low)
    longest = shape.index(max(shape))
    index_at[longest] = (index_at[longest] + 1) % shape[longest]
    return array.at[tuple(index_at)].set(high)


def level_of(own_key, extent, pieces, least, largest):
    level, own = 1.0, jax.random.fold_in(own_key, 6)
    for dim, parts in pieces:
        steps = jnp.exp(jax.random.uniform(jax.random.fold_in(own, dim), (parts,), jnp.float32, least / len(pieces), largest / len(pieces)))
        level = level * jnp.repeat(steps, extent[dim] // parts).reshape([-1 if axis == dim else 1 for axis in range(len(extent))])
    return level


def routed_block(rng, own, number, rows, amount, top, reach, slope):
    sequence = jax.random.permutation(rng, amount)
    heavy_load, ordinary = shares(amount, rows * top, reach, slope, True), shares(amount, rows * top, reach, slope, False)
    places = jnp.arange(amount)

    def named(tallies, rotation):
        used = int((tallies > 0).sum())
        fixed = max(1, used // 4)
        shifted = fixed + (places - fixed + rotation * (used - fixed)) % max(1, amount - fixed)
        return jnp.zeros((amount,), jnp.int32).at[sequence[jnp.where(places < fixed, places, shifted)]].set(jnp.asarray(tallies, jnp.int32))

    tallies = jnp.where(number % 4 == 0, named(heavy_load, number // 4), named(ordinary, number - number // 4 - 1))
    mixed = jax.random.permutation(jax.random.fold_in(own, 3), amount)
    giver, taker = mixed[0:amount // 2 * 2:2], mixed[1:amount // 2 * 2:2]
    margin = jnp.minimum(tallies[giver] - 1, reach - tallies[taker]) // 2
    margin = jnp.where((giver == sequence[0]) | (taker == sequence[0]) | (tallies[taker] == 0), 0, jnp.maximum(margin, 0))
    shifted = jax.random.randint(jax.random.fold_in(own, 4), (amount // 2,), 0, 1 << 20) % (margin + 1)
    tallies = tallies.at[giver].add(-shifted).at[taker].add(shifted)
    labels = jnp.searchsorted(jnp.cumsum(tallies), jnp.arange(rows * top), side="right").astype(jnp.int32)
    table = labels.reshape(top, rows).T
    table = table[jax.random.permutation(jax.random.fold_in(own, 1), rows)]
    rotation = jax.random.randint(jax.random.fold_in(own, 2), (rows, 1), 0, top)
    return jnp.take_along_axis(table, (jnp.arange(top)[None, :] + rotation) % top, axis=1)


def shares(count, total, reach, slope, full):
    loads = [(1 << 20) // math.isqrt(grade ** slope) + 1 for grade in range(1, count + 1)]
    largest = reach if full else min(reach, max(-(-total // count), total * loads[0] // sum(loads)))
    least = 1 if total - largest >= count - 1 else 0
    given, surplus = [largest] + [least] * (count - 1), total - largest - least * (count - 1)
    while surplus > 0:
        free = [i for i in range(1, count) if given[i] < largest] or [i for i in range(1, count) if given[i] < reach]
        pool, left = sum([loads[i] for i in free]), surplus
        for i in free:
            extra = min(reach - given[i], max(1, left * loads[i] // pool), surplus)
            given[i] = given[i] + extra
            surplus = surplus - extra
    return np.array(given)


def centred(rng, dims, deviation, bound, shards=(), kind=jnp.bfloat16):
    array = deviation * jax.random.normal(rng, dims, jnp.float32)
    if shards:
        array = array * level_of(rng, dims, shards, -0.22, 0.18)
    return jnp.clip(array, -bound, bound).astype(kind)


def setup_inputs(seed: int = 0) -> dict:
    seeds = jax.random.split(jax.random.key(seed), 10)
    gas = centred(seeds[0], (NFX, NFZ), 1.0, 6.0, ((0, 8), (1, 4)), jnp.float32)
    gas_speed = jnp.clip(0.2 + 0.5 * jax.random.uniform(seeds[1], (NFX, NFZ), jnp.float32) ** level_of(seeds[1], (NFX, NFZ), ((0, 8), (1, 4)), -0.2, 0.2), 0.2, 0.7)
    solid = centred(seeds[2], (NSY, NSZ), 1.0, 6.0, ((0, 8), (1, 4)), jnp.float32)
    material = place_ends(jax.random.randint(seeds[3], (NSY, NSZ), 0, 3), jax.random.fold_in(seeds[3], 1), 0, 2).astype(jnp.int32)
    face_cell = place_ends(jax.random.randint(seeds[4], (FACES,), 0, FXL * FZL), jax.random.fold_in(seeds[4], 1), 0, (FXL * FZL) - 1).astype(jnp.int32)
    face_owner_keys = jax.random.split(jax.random.fold_in(seeds[5], 1), FACES // NF)
    face_owner_turns = jax.random.permutation(jax.random.fold_in(seeds[5], 3), FACES // NF)
    face_owner = jax.vmap(lambda own, number: routed_block(jax.random.fold_in(seeds[5], 2), own, number, NF, DEVICES, 1, CAP, 1))(face_owner_keys, face_owner_turns).reshape((FACES, 1))
    face_surface = place_ends(jax.random.randint(seeds[6], (FACES,), 0, 2 * SZL), jax.random.fold_in(seeds[6], 1), 0, (2 * SZL) - 1).astype(jnp.int32)
    film = jnp.clip(jnp.exp(math.log(1.0) - 2.3025851 * jax.random.uniform(seeds[7], (FACES,), jnp.float32) ** level_of(seeds[7], (FACES,), ((0, 32),), -0.2, 0.2)), 0.1, 1.0)
    wall_previous = centred(seeds[8], (FACES,), 1.0, 6.0, ((0, 32),), jnp.float32)
    return dict(gas=gas, gas_speed=gas_speed, solid=solid, material=material, face_cell=face_cell, face_owner=face_owner, face_surface=face_surface, film=film, wall_previous=wall_previous)


DIFFUSE = 0.05
SOLID_STEP = 0.1
SOFTEN = 0.08


def gas_tendency(values, speed):
    padded = jnp.pad(values, 1)
    centre = padded[1:-1, 1:-1]
    laplace = padded[2:, 1:-1] + padded[:-2, 1:-1] + padded[1:-1, 2:] + padded[1:-1, :-2] - 4.0 * centre
    return -speed * (centre - padded[1:-1, :-2]) + DIFFUSE * laplace


def stencil(padded_t, padded_k, source):
    centre = padded_t[1:-1, 1:-1]
    conduct = padded_k[1:-1, 1:-1]
    flux = 0.5 * (conduct + padded_k[2:, 1:-1]) * (padded_t[2:, 1:-1] - centre)
    flux = flux + 0.5 * (conduct + padded_k[:-2, 1:-1]) * (padded_t[:-2, 1:-1] - centre)
    flux = flux + 0.5 * (conduct + padded_k[1:-1, 2:]) * (padded_t[1:-1, 2:] - centre)
    flux = flux + 0.5 * (conduct + padded_k[1:-1, :-2]) * (padded_t[1:-1, :-2] - centre)
    return centre + SOLID_STEP * (flux + source)


def base_conductivity(material):
    return jnp.where(material == 0, jnp.float32(1.0), jnp.where(material == 1, jnp.float32(0.3), jnp.float32(0.08)))


def reference(gas, gas_speed, solid, material, face_cell, face_owner, face_surface, film, wall_previous):
    section_one = gas + gas_tendency(gas, gas_speed)
    gas_next = 0.5 * (gas + section_one + gas_tendency(section_one, gas_speed))
    tiled = gas_next.reshape(N_PASSAGE, FXL, N_TILE, FZL).transpose(0, 2, 1, 3).reshape(DEVICES, FXL * FZL)
    face_device = jnp.arange(FACES, dtype=jnp.int32) // NF
    heat = film * (tiled[face_device, face_cell] - wall_previous)
    target = face_owner[:, 0] * (2 * SZL) + face_surface
    deposit = jnp.zeros((DEVICES * 2 * SZL,), jnp.float32).at[target].add(heat)
    rows = deposit.reshape(N_PASSAGE, N_TILE, 2, SZL).transpose(0, 2, 1, 3)
    source = jnp.zeros((N_PASSAGE, SYL, N_TILE, SZL), jnp.float32).at[:, :2].set(rows).reshape(NSY, NSZ)
    kbase = base_conductivity(material)
    temper = solid
    for substep in range(SUBSTEPS):
        conduct = kbase * jnp.exp(SOFTEN * temper)
        temper = stencil(jnp.pad(temper, 1), jnp.pad(conduct, 1), source)
    surface = temper.reshape(N_PASSAGE, SYL, N_TILE, SZL)[:, :2].transpose(0, 2, 1, 3).reshape(-1)
    wall_temps = surface[target]
    return gas_next, temper, wall_temps
```

```python
import functools

import jax
import jax.numpy as jnp
from jax import lax
from jax.experimental import pallas as pl
from jax.experimental.pallas import tpu as pltpu
from jax.sharding import PartitionSpec as P

SUBSTEPS = 4
DIFFUSE = 0.05
SOLID_STEP = 0.1
SOFTEN = 0.08
LANES = 128
ROWS = 8
ROUTE_ROWS = 8
EDGE = SUBSTEPS - 1
F32 = jnp.float32
BF16 = jnp.bfloat16
VMEM = pltpu.VMEM
MIB = 2**20


def params(mib):
    return pltpu.CompilerParams(vmem_limit_bytes=mib * MIB)


def whole(space=pltpu.VMEM):
    return pl.BlockSpec(memory_space=space)


def iota(shape, dim):
    return lax.broadcasted_iota(jnp.int32, shape, dim)


def base_conductivity(material):
    return jnp.where(
        material == 0,
        jnp.float32(1.0),
        jnp.where(material == 1, jnp.float32(0.3), jnp.float32(0.08)),
    )


def even(axis):
    return lax.rem(lax.axis_index(axis), 2) == 0


def split3(x):
    one = x.astype(BF16).astype(F32)
    rest = x - one
    two = rest.astype(BF16).astype(F32)
    return one, two, (rest - two).astype(BF16).astype(F32)


def dot_lanes(a, b):
    return lax.dot_general(a, b, (((1,), (1,)), ((), ())), preferred_element_type=F32)


def dot(a, b):
    return lax.dot_general(a, b, (((1,), (0,)), ((), ())), preferred_element_type=F32)


def pair_swaps(axis, count):
    first = [(i, i + 1) for i in range(0, count - 1, 2)]
    second = [(i, i + 1) for i in range(1, count - 1, 2)]

    def both(pairs):
        return pairs + [(b, a) for a, b in pairs]

    def run(one, two):
        return lax.ppermute(one, axis, both(first)), lax.ppermute(two, axis, both(second))

    return run


def pack_columns(gl, gr, sl, sr, ul, ur, ml, mr, one_ref, two_ref):
    lane = iota(gl.shape, 1)
    head = jnp.where(
        lane < 4,
        ul[...],
        jnp.where(
            lane < 8,
            pltpu.roll(base_conductivity(ml[...]), 4, 1),
            jnp.where(lane < 10, pltpu.roll(gl[...], 8, 1), pltpu.roll(sl[...], 10, 1)),
        ),
    )
    tail = jnp.where(
        lane >= 124,
        ur[...],
        jnp.where(
            lane >= 120,
            pltpu.roll(base_conductivity(mr[...]), 124, 1),
            jnp.where(lane >= 118, pltpu.roll(gr[...], 120, 1), pltpu.roll(sr[...], 118, 1)),
        ),
    )
    head = head.T[0:16]
    tail = tail.T[112:128]
    is_even = even("tile")
    one_ref[...] = jnp.where(is_even, tail, head)
    two_ref[...] = jnp.where(is_even, head, tail)


def halo_tiles(w):
    lane = iota(w.shape, 1)
    zero = jnp.zeros_like(w)
    solid = jnp.where((lane < 4) | (lane >= 124), w, zero)
    conduct = jnp.where(
        lane < 4, pltpu.roll(w, 124, 1), jnp.where(lane >= 124, pltpu.roll(w, 4, 1), zero)
    )
    return solid, conduct


def gas_halo_tiles(w):
    lane = iota(w.shape, 1)
    zero = jnp.zeros_like(w)
    gas = jnp.where(
        lane < 2, pltpu.roll(w, 120, 1), jnp.where(lane >= 126, pltpu.roll(w, 8, 1), zero)
    )
    speed = jnp.where(
        lane < 1, pltpu.roll(w, 118, 1), jnp.where(lane >= 127, pltpu.roll(w, 10, 1), zero)
    )
    return gas, speed


def pack_rows(one, two, gt, gb, st, sb, ut, ub, mt, mb, w_ref, a_ref, b_ref, wt):
    is_even = even("tile")
    wt[...] = jnp.zeros_like(wt)
    wt[0:16, :] = jnp.where(is_even, one[...], two[...])
    wt[112:128, :] = jnp.where(is_even, two[...], one[...])
    w = wt[...].T
    w_ref[...] = w
    size = w.shape[0]
    wide = gt.shape[1] + LANES

    def rows(g, s, u, m, part, step, keep):
        uh, kh = halo_tiles(part)
        gh, sh = gas_halo_tiles(part)
        g = jnp.concatenate([g[...], gh], axis=1)
        s = jnp.concatenate([s[...], sh], axis=1)
        u = jnp.concatenate([u[...], uh], axis=1)
        k = jnp.concatenate([base_conductivity(m[...]), kh], axis=1)
        before = pltpu.roll(g, 1, 1)
        after = pltpu.roll(g, wide - 1, 1)
        inner = pltpu.roll(g, step, 0)
        partial = g - s * (g - before) + DIFFUSE * (inner + before + after - 4.0 * g)
        return g, partial, u, k

    row = iota((ROWS, wide), 0)
    zero = jnp.zeros((ROWS, wide), F32)
    g, partial, u, k = rows(gt, st, ut, mt, w[0:ROWS], ROWS - 1, 0)

    def first_two(x, y):
        return jnp.where(row == 0, x, jnp.where(row == 1, pltpu.roll(y, 1, 0), zero))

    up = (first_two(g, u), first_two(partial, k))
    g, partial, u, k = rows(gb, sb, ub, mb, w[size - ROWS : size], 1, 0)

    def last_rows(x, y):
        return jnp.where(row == 0, pltpu.roll(x, 1, 0), y)

    down = (last_rows(g, u), last_rows(partial, k))
    is_even = even("passage")
    for half in range(2):
        a_ref[half * ROWS : (half + 1) * ROWS, :] = jnp.where(is_even, down[half], up[half])
        b_ref[half * ROWS : (half + 1) * ROWS, :] = jnp.where(is_even, up[half], down[half])


def find_slots(devices, per_owner, rows, cols, owner, surface, cell, slot_ref, row_ref, idx_ref, held, lhs, rhs):
    blocks = owner.shape[0]
    owners = iota((devices, LANES), 0)
    for b in range(blocks):
        held[b * devices : (b + 1) * devices, :] = jnp.where(owner[b : b + 1, :] == owners, 1.0, 0.0).astype(BF16)
    r, c = iota((LANES, 2 * LANES), 0), iota((LANES, 2 * LANES), 1)
    before = jnp.where((r < c) | (c >= LANES), 1.0, 0.0).astype(BF16)
    counts = dot(held[...], before)
    high = slot_ref.shape[0]
    table = idx_ref.shape[0]
    start = jnp.zeros((devices, LANES), F32)
    highs, lows = iota((table, LANES), 0), iota((LANES, LANES), 0)
    for b in range(blocks):
        own = counts[b * devices : (b + 1) * devices]
        mine = owner[b : b + 1, :]
        rank = jnp.sum(
            jnp.where(mine == owners, own[:, :LANES] + start, 0.0), axis=0, keepdims=True
        ).astype(jnp.int32)
        start = start + own[:, LANES:]
        hi = mine * per_owner + lax.shift_right_logical(rank, 7)
        lo = rank & (LANES - 1)
        slot_ref[b : b + 1, :] = hi * LANES + lo
        value = surface[b : b + 1, :]
        coarse = (value & ~255).astype(F32)
        fine = (value & 255).astype(F32)
        at = slice(b * LANES, (b + 1) * LANES)
        lhs[0:table, at] = jnp.where(highs == hi, coarse, 0.0).astype(BF16)
        lhs[table : 2 * table, at] = jnp.where(highs == hi, fine, 0.0).astype(BF16)
        rhs[:, at] = jnp.where(lows == lo, 1.0, 0.0).astype(BF16)
    both = dot_lanes(lhs[...], rhs[...])
    idx_ref[...] = both[0:table] + both[table : 2 * table]
    place = cell[...]
    row_ref[...] = lax.div(lax.rem(place, cols), LANES) * rows + lax.div(place, cols)


def shifted(tiles, lane):
    count = len(tiles)
    left = [pltpu.roll(x, LANES - 1, 1) for x in tiles]
    right = [pltpu.roll(x, 1, 1) for x in tiles]
    after = [jnp.where(lane == LANES - 1, left[(i + 1) % count], left[i]) for i in range(count)]
    before = [jnp.where(lane == 0, right[i - 1], right[i]) for i in range(count)]
    return after, before


def gas_kernel(
    tiles_across, per_owner, gas, speed, w, ra, rb, rowidx, cell, owner, surface, slot, film, wall, idx,
    out, route, gx, sx, s1, tab, stage, lhs, rhs, sums, sem,
):
    rows, cols = gas.shape
    nt = cols // LANES
    devices = route.shape[0]
    blocks = owner.shape[0]
    table = idx.shape[0]
    copies = []
    for ct in range(nt):
        at = pl.ds(ct * LANES, LANES)
        copies.append(pltpu.make_async_copy(gas.at[:, at], gx.at[ct, pl.ds(ROWS, rows)], sem.at[0, ct]))
        copies.append(pltpu.make_async_copy(speed.at[:, at], sx.at[ct], sem.at[1, ct]))
    for copy in copies:
        copy.start()
    gh, sh = gas_halo_tiles(w[...])
    gx[nt, ROWS : ROWS + rows, :] = gh
    sx[nt] = sh
    is_even = even("passage")
    place = lax.axis_index("passage")
    in_top = jnp.where(place > 0, 1.0, 0.0)
    in_bottom = jnp.where(place < lax.axis_size("passage") - 1, 1.0, 0.0)

    def top(row, ct):
        at = slice(ct * LANES, (ct + 1) * LANES)
        return jnp.where(is_even, rb[row : row + 1, at], ra[row : row + 1, at])

    def bottom(row, ct):
        at = slice(ct * LANES, (ct + 1) * LANES)
        return jnp.where(is_even, ra[row : row + 1, at], rb[row : row + 1, at])

    for ct in range(nt + 1):
        gx[ct, ROWS - 1 : ROWS, :] = top(0, ct)
        gx[ct, ROWS + rows : ROWS + rows + 1, :] = bottom(0, ct)
    for copy in copies:
        copy.wait()
    for ct in range(nt):
        s1[ct, ROWS - 1 : ROWS, :] = in_top * (top(8, ct) + DIFFUSE * gx[ct, ROWS : ROWS + 1, :])
        s1[ct, ROWS + rows : ROWS + rows + 1, :] = in_bottom * (
            bottom(8, ct) + DIFFUSE * gx[ct, ROWS + rows - 1 : ROWS + rows, :]
        )
    lane = iota((ROWS, LANES), 1)

    def tendency(v, north, south, after, before, s):
        return DIFFUSE * (south + north + after + before - 4.0 * v) - s * (v - before)

    def first(i, carry):
        r0 = pl.multiple_of(i * ROWS, ROWS)
        v = [gx[ct, pl.ds(ROWS + r0, ROWS), :] for ct in range(nt + 1)]
        after, before = shifted(v, lane)
        for ct in range(nt + 1):
            north = gx[ct, pl.ds(ROWS - 1 + r0, ROWS), :]
            south = gx[ct, pl.ds(ROWS + 1 + r0, ROWS), :]
            s = sx[ct, pl.ds(r0, ROWS), :]
            new = v[ct] + tendency(v[ct], north, south, after[ct], before[ct], s)
            if ct == nt:
                new = jnp.where(s > 0, new, 0.0)
            s1[ct, pl.ds(ROWS + r0, ROWS), :] = new
        return carry

    lax.fori_loop(0, rows // ROWS, first, 0)

    def second(i, carry):
        r0 = pl.multiple_of(i * ROWS, ROWS)
        v = [s1[ct, pl.ds(ROWS + r0, ROWS), :] for ct in range(nt + 1)]
        after, before = shifted(v, lane)
        for ct in range(nt):
            north = s1[ct, pl.ds(ROWS - 1 + r0, ROWS), :]
            south = s1[ct, pl.ds(ROWS + 1 + r0, ROWS), :]
            s = sx[ct, pl.ds(r0, ROWS), :]
            g = gx[ct, pl.ds(ROWS + r0, ROWS), :]
            tab[pl.ds(ct * rows + r0, ROWS), :] = 0.5 * (
                g + v[ct] + tendency(v[ct], north, south, after[ct], before[ct], s)
            )
        return carry

    lax.fori_loop(0, rows // ROWS, second, 0)
    outs = [
        pltpu.make_async_copy(tab.at[pl.ds(ct * rows, rows)], out.at[:, pl.ds(ct * LANES, LANES)], sem.at[0, ct])
        for ct in range(nt)
    ]
    for copy in outs:
        copy.start()
    sub = iota((ROWS, LANES), 0)
    unroll = 8

    def gather(i, carry):
        base = pl.multiple_of(i * (ROWS * unroll), ROWS * unroll)
        for g in range(unroll):
            acc = jnp.broadcast_to(tab[pl.ds(rowidx[base + g * ROWS], 1), :], (ROWS, LANES))
            for j in range(1, ROWS):
                row = tab[pl.ds(rowidx[base + g * ROWS + j], 1), :]
                acc = jnp.where(sub == j, jnp.broadcast_to(row, (ROWS, LANES)), acc)
            stage[pl.ds(base + g * ROWS, ROWS), :] = acc
        return carry

    lax.fori_loop(0, stage.shape[0] // (ROWS * unroll), gather, 0)
    lanes_down = iota((LANES, LANES), 0)
    highs = iota((table, LANES), 0)
    owners = iota((devices, LANES), 0)
    part = table + devices
    for b in range(blocks):
        at = slice(b * LANES, (b + 1) * LANES)
        picked = jnp.where(lanes_down == (cell[b : b + 1, :] & (LANES - 1)), stage[at, :].T, 0.0)
        face = jnp.sum(picked, axis=0, keepdims=True)
        heat = split3(film[b : b + 1, :] * (face - wall[b : b + 1, :]))
        place_of = slot[b : b + 1, :]
        hi = lax.shift_right_logical(place_of, 7)
        lo = place_of & (LANES - 1)
        mine = owner[b : b + 1, :]
        voxel = surface[b : b + 1, :]
        line = lax.div(voxel, cols)
        col = lax.rem(voxel, cols)
        tile = lax.rem(mine, tiles_across)
        to_right = (col >= cols - EDGE) & (tile < tiles_across - 1)
        to_left = (col < EDGE) & (tile > 0)
        dest = jnp.where(to_right, mine + 1, jnp.where(to_left, mine - 1, -1))
        code = jnp.where(to_right, col - (cols - EDGE), 16 + col) + 8 * line
        for k in range(3):
            lhs[k * part : k * part + table, at] = jnp.where(highs == hi, heat[k], 0.0).astype(BF16)
            lhs[k * part + table : (k + 1) * part, at] = jnp.where(owners == dest, heat[k], 0.0).astype(BF16)
        rhs[0:LANES, at] = jnp.where(lanes_down == lo, 1.0, 0.0).astype(BF16)
        rhs[LANES : LANES + 32, at] = jnp.where(iota((32, LANES), 0) == code, 1.0, 0.0).astype(BF16)
    three = dot_lanes(lhs[...], rhs[...])
    sums[...] = three[0:part] + three[part : 2 * part] + three[2 * part : 3 * part]
    route[...] = jnp.zeros_like(route)
    for o in range(devices):
        own = slice(o * per_owner, (o + 1) * per_owner)
        route[o, 0:per_owner, :] = sums[own, 0:LANES]
        route[o, per_owner : 2 * per_owner, :] = idx[own, :]
        route[o, 2 * per_owner : 2 * per_owner + 1, 0:32] = sums[table + o : table + o + 1, LANES : LANES + 32]
    for copy in outs:
        copy.wait()


def strip_kernel(per_owner, recv, ra, rb, w, solid, material, top_ref, up_ref, ret_ref, lhs, rhs, dep, src, tabu):
    devices = recv.shape[0]
    cols = solid.shape[1]
    nt = cols // LANES
    wide = cols + LANES
    high = 2 * nt
    highs = iota((high, LANES), 0)
    lanes_down = iota((LANES, LANES), 0)
    for d in range(devices):
        for q in range(per_owner):
            at = slice((d * per_owner + q) * LANES, (d * per_owner + q + 1) * LANES)
            heat = split3(recv[d, q : q + 1, :])
            where = recv[d, per_owner + q : per_owner + q + 1, :].astype(jnp.int32)
            hi = lax.shift_right_logical(where, 7)
            for k in range(3):
                lhs[k * high : (k + 1) * high, at] = jnp.where(highs == hi, heat[k], 0.0).astype(BF16)
            rhs[:, at] = jnp.where(lanes_down == (where & (LANES - 1)), 1.0, 0.0).astype(BF16)
    three = dot_lanes(lhs[...], rhs[...])
    dep[...] = three[0:high] + three[high : 2 * high] + three[2 * high : 3 * high]
    edges = recv[0, 2 * per_owner : 2 * per_owner + 1, :]
    for d in range(1, devices):
        edges = edges + recv[d, 2 * per_owner : 2 * per_owner + 1, :]
    src[...] = jnp.zeros_like(src)
    lane = iota((1, LANES), 1)
    for line in range(2):
        for ct in range(nt):
            src[line : line + 1, ct * LANES : (ct + 1) * LANES] = dep[line * nt + ct : line * nt + ct + 1, :]
        left = pltpu.roll(edges, LANES - EDGE - 8 * line, 1)
        right = pltpu.roll(edges, LANES - 16 - 8 * line, 1)
        src[line : line + 1, cols:wide] = jnp.where(
            lane >= LANES - EDGE, left, jnp.where(lane < EDGE, right, 0.0)
        )
    is_even = even("passage")
    row8 = iota((ROWS, wide), 0)

    def above(at):
        return jnp.where(row8 > 0, jnp.where(is_even, rb[at : at + ROWS, :], ra[at : at + ROWS, :]), 0.0)

    uh, kh = halo_tiles(w[...])
    u = jnp.concatenate([above(0), jnp.concatenate([solid[...], uh], axis=1)], axis=0)
    k0 = jnp.concatenate([above(8), jnp.concatenate([base_conductivity(material[...]), kh], axis=1)], axis=0)
    inside = jnp.where(k0 > 0, 0.5 * SOLID_STEP, 0.0)
    source = jnp.concatenate(
        [jnp.zeros((ROWS, wide), F32), 2.0 * src[...], jnp.zeros((ROWS, wide), F32)], axis=0
    )
    high_rows = 3 * ROWS
    for _ in range(SUBSTEPS):
        k = k0 * jnp.exp(SOFTEN * u)
        across = (k + pltpu.roll(k, wide - 1, 1)) * (pltpu.roll(u, wide - 1, 1) - u)
        down = (k + pltpu.roll(k, high_rows - 1, 0)) * (pltpu.roll(u, high_rows - 1, 0) - u)
        flux = across - pltpu.roll(across, 1, 1) + down - pltpu.roll(down, 1, 0)
        u = u + inside * (flux + source)
    up_ref[...] = u[0:ROWS, 0:cols]
    top_ref[...] = u[ROWS : 2 * ROWS, 0:cols]
    for line in range(2):
        for ct in range(nt):
            tabu[line * nt + ct : line * nt + ct + 1, :] = top_ref[line : line + 1, ct * LANES : (ct + 1) * LANES]
    parts = jnp.concatenate(split3(tabu[...]), axis=0).astype(BF16)
    for d in range(devices):
        for q in range(per_owner):
            at = slice((d * per_owner + q) * LANES, (d * per_owner + q + 1) * LANES)
            x = dot(parts, rhs[:, at])
            x = x[0:high] + x[high : 2 * high] + x[2 * high : 3 * high]
            where = recv[d, per_owner + q : per_owner + q + 1, :].astype(jnp.int32)
            hi = lax.shift_right_logical(where, 7)
            ret_ref[d, q : q + 1, :] = jnp.sum(jnp.where(highs == hi, x, 0.0), axis=0, keepdims=True)


def bulk_kernel(solid, material, w, ra, rb, out, ua, ub, ka, kb, k0, mat, sem):
    rows, cols = solid.shape
    nt = cols // LANES
    copies = []
    for ct in range(nt):
        at = pl.ds(ct * LANES, LANES)
        copies.append(pltpu.make_async_copy(solid.at[:, at], ua.at[ct, pl.ds(ROWS, rows)], sem.at[0, ct]))
        copies.append(pltpu.make_async_copy(material.at[:, at], mat.at[ct], sem.at[1, ct]))
    for copy in copies:
        copy.start()
    uh, kh = halo_tiles(w[...])
    ua[nt, ROWS : ROWS + rows, :] = uh
    k0[nt] = kh
    ka[nt, ROWS : ROWS + rows, :] = kh * jnp.exp(SOFTEN * uh)
    is_even = even("passage")
    zero = jnp.zeros((ROWS, LANES), F32)
    for ct in range(nt + 1):
        at = slice(ct * LANES, (ct + 1) * LANES)
        below = jnp.where(is_even, ra[1:2, at], rb[1:2, at])
        below_k = jnp.where(is_even, ra[9:10, at], rb[9:10, at]) * jnp.exp(SOFTEN * below)
        for u, k in ((ua, ka), (ub, kb)):
            u[ct, 0:ROWS, :] = zero
            k[ct, 0:ROWS, :] = zero
            u[ct, ROWS + rows : ROWS + rows + 1, :] = below
            k[ct, ROWS + rows : ROWS + rows + 1, :] = below_k
    for copy in copies:
        copy.wait()

    def begin(i, carry):
        r0 = pl.multiple_of(i * ROWS, ROWS)
        for ct in range(nt):
            base = base_conductivity(mat[ct, pl.ds(r0, ROWS), :])
            k0[ct, pl.ds(r0, ROWS), :] = base
            ka[ct, pl.ds(ROWS + r0, ROWS), :] = base * jnp.exp(SOFTEN * ua[ct, pl.ds(ROWS + r0, ROWS), :])
        return carry

    lax.fori_loop(0, rows // ROWS, begin, 0)
    lane = iota((ROWS, LANES), 1)
    for step in range(SUBSTEPS):
        last = step == SUBSTEPS - 1
        u, k, nu, nk = (ua, ka, ub, kb) if step % 2 == 0 else (ub, kb, ua, ka)

        def body(i, carry, u=u, k=k, nu=nu, nk=nk, last=last):
            r0 = pl.multiple_of(i * ROWS, ROWS)
            at = pl.ds(ROWS + r0, ROWS)
            north, south = pl.ds(ROWS - 1 + r0, ROWS), pl.ds(ROWS + 1 + r0, ROWS)
            here = [u[ct, at, :] for ct in range(nt + 1)]
            cond = [k[ct, at, :] for ct in range(nt + 1)]
            turned = [pltpu.roll(x, LANES - 1, 1) for x in here]
            turned_k = [pltpu.roll(x, LANES - 1, 1) for x in cond]
            edge = lane == LANES - 1
            across = []
            for ct in range(nt + 1):
                after = jnp.where(edge, turned[(ct + 1) % (nt + 1)], turned[ct])
                after_k = jnp.where(edge, turned_k[(ct + 1) % (nt + 1)], turned_k[ct])
                across.append((cond[ct] + after_k) * (after - here[ct]))
            back = [pltpu.roll(x, 1, 1) for x in across]
            for ct in range(nt if last else nt + 1):
                flux = across[ct] - jnp.where(lane == 0, back[ct - 1], back[ct])
                flux = flux + (cond[ct] + k[ct, north, :]) * (u[ct, north, :] - here[ct])
                flux = flux + (cond[ct] + k[ct, south, :]) * (u[ct, south, :] - here[ct])
                base = k0[ct, pl.ds(r0, ROWS), :]
                if ct == nt:
                    flux = jnp.where(base > 0, flux, 0.0)
                new = here[ct] + 0.5 * SOLID_STEP * flux
                nu[ct, at, :] = new
                if not last:
                    nk[ct, at, :] = base * jnp.exp(SOFTEN * new)
            return carry

        lax.fori_loop(0, rows // ROWS, body, 0)
    final = ua if SUBSTEPS % 2 == 0 else ub
    outs = [
        pltpu.make_async_copy(final.at[ct, pl.ds(ROWS, rows)], out.at[:, pl.ds(ct * LANES, LANES)], sem.at[0, ct])
        for ct in range(nt)
    ]
    for copy in outs:
        copy.start()
    for copy in outs:
        copy.wait()


def finish_kernel(recv, slot, top, below, solid, wall_ref, out, tabl, edge, sem):
    devices, per_owner = recv.shape[0], recv.shape[1]
    rows = solid.shape[0]
    keep = rows - EDGE
    fetch = pltpu.make_async_copy(out.at[pl.ds(rows - ROWS, ROWS)], edge, sem.at[0])
    fetch.start()
    put = pltpu.make_async_copy(top, out.at[pl.ds(0, ROWS)], sem.at[1])
    put.start()
    for d in range(devices):
        tabl[d * per_owner : (d + 1) * per_owner, :] = recv[d]
    table = tabl.shape[0]
    parts = jnp.concatenate(split3(tabl[...]), axis=0).astype(BF16)
    highs, lanes_down = iota((table, LANES), 0), iota((LANES, LANES), 0)
    fetch.wait()
    last = lax.axis_index("passage") == lax.axis_size("passage") - 1
    row = iota(edge.shape, 0) + (rows - ROWS)
    edge[...] = jnp.where((row >= keep) & jnp.logical_not(last), below[...], edge[...])
    store = pltpu.make_async_copy(edge, out.at[pl.ds(rows - ROWS, ROWS)], sem.at[0])
    store.start()
    for b in range(slot.shape[0]):
        place = slot[b : b + 1, :]
        lows = jnp.where(lanes_down == (place & (LANES - 1)), 1.0, 0.0).astype(BF16)
        x = dot(parts, lows)
        x = x[0:table] + x[table : 2 * table] + x[2 * table : 3 * table]
        hi = lax.shift_right_logical(place, 7)
        wall_ref[b : b + 1, :] = jnp.sum(jnp.where(highs == hi, x, 0.0), axis=0, keepdims=True)
    put.wait()
    store.wait()


def shards(gas, gas_speed, solid, material, face_cell, face_owner, face_surface, film, wall_previous):
    passages = lax.axis_size("passage")
    tiles = lax.axis_size("tile")
    devices = passages * tiles
    rows, cols = solid.shape
    nt = cols // LANES
    faces = face_cell.shape[0]
    blocks = faces // LANES
    cap = 2 * faces // devices
    per_owner = max(1, cap // LANES)
    table = devices * per_owner
    wide = cols + LANES

    def shape(dims, kind=F32):
        return jax.ShapeDtypeStruct(dims, kind)

    def cost(flops, moved, hard=0):
        return pl.CostEstimate(flops=flops, bytes_accessed=moved, transcendentals=hard)

    fields = (gas, gas_speed, solid, material)
    left = pl.BlockSpec((rows, LANES), lambda i: (0, 0))
    right = pl.BlockSpec((rows, LANES), lambda i: (0, nt - 1))
    column = pl.BlockSpec((16, rows), lambda i: (0, 0))
    one, two = pl.pallas_call(
        pack_columns,
        grid=(1,),
        in_specs=[left, right] * 4,
        out_specs=[column, column],
        out_shape=[shape((16, rows))] * 2,
        name="pack_columns",
        cost_estimate=cost(1000000, 8 * rows * LANES * 4),
    )(*[x for field in fields for x in (field, field)])
    one, two = pair_swaps("tile", tiles)(one, two)

    def tall(count, row):
        return pl.BlockSpec((count, cols), lambda i: (row, 0))

    full = pl.BlockSpec((rows, LANES), lambda i: (0, 0))
    band = pl.BlockSpec((16, wide), lambda i: (0, 0))
    w, ra, rb = pl.pallas_call(
        pack_rows,
        grid=(1,),
        in_specs=[column, column] + [tall(ROWS, 0), tall(ROWS, rows // ROWS - 1)] * 4,
        out_specs=[full, band, band],
        out_shape=[shape((rows, LANES)), shape((16, wide)), shape((16, wide))],
        scratch_shapes=[VMEM((LANES, rows), F32)],
        name="pack_rows",
        cost_estimate=cost(1000000, 8 * ROWS * cols * 4),
    )(one, two, *[x for field in fields for x in (field, field)])
    ra, rb = pair_swaps("passage", passages)(ra, rb)

    def folded(x):
        return x.reshape(blocks, LANES)

    owner, surface, cell = folded(face_owner), folded(face_surface), folded(face_cell)
    slot, rowidx, idx = pl.pallas_call(
        functools.partial(find_slots, devices, per_owner, rows, cols),
        in_specs=[whole()] * 3,
        out_specs=[whole()] * 3,
        out_shape=[shape((blocks, LANES), jnp.int32), shape((blocks, LANES), jnp.int32), shape((table, LANES))],
        scratch_shapes=[
            VMEM((blocks * devices, LANES), BF16),
            VMEM((2 * table, faces), BF16),
            VMEM((LANES, faces), BF16),
        ],
        compiler_params=params(24),
        name="find_slots",
        cost_estimate=cost(20000000, 1000000),
    )(owner, surface, cell)

    part = table + devices
    gas_next, route = pl.pallas_call(
        functools.partial(gas_kernel, tiles, per_owner),
        in_specs=[whole(pl.ANY)] * 2 + [whole()] * 3 + [whole(pltpu.SMEM)] + [whole()] * 7,
        out_specs=[whole(pl.ANY), whole()],
        out_shape=[shape((rows, cols)), shape((devices, ROUTE_ROWS, LANES))],
        scratch_shapes=[
            VMEM((nt + 1, rows + 2 * ROWS, LANES), F32),
            VMEM((nt + 1, rows, LANES), F32),
            VMEM((nt + 1, rows + 2 * ROWS, LANES), F32),
            VMEM((nt * rows, LANES), F32),
            VMEM((faces, LANES), F32),
            VMEM((3 * part, faces), BF16),
            VMEM((LANES + 32, faces), BF16),
            VMEM((part, LANES + 32), F32),
            pltpu.SemaphoreType.DMA((2, nt)),
        ],
        compiler_params=params(40),
        name="gas_and_heat",
        cost_estimate=cost(60000000, 40000000),
    )(
        gas, gas_speed, w, ra, rb, rowidx.reshape(faces), cell, owner, surface, slot,
        folded(film), folded(wall_previous), idx,
    )
    recv = lax.all_to_all(route, ("passage", "tile"), 0, 0, tiled=True)

    bulk = pl.pallas_call(
        bulk_kernel,
        in_specs=[whole(pl.ANY)] * 2 + [whole()] * 3,
        out_specs=whole(pl.ANY),
        out_shape=shape((rows, cols)),
        scratch_shapes=[VMEM((nt + 1, rows + 2 * ROWS, LANES), F32)] * 4
        + [
            VMEM((nt + 1, rows, LANES), F32),
            VMEM((nt, rows, LANES), jnp.int32),
            pltpu.SemaphoreType.DMA((2, nt)),
        ],
        compiler_params=params(40),
        name="solid_bulk",
        cost_estimate=cost(60000000, 40000000),
    )(solid, material, w, ra, rb)

    slots = table * LANES
    top, up, ret = pl.pallas_call(
        functools.partial(strip_kernel, per_owner),
        grid=(1,),
        in_specs=[
            pl.BlockSpec((devices, ROUTE_ROWS, LANES), lambda i: (0, 0, 0)),
            band,
            band,
            pl.BlockSpec((16, LANES), lambda i: (0, 0)),
            tall(16, 0),
            tall(16, 0),
        ],
        out_specs=[
            pl.BlockSpec((ROWS, cols), lambda i: (0, 0)),
            pl.BlockSpec((ROWS, cols), lambda i: (0, 0)),
            pl.BlockSpec((devices, per_owner, LANES), lambda i: (0, 0, 0)),
        ],
        out_shape=[shape((ROWS, cols)), shape((ROWS, cols)), shape((devices, per_owner, LANES))],
        scratch_shapes=[
            VMEM((6 * nt, slots), BF16),
            VMEM((LANES, slots), BF16),
            VMEM((2 * nt, LANES), F32),
            VMEM((ROWS, wide), F32),
            VMEM((2 * nt, LANES), F32),
        ],
        compiler_params=params(32),
        name="solid_strip",
        cost_estimate=cost(20000000, 4000000),
    )(recv, ra, rb, w, solid, material)
    ret = lax.all_to_all(ret, ("passage", "tile"), 0, 0, tiled=True)
    below = lax.ppermute(up, "passage", [(i + 1, i) for i in range(passages - 1)])

    wall, solid_next = pl.pallas_call(
        finish_kernel,
        in_specs=[whole()] * 4 + [whole(pl.ANY)],
        out_specs=[whole(), whole(pl.ANY)],
        out_shape=[shape((blocks, LANES)), shape((rows, cols))],
        input_output_aliases={4: 1},
        scratch_shapes=[
            VMEM((table, LANES), F32),
            VMEM((ROWS, cols), F32),
            pltpu.SemaphoreType.DMA((2,)),
        ],
        compiler_params=params(24),
        name="wall_temperatures",
        cost_estimate=cost(20000000, 4000000),
    )(ret, slot, top, below, bulk)
    return gas_next, solid_next, wall.reshape(faces)


def solution(mesh):
    in_specs = (
        P("passage", "tile"),
        P("passage", "tile"),
        P("passage", "tile"),
        P("passage", "tile"),
        P(("passage", "tile")),
        P(("passage", "tile"), None),
        P(("passage", "tile")),
        P(("passage", "tile")),
        P(("passage", "tile")),
    )
    out_specs = (P("passage", "tile"), P("passage", "tile"), P(("passage", "tile")))
    return jax.shard_map(shards, mesh=mesh, in_specs=in_specs, out_specs=out_specs, check_vma=False)
```

```python
import functools

import jax
import jax.numpy as jnp
from jax import lax
from jax.experimental import pallas as pl
from jax.experimental.pallas import tpu as pltpu
from jax.sharding import PartitionSpec as P

SUBSTEPS = 4
DIFFUSE = 0.05
SOLID_STEP = 0.1
SOFTEN = 0.08
LANES = 128
ROWS = 8
ROUTE_ROWS = 8
EDGE = SUBSTEPS - 1
F32 = jnp.float32
BF16 = jnp.bfloat16
VMEM = pltpu.VMEM
MIB = 2**20


def params(mib):
    return pltpu.CompilerParams(vmem_limit_bytes=mib * MIB)


def whole(space=pltpu.VMEM):
    return pl.BlockSpec(memory_space=space)


def iota(shape, dim):
    return lax.broadcasted_iota(jnp.int32, shape, dim)


def base_conductivity(material):
    return jnp.where(
        material == 0,
        jnp.float32(1.0),
        jnp.where(material == 1, jnp.float32(0.3), jnp.float32(0.08)),
    )


def even(axis):
    return lax.rem(lax.axis_index(axis), 2) == 0


def split3(x):
    one = x.astype(BF16).astype(F32)
    rest = x - one
    two = rest.astype(BF16).astype(F32)
    return one, two, (rest - two).astype(BF16).astype(F32)


def dot_lanes(a, b):
    return lax.dot_general(a, b, (((1,), (1,)), ((), ())), preferred_element_type=F32)


def dot(a, b):
    return lax.dot_general(a, b, (((1,), (0,)), ((), ())), preferred_element_type=F32)


def pair_swaps(axis, count):
    first = [(i, i + 1) for i in range(0, count - 1, 2)]
    second = [(i, i + 1) for i in range(1, count - 1, 2)]

    def both(pairs):
        return pairs + [(b, a) for a, b in pairs]

    def run(one, two):
        return lax.ppermute(one, axis, both(first)), lax.ppermute(two, axis, both(second))

    return run


def pack_columns(gl, gr, sl, sr, ul, ur, ml, mr, one_ref, two_ref):
    lane = iota(gl.shape, 1)
    head = jnp.where(
        lane < 4,
        ul[...],
        jnp.where(
            lane < 8,
            pltpu.roll(base_conductivity(ml[...]), 4, 1),
            jnp.where(lane < 10, pltpu.roll(gl[...], 8, 1), pltpu.roll(sl[...], 10, 1)),
        ),
    )
    tail = jnp.where(
        lane >= 124,
        ur[...],
        jnp.where(
            lane >= 120,
            pltpu.roll(base_conductivity(mr[...]), 124, 1),
            jnp.where(lane >= 118, pltpu.roll(gr[...], 120, 1), pltpu.roll(sr[...], 118, 1)),
        ),
    )
    head = head.T[0:16]
    tail = tail.T[112:128]
    is_even = even("tile")
    one_ref[...] = jnp.where(is_even, tail, head)
    two_ref[...] = jnp.where(is_even, head, tail)


def halo_tiles(w):
    lane = iota(w.shape, 1)
    zero = jnp.zeros_like(w)
    solid = jnp.where((lane < 4) | (lane >= 124), w, zero)
    conduct = jnp.where(
        lane < 4, pltpu.roll(w, 124, 1), jnp.where(lane >= 124, pltpu.roll(w, 4, 1), zero)
    )
    return solid, conduct


def gas_halo_tiles(w):
    lane = iota(w.shape, 1)
    zero = jnp.zeros_like(w)
    gas = jnp.where(
        lane < 2, pltpu.roll(w, 120, 1), jnp.where(lane >= 126, pltpu.roll(w, 8, 1), zero)
    )
    speed = jnp.where(
        lane < 1, pltpu.roll(w, 118, 1), jnp.where(lane >= 127, pltpu.roll(w, 10, 1), zero)
    )
    return gas, speed


def pack_rows(one, two, gt, gb, st, sb, ut, ub, mt, mb, w_ref, a_ref, b_ref, wt):
    is_even = even("tile")
    wt[...] = jnp.zeros_like(wt)
    wt[0:16, :] = jnp.where(is_even, one[...], two[...])
    wt[112:128, :] = jnp.where(is_even, two[...], one[...])
    w = wt[...].T
    w_ref[...] = w
    size = w.shape[0]
    wide = gt.shape[1] + LANES

    def rows(g, s, u, m, part, step, keep):
        uh, kh = halo_tiles(part)
        gh, sh = gas_halo_tiles(part)
        g = jnp.concatenate([g[...], gh], axis=1)
        s = jnp.concatenate([s[...], sh], axis=1)
        u = jnp.concatenate([u[...], uh], axis=1)
        k = jnp.concatenate([base_conductivity(m[...]), kh], axis=1)
        before = pltpu.roll(g, 1, 1)
        after = pltpu.roll(g, wide - 1, 1)
        inner = pltpu.roll(g, step, 0)
        partial = g - s * (g - before) + DIFFUSE * (inner + before + after - 4.0 * g)
        return g, partial, u, k

    row = iota((ROWS, wide), 0)
    zero = jnp.zeros((ROWS, wide), F32)
    g, partial, u, k = rows(gt, st, ut, mt, w[0:ROWS], ROWS - 1, 0)

    def first_two(x, y):
        return jnp.where(row == 0, x, jnp.where(row == 1, pltpu.roll(y, 1, 0), zero))

    up = (first_two(g, u), first_two(partial, k))
    g, partial, u, k = rows(gb, sb, ub, mb, w[size - ROWS : size], 1, 0)

    def last_rows(x, y):
        return jnp.where(row == 0, pltpu.roll(x, 1, 0), y)

    down = (last_rows(g, u), last_rows(partial, k))
    is_even = even("passage")
    for half in range(2):
        a_ref[half * ROWS : (half + 1) * ROWS, :] = jnp.where(is_even, down[half], up[half])
        b_ref[half * ROWS : (half + 1) * ROWS, :] = jnp.where(is_even, up[half], down[half])


def find_slots(devices, per_owner, rows, cols, owner, surface, cell, slot_ref, row_ref, idx_ref, held, lhs, rhs):
    blocks = owner.shape[0]
    owners = iota((devices, LANES), 0)
    for b in range(blocks):
        held[b * devices : (b + 1) * devices, :] = jnp.where(owner[b : b + 1, :] == owners, 1.0, 0.0).astype(BF16)
    r, c = iota((LANES, 2 * LANES), 0), iota((LANES, 2 * LANES), 1)
    before = jnp.where((r < c) | (c >= LANES), 1.0, 0.0).astype(BF16)
    counts = dot(held[...], before)
    high = slot_ref.shape[0]
    table = idx_ref.shape[0]
    start = jnp.zeros((devices, LANES), F32)
    highs, lows = iota((table, LANES), 0), iota((LANES, LANES), 0)
    for b in range(blocks):
        own = counts[b * devices : (b + 1) * devices]
        mine = owner[b : b + 1, :]
        rank = jnp.sum(
            jnp.where(mine == owners, own[:, :LANES] + start, 0.0), axis=0, keepdims=True
        ).astype(jnp.int32)
        start = start + own[:, LANES:]
        hi = mine * per_owner + lax.shift_right_logical(rank, 7)
        lo = rank & (LANES - 1)
        slot_ref[b : b + 1, :] = hi * LANES + lo
        value = surface[b : b + 1, :]
        coarse = (value & ~255).astype(F32)
        fine = (value & 255).astype(F32)
        at = slice(b * LANES, (b + 1) * LANES)
        lhs[0:table, at] = jnp.where(highs == hi, coarse, 0.0).astype(BF16)
        lhs[table : 2 * table, at] = jnp.where(highs == hi, fine, 0.0).astype(BF16)
        rhs[:, at] = jnp.where(lows == lo, 1.0, 0.0).astype(BF16)
    both = dot_lanes(lhs[...], rhs[...])
    idx_ref[...] = both[0:table] + both[table : 2 * table]
    place = cell[...]
    row_ref[...] = lax.div(lax.rem(place, cols), LANES) * rows + lax.div(place, cols)


def shifted(tiles, lane):
    count = len(tiles)
    left = [pltpu.roll(x, LANES - 1, 1) for x in tiles]
    right = [pltpu.roll(x, 1, 1) for x in tiles]
    after = [jnp.where(lane == LANES - 1, left[(i + 1) % count], left[i]) for i in range(count)]
    before = [jnp.where(lane == 0, right[i - 1], right[i]) for i in range(count)]
    return after, before


def gas_kernel(
    tiles_across, per_owner, gas, speed, w, ra, rb, rowidx, cell, owner, surface, slot, film, wall, idx,
    out, route, gx, sx, s1, tab, stage, lhs, rhs, sums, sem,
):
    rows, cols = gas.shape
    nt = cols // LANES
    devices = route.shape[0]
    blocks = owner.shape[0]
    table = idx.shape[0]
    copies = []
    for ct in range(nt):
        at = pl.ds(ct * LANES, LANES)
        copies.append(pltpu.make_async_copy(gas.at[:, at], gx.at[ct, pl.ds(ROWS, rows)], sem.at[0, ct]))
        copies.append(pltpu.make_async_copy(speed.at[:, at], sx.at[ct], sem.at[1, ct]))
    for copy in copies:
        copy.start()
    gh, sh = gas_halo_tiles(w[...])
    gx[nt, ROWS : ROWS + rows, :] = gh
    sx[nt] = sh
    is_even = even("passage")
    place = lax.axis_index("passage")
    in_top = jnp.where(place > 0, 1.0, 0.0)
    in_bottom = jnp.where(place < lax.axis_size("passage") - 1, 1.0, 0.0)

    def top(row, ct):
        at = slice(ct * LANES, (ct + 1) * LANES)
        return jnp.where(is_even, rb[row : row + 1, at], ra[row : row + 1, at])

    def bottom(row, ct):
        at = slice(ct * LANES, (ct + 1) * LANES)
        return jnp.where(is_even, ra[row : row + 1, at], rb[row : row + 1, at])

    for ct in range(nt + 1):
        gx[ct, ROWS - 1 : ROWS, :] = top(0, ct)
        gx[ct, ROWS + rows : ROWS + rows + 1, :] = bottom(0, ct)
    for copy in copies:
        copy.wait()
    for ct in range(nt):
        s1[ct, ROWS - 1 : ROWS, :] = in_top * (top(8, ct) + DIFFUSE * gx[ct, ROWS : ROWS + 1, :])
        s1[ct, ROWS + rows : ROWS + rows + 1, :] = in_bottom * (
            bottom(8, ct) + DIFFUSE * gx[ct, ROWS + rows - 1 : ROWS + rows, :]
        )
    lane = iota((ROWS, LANES), 1)

    def tendency(v, north, south, after, before, s):
        return DIFFUSE * (south + north + after + before - 4.0 * v) - s * (v - before)

    def first(i, carry):
        r0 = pl.multiple_of(i * ROWS, ROWS)
        v = [gx[ct, pl.ds(ROWS + r0, ROWS), :] for ct in range(nt + 1)]
        after, before = shifted(v, lane)
        for ct in range(nt + 1):
            north = gx[ct, pl.ds(ROWS - 1 + r0, ROWS), :]
            south = gx[ct, pl.ds(ROWS + 1 + r0, ROWS), :]
            s = sx[ct, pl.ds(r0, ROWS), :]
            new = v[ct] + tendency(v[ct], north, south, after[ct], before[ct], s)
            if ct == nt:
                new = jnp.where(s > 0, new, 0.0)
            s1[ct, pl.ds(ROWS + r0, ROWS), :] = new
        return carry

    lax.fori_loop(0, rows // ROWS, first, 0, unroll=4)

    def second(i, carry):
        r0 = pl.multiple_of(i * ROWS, ROWS)
        v = [s1[ct, pl.ds(ROWS + r0, ROWS), :] for ct in range(nt + 1)]
        after, before = shifted(v, lane)
        for ct in range(nt):
            north = s1[ct, pl.ds(ROWS - 1 + r0, ROWS), :]
            south = s1[ct, pl.ds(ROWS + 1 + r0, ROWS), :]
            s = sx[ct, pl.ds(r0, ROWS), :]
            g = gx[ct, pl.ds(ROWS + r0, ROWS), :]
            tab[pl.ds(ct * rows + r0, ROWS), :] = 0.5 * (
                g + v[ct] + tendency(v[ct], north, south, after[ct], before[ct], s)
            )
        return carry

    lax.fori_loop(0, rows // ROWS, second, 0, unroll=4)
    outs = [
        pltpu.make_async_copy(tab.at[pl.ds(ct * rows, rows)], out.at[:, pl.ds(ct * LANES, LANES)], sem.at[0, ct])
        for ct in range(nt)
    ]
    for copy in outs:
        copy.start()
    sub = iota((ROWS, LANES), 0)
    unroll = 8

    def gather(i, carry):
        base = pl.multiple_of(i * (ROWS * unroll), ROWS * unroll)
        for g in range(unroll):
            acc = jnp.broadcast_to(tab[pl.ds(rowidx[base + g * ROWS], 1), :], (ROWS, LANES))
            for j in range(1, ROWS):
                row = tab[pl.ds(rowidx[base + g * ROWS + j], 1), :]
                acc = jnp.where(sub == j, jnp.broadcast_to(row, (ROWS, LANES)), acc)
            stage[pl.ds(base + g * ROWS, ROWS), :] = acc
        return carry

    lax.fori_loop(0, stage.shape[0] // (ROWS * unroll), gather, 0)
    lanes_down = iota((LANES, LANES), 0)
    highs = iota((table, LANES), 0)
    owners = iota((devices, LANES), 0)
    part = table + devices
    for b in range(blocks):
        at = slice(b * LANES, (b + 1) * LANES)
        picked = jnp.where(lanes_down == (cell[b : b + 1, :] & (LANES - 1)), stage[at, :].T, 0.0)
        face = jnp.sum(picked, axis=0, keepdims=True)
        heat = split3(film[b : b + 1, :] * (face - wall[b : b + 1, :]))
        place_of = slot[b : b + 1, :]
        hi = lax.shift_right_logical(place_of, 7)
        lo = place_of & (LANES - 1)
        mine = owner[b : b + 1, :]
        voxel = surface[b : b + 1, :]
        line = lax.div(voxel, cols)
        col = lax.rem(voxel, cols)
        tile = lax.rem(mine, tiles_across)
        to_right = (col >= cols - EDGE) & (tile < tiles_across - 1)
        to_left = (col < EDGE) & (tile > 0)
        dest = jnp.where(to_right, mine + 1, jnp.where(to_left, mine - 1, -1))
        code = jnp.where(to_right, col - (cols - EDGE), 16 + col) + 8 * line
        for k in range(3):
            lhs[k * part : k * part + table, at] = jnp.where(highs == hi, heat[k], 0.0).astype(BF16)
            lhs[k * part + table : (k + 1) * part, at] = jnp.where(owners == dest, heat[k], 0.0).astype(BF16)
        rhs[0:LANES, at] = jnp.where(lanes_down == lo, 1.0, 0.0).astype(BF16)
        rhs[LANES : LANES + 32, at] = jnp.where(iota((32, LANES), 0) == code, 1.0, 0.0).astype(BF16)
    three = dot_lanes(lhs[...], rhs[...])
    sums[...] = three[0:part] + three[part : 2 * part] + three[2 * part : 3 * part]
    route[...] = jnp.zeros_like(route)
    for o in range(devices):
        own = slice(o * per_owner, (o + 1) * per_owner)
        route[o, 0:per_owner, :] = sums[own, 0:LANES]
        route[o, per_owner : 2 * per_owner, :] = idx[own, :]
        route[o, 2 * per_owner : 2 * per_owner + 1, 0:32] = sums[table + o : table + o + 1, LANES : LANES + 32]
    for copy in outs:
        copy.wait()


def strip_kernel(per_owner, recv, ra, rb, w, solid, material, token, top_ref, up_ref, ret_ref, lhs, rhs, dep, src, tabu):
    devices = recv.shape[0]
    cols = solid.shape[1]
    nt = cols // LANES
    wide = cols + LANES
    high = 2 * nt
    highs = iota((high, LANES), 0)
    lanes_down = iota((LANES, LANES), 0)
    for d in range(devices):
        for q in range(per_owner):
            at = slice((d * per_owner + q) * LANES, (d * per_owner + q + 1) * LANES)
            heat = split3(recv[d, q : q + 1, :])
            where = recv[d, per_owner + q : per_owner + q + 1, :].astype(jnp.int32)
            hi = lax.shift_right_logical(where, 7)
            for k in range(3):
                lhs[k * high : (k + 1) * high, at] = jnp.where(highs == hi, heat[k], 0.0).astype(BF16)
            rhs[:, at] = jnp.where(lanes_down == (where & (LANES - 1)), 1.0, 0.0).astype(BF16)
    three = dot_lanes(lhs[...], rhs[...])
    dep[...] = three[0:high] + three[high : 2 * high] + three[2 * high : 3 * high]
    edges = recv[0, 2 * per_owner : 2 * per_owner + 1, :]
    for d in range(1, devices):
        edges = edges + recv[d, 2 * per_owner : 2 * per_owner + 1, :]
    src[...] = jnp.zeros_like(src)
    lane = iota((1, LANES), 1)
    for line in range(2):
        for ct in range(nt):
            src[line : line + 1, ct * LANES : (ct + 1) * LANES] = dep[line * nt + ct : line * nt + ct + 1, :]
        left = pltpu.roll(edges, LANES - EDGE - 8 * line, 1)
        right = pltpu.roll(edges, LANES - 16 - 8 * line, 1)
        src[line : line + 1, cols:wide] = jnp.where(
            lane >= LANES - EDGE, left, jnp.where(lane < EDGE, right, 0.0)
        )
    is_even = even("passage")
    row8 = iota((ROWS, wide), 0)

    def above(at):
        return jnp.where(row8 > 0, jnp.where(is_even, rb[at : at + ROWS, :], ra[at : at + ROWS, :]), 0.0)

    uh, kh = halo_tiles(w[...])
    u = jnp.concatenate([above(0), jnp.concatenate([solid[...], uh], axis=1)], axis=0)
    k0 = jnp.concatenate([above(8), jnp.concatenate([base_conductivity(material[...]), kh], axis=1)], axis=0)
    inside = jnp.where(k0 > 0, 0.5 * SOLID_STEP, 0.0)
    source = jnp.concatenate(
        [jnp.zeros((ROWS, wide), F32), 2.0 * src[...], jnp.zeros((ROWS, wide), F32)], axis=0
    )
    high_rows = 3 * ROWS
    for _ in range(SUBSTEPS):
        k = k0 * jnp.exp(SOFTEN * u)
        across = (k + pltpu.roll(k, wide - 1, 1)) * (pltpu.roll(u, wide - 1, 1) - u)
        down = (k + pltpu.roll(k, high_rows - 1, 0)) * (pltpu.roll(u, high_rows - 1, 0) - u)
        flux = across - pltpu.roll(across, 1, 1) + down - pltpu.roll(down, 1, 0)
        u = u + inside * (flux + source)
    up_ref[...] = u[0:ROWS, 0:cols]
    top_ref[...] = u[ROWS : 2 * ROWS, 0:cols]
    for line in range(2):
        for ct in range(nt):
            tabu[line * nt + ct : line * nt + ct + 1, :] = top_ref[line : line + 1, ct * LANES : (ct + 1) * LANES]
    parts = jnp.concatenate(split3(tabu[...]), axis=0).astype(BF16)
    for d in range(devices):
        for q in range(per_owner):
            at = slice((d * per_owner + q) * LANES, (d * per_owner + q + 1) * LANES)
            x = dot(parts, rhs[:, at])
            x = x[0:high] + x[high : 2 * high] + x[2 * high : 3 * high]
            where = recv[d, per_owner + q : per_owner + q + 1, :].astype(jnp.int32)
            hi = lax.shift_right_logical(where, 7)
            ret_ref[d, q : q + 1, :] = jnp.sum(jnp.where(highs == hi, x, 0.0), axis=0, keepdims=True)


def bulk_kernel(first, last_half, solid, material, w, ra, rb, after, *rest):
    out, ua, ub, ka, kb, k0, k1, mat, sem = rest[1:] if last_half else rest[:1] + rest[2:]
    rows, cols = solid.shape
    half = mat.shape[1] - ROWS
    top = first - ROWS if last_half else first
    count = half + ROWS
    nt = cols // LANES
    copies = []
    for ct in range(nt):
        at = pl.ds(ct * LANES, LANES)
        copies.append(
            pltpu.make_async_copy(solid.at[pl.ds(top, count), at], ua.at[ct, pl.ds(ROWS, count)], sem.at[0, ct])
        )
        copies.append(pltpu.make_async_copy(material.at[pl.ds(top, count), at], mat.at[ct], sem.at[1, ct]))
    for copy in copies:
        copy.start()
    uh, kh = halo_tiles(w[top : top + count, :])
    ua[nt, ROWS : ROWS + count, :] = uh
    k0[nt] = kh
    ka[nt, ROWS : ROWS + count, :] = kh * jnp.exp(SOFTEN * uh)
    is_even = even("passage")
    zero = jnp.zeros((ROWS, LANES), F32)
    for ct in range(nt + 1):
        at = slice(ct * LANES, (ct + 1) * LANES)
        if last_half:
            below = jnp.where(is_even, ra[1:2, at], rb[1:2, at])
            below_k = jnp.where(is_even, ra[9:10, at], rb[9:10, at]) * jnp.exp(SOFTEN * below)
        for u, k in ((ua, ka), (ub, kb)):
            u[ct, 0:ROWS, :] = zero
            k[ct, 0:ROWS, :] = zero
            if last_half:
                u[ct, ROWS + count : ROWS + count + 1, :] = below
                k[ct, ROWS + count : ROWS + count + 1, :] = below_k
            else:
                u[ct, ROWS + count : 2 * ROWS + count, :] = zero
                k[ct, ROWS + count : 2 * ROWS + count, :] = zero
    for copy in copies:
        copy.wait()
    lane = iota((ROWS, LANES), 1)
    edge = lane == LANES - 1

    def begin(i, carry):
        r0 = pl.multiple_of(i * ROWS, ROWS)
        bases = []
        for ct in range(nt):
            base = base_conductivity(mat[ct, pl.ds(r0, ROWS), :])
            k0[ct, pl.ds(r0, ROWS), :] = base
            ka[ct, pl.ds(ROWS + r0, ROWS), :] = base * jnp.exp(SOFTEN * ua[ct, pl.ds(ROWS + r0, ROWS), :])
            bases.append(base)
        bases.append(k0[nt, pl.ds(r0, ROWS), :])
        turned = [pltpu.roll(x, LANES - 1, 1) for x in bases]
        for ct in range(nt + 1):
            k1[ct, pl.ds(r0, ROWS), :] = jnp.where(edge, turned[(ct + 1) % (nt + 1)], turned[ct])
        return carry

    lax.fori_loop(0, count // ROWS, begin, 0, unroll=2)
    for step in range(SUBSTEPS):
        final = step == SUBSTEPS - 1
        u, k, nu, nk = (ua, ka, ub, kb) if step % 2 == 0 else (ub, kb, ua, ka)

        def body(i, carry, u=u, k=k, nu=nu, nk=nk, final=final):
            r0 = pl.multiple_of(i * ROWS, ROWS)
            at = pl.ds(ROWS + r0, ROWS)
            north, south = pl.ds(ROWS - 1 + r0, ROWS), pl.ds(ROWS + 1 + r0, ROWS)
            here = [u[ct, at, :] for ct in range(nt + 1)]
            cond = [k[ct, at, :] for ct in range(nt + 1)]
            turned = [pltpu.roll(x, LANES - 1, 1) for x in here]
            across = []
            for ct in range(nt + 1):
                nearby = jnp.where(edge, turned[(ct + 1) % (nt + 1)], turned[ct])
                nearby_k = k1[ct, pl.ds(r0, ROWS), :] * jnp.exp(SOFTEN * nearby)
                across.append((cond[ct] + nearby_k) * (nearby - here[ct]))
            back = [pltpu.roll(x, 1, 1) for x in across]
            for ct in range(nt if final else nt + 1):
                flux = across[ct] - jnp.where(lane == 0, back[ct - 1], back[ct])
                flux = flux + (cond[ct] + k[ct, north, :]) * (u[ct, north, :] - here[ct])
                flux = flux + (cond[ct] + k[ct, south, :]) * (u[ct, south, :] - here[ct])
                base = k0[ct, pl.ds(r0, ROWS), :]
                if ct == nt:
                    flux = jnp.where(base > 0, flux, 0.0)
                new = here[ct] + 0.5 * SOLID_STEP * flux
                nu[ct, at, :] = new
                if not final:
                    nk[ct, at, :] = base * jnp.exp(SOFTEN * new)
            return carry

        lax.fori_loop(0, count // ROWS, body, 0, unroll=4)
    final = ua if SUBSTEPS % 2 == 0 else ub
    skip = ROWS if last_half else 0
    outs = [
        pltpu.make_async_copy(
            final.at[ct, pl.ds(ROWS + skip, half)],
            out.at[pl.ds(first, half), pl.ds(ct * LANES, LANES)],
            sem.at[0, ct],
        )
        for ct in range(nt)
    ]
    for copy in outs:
        copy.start()
    if not last_half:
        rest[1][...] = zero
    for copy in outs:
        copy.wait()


def finish_kernel(recv, slot, top, below, solid, wall_ref, out, tabl, edge, sem):
    devices, per_owner = recv.shape[0], recv.shape[1]
    rows = solid.shape[0]
    keep = rows - EDGE
    fetch = pltpu.make_async_copy(out.at[pl.ds(rows - ROWS, ROWS)], edge, sem.at[0])
    fetch.start()
    put = pltpu.make_async_copy(top, out.at[pl.ds(0, ROWS)], sem.at[1])
    put.start()
    for d in range(devices):
        tabl[d * per_owner : (d + 1) * per_owner, :] = recv[d]
    table = tabl.shape[0]
    parts = jnp.concatenate(split3(tabl[...]), axis=0).astype(BF16)
    highs, lanes_down = iota((table, LANES), 0), iota((LANES, LANES), 0)
    fetch.wait()
    last = lax.axis_index("passage") == lax.axis_size("passage") - 1
    row = iota(edge.shape, 0) + (rows - ROWS)
    edge[...] = jnp.where((row >= keep) & jnp.logical_not(last), below[...], edge[...])
    store = pltpu.make_async_copy(edge, out.at[pl.ds(rows - ROWS, ROWS)], sem.at[0])
    store.start()
    for b in range(slot.shape[0]):
        place = slot[b : b + 1, :]
        lows = jnp.where(lanes_down == (place & (LANES - 1)), 1.0, 0.0).astype(BF16)
        x = dot(parts, lows)
        x = x[0:table] + x[table : 2 * table] + x[2 * table : 3 * table]
        hi = lax.shift_right_logical(place, 7)
        wall_ref[b : b + 1, :] = jnp.sum(jnp.where(highs == hi, x, 0.0), axis=0, keepdims=True)
    put.wait()
    store.wait()


def shards(gas, gas_speed, solid, material, face_cell, face_owner, face_surface, film, wall_previous):
    passages = lax.axis_size("passage")
    tiles = lax.axis_size("tile")
    devices = passages * tiles
    rows, cols = solid.shape
    nt = cols // LANES
    faces = face_cell.shape[0]
    blocks = faces // LANES
    cap = 2 * faces // devices
    per_owner = max(1, cap // LANES)
    table = devices * per_owner
    wide = cols + LANES

    def shape(dims, kind=F32):
        return jax.ShapeDtypeStruct(dims, kind)

    def cost(flops, moved, hard=0):
        return pl.CostEstimate(flops=flops, bytes_accessed=moved, transcendentals=hard)

    fields = (gas, gas_speed, solid, material)
    left = pl.BlockSpec((rows, LANES), lambda i: (0, 0))
    right = pl.BlockSpec((rows, LANES), lambda i: (0, nt - 1))
    column = pl.BlockSpec((16, rows), lambda i: (0, 0))
    one, two = pl.pallas_call(
        pack_columns,
        grid=(1,),
        compiler_params=params(60),
        in_specs=[left, right] * 4,
        out_specs=[column, column],
        out_shape=[shape((16, rows))] * 2,
        name="pack_columns",
        cost_estimate=cost(1000000, 8 * rows * LANES * 4),
    )(*[x for field in fields for x in (field, field)])
    one, two = pair_swaps("tile", tiles)(one, two)

    def tall(count, row):
        return pl.BlockSpec((count, cols), lambda i: (row, 0))

    full = pl.BlockSpec((rows, LANES), lambda i: (0, 0))
    band = pl.BlockSpec((16, wide), lambda i: (0, 0))
    w, ra, rb = pl.pallas_call(
        pack_rows,
        grid=(1,),
        compiler_params=params(60),
        in_specs=[column, column] + [tall(ROWS, 0), tall(ROWS, rows // ROWS - 1)] * 4,
        out_specs=[full, band, band],
        out_shape=[shape((rows, LANES)), shape((16, wide)), shape((16, wide))],
        scratch_shapes=[VMEM((LANES, rows), F32)],
        name="pack_rows",
        cost_estimate=cost(1000000, 8 * ROWS * cols * 4),
    )(one, two, *[x for field in fields for x in (field, field)])
    ra, rb = pair_swaps("passage", passages)(ra, rb)

    def folded(x):
        return x.reshape(blocks, LANES)

    owner, surface, cell = folded(face_owner), folded(face_surface), folded(face_cell)
    slot, rowidx, idx = pl.pallas_call(
        functools.partial(find_slots, devices, per_owner, rows, cols),
        in_specs=[whole()] * 3,
        out_specs=[whole()] * 3,
        out_shape=[shape((blocks, LANES), jnp.int32), shape((blocks, LANES), jnp.int32), shape((table, LANES))],
        scratch_shapes=[
            VMEM((blocks * devices, LANES), BF16),
            VMEM((2 * table, faces), BF16),
            VMEM((LANES, faces), BF16),
        ],
        compiler_params=params(60),
        name="find_slots",
        cost_estimate=cost(20000000, 1000000),
    )(owner, surface, cell)

    part = table + devices
    gas_next, route = pl.pallas_call(
        functools.partial(gas_kernel, tiles, per_owner),
        in_specs=[whole(pl.ANY)] * 2 + [whole()] * 3 + [whole(pltpu.SMEM)] + [whole()] * 7,
        out_specs=[whole(pl.ANY), whole()],
        out_shape=[shape((rows, cols)), shape((devices, ROUTE_ROWS, LANES))],
        scratch_shapes=[
            VMEM((nt + 1, rows + 2 * ROWS, LANES), F32),
            VMEM((nt + 1, rows, LANES), F32),
            VMEM((nt + 1, rows + 2 * ROWS, LANES), F32),
            VMEM((nt * rows, LANES), F32),
            VMEM((faces, LANES), F32),
            VMEM((3 * part, faces), BF16),
            VMEM((LANES + 32, faces), BF16),
            VMEM((part, LANES + 32), F32),
            pltpu.SemaphoreType.DMA((2, nt)),
        ],
        compiler_params=params(60),
        name="gas_and_heat",
        cost_estimate=cost(60000000, 40000000),
    )(
        gas, gas_speed, w, ra, rb, rowidx.reshape(faces), cell, owner, surface, slot,
        folded(film), folded(wall_previous), idx,
    )
    recv = lax.all_to_all(route, ("passage", "tile"), 0, 0, tiled=True)

    half = rows // 2 // ROWS * ROWS

    def bulk_half(first, count, after, whole_so_far):
        last_half = first > 0
        return pl.pallas_call(
            functools.partial(bulk_kernel, first, last_half),
            in_specs=[whole(pl.ANY)] * 2 + [whole()] * 3 + [whole(pl.ANY)] * (2 if last_half else 1),
            out_specs=[whole(pl.ANY)] + ([] if last_half else [whole()]),
            out_shape=[shape((rows, cols))] + ([] if last_half else [shape((ROWS, LANES))]),
            input_output_aliases={6: 0} if last_half else {},
            scratch_shapes=[VMEM((nt + 1, count + 3 * ROWS, LANES), F32)] * 4
            + [VMEM((nt + 1, count + ROWS, LANES), F32)] * 2
            + [
                VMEM((nt, count + ROWS, LANES), jnp.int32),
                pltpu.SemaphoreType.DMA((2, nt)),
            ],
            compiler_params=params(60),
            name="solid_bulk",
            cost_estimate=cost(60000000, 30000000),
        )(solid, material, w, ra, rb, after, *([whole_so_far] if last_half else []))

    bulk, token = bulk_half(0, half, gas_next, None)

    slots = table * LANES
    top, up, ret = pl.pallas_call(
        functools.partial(strip_kernel, per_owner),
        grid=(1,),
        in_specs=[
            pl.BlockSpec((devices, ROUTE_ROWS, LANES), lambda i: (0, 0, 0)),
            band,
            band,
            pl.BlockSpec((16, LANES), lambda i: (0, 0)),
            tall(16, 0),
            tall(16, 0),
            pl.BlockSpec((ROWS, LANES), lambda i: (0, 0)),
        ],
        out_specs=[
            pl.BlockSpec((ROWS, cols), lambda i: (0, 0)),
            pl.BlockSpec((ROWS, cols), lambda i: (0, 0)),
            pl.BlockSpec((devices, per_owner, LANES), lambda i: (0, 0, 0)),
        ],
        out_shape=[shape((ROWS, cols)), shape((ROWS, cols)), shape((devices, per_owner, LANES))],
        scratch_shapes=[
            VMEM((6 * nt, slots), BF16),
            VMEM((LANES, slots), BF16),
            VMEM((2 * nt, LANES), F32),
            VMEM((ROWS, wide), F32),
            VMEM((2 * nt, LANES), F32),
        ],
        compiler_params=params(60),
        name="solid_strip",
        cost_estimate=cost(20000000, 4000000),
    )(recv, ra, rb, w, solid, material, token)
    ret = lax.all_to_all(ret, ("passage", "tile"), 0, 0, tiled=True)
    below = lax.ppermute(up, "passage", [(i + 1, i) for i in range(passages - 1)])

    (bulk,) = bulk_half(half, rows - half, top, bulk)
    wall, solid_next = pl.pallas_call(
        finish_kernel,
        in_specs=[whole()] * 4 + [whole(pl.ANY)],
        out_specs=[whole(), whole(pl.ANY)],
        out_shape=[shape((blocks, LANES)), shape((rows, cols))],
        input_output_aliases={4: 1},
        scratch_shapes=[
            VMEM((table, LANES), F32),
            VMEM((ROWS, cols), F32),
            pltpu.SemaphoreType.DMA((2,)),
        ],
        compiler_params=params(60),
        name="wall_temperatures",
        cost_estimate=cost(20000000, 4000000),
    )(ret, slot, top, below, bulk)
    return gas_next, solid_next, wall.reshape(faces)


def solution(mesh):
    in_specs = (
        P("passage", "tile"),
        P("passage", "tile"),
        P("passage", "tile"),
        P("passage", "tile"),
        P(("passage", "tile")),
        P(("passage", "tile"), None),
        P(("passage", "tile")),
        P(("passage", "tile")),
        P(("passage", "tile")),
    )
    out_specs = (P("passage", "tile"), P("passage", "tile"), P(("passage", "tile")))
    return jax.shard_map(shards, mesh=mesh, in_specs=in_specs, out_specs=out_specs, check_vma=False)
```

```python
import functools

import jax
import jax.numpy as jnp
from jax import lax
from jax.experimental import pallas as pl
from jax.experimental.pallas import tpu as pltpu
from jax.sharding import PartitionSpec as P

SUBSTEPS = 4
DIFFUSE = 0.05
SOLID_STEP = 0.1
SOFTEN = 0.08
SCALE = SOFTEN * 1.4426950408889634
SHARE = 0.5 * SOLID_STEP
LANES = 128
ROWS = 8
ROUTE_ROWS = 8
EDGE = SUBSTEPS - 1
F32 = jnp.float32
BF16 = jnp.bfloat16
VMEM = pltpu.VMEM
MIB = 2**20


def params(mib):
    return pltpu.CompilerParams(vmem_limit_bytes=int(mib * MIB))


def whole(space=pltpu.VMEM):
    return pl.BlockSpec(memory_space=space)


def iota(shape, dim):
    return lax.broadcasted_iota(jnp.int32, shape, dim)


def base_conductivity(material, share=1.0):
    return jnp.where(
        material == 0,
        jnp.float32(share),
        jnp.where(material == 1, jnp.float32(0.3 * share), jnp.float32(0.08 * share)),
    )


def even(axis):
    return lax.rem(lax.axis_index(axis), 2) == 0


def split3(x):
    one = x.astype(BF16).astype(F32)
    rest = x - one
    two = rest.astype(BF16).astype(F32)
    return one, two, (rest - two).astype(BF16).astype(F32)


def dot_lanes(a, b):
    return lax.dot_general(a, b, (((1,), (1,)), ((), ())), preferred_element_type=F32)


def dot(a, b):
    return lax.dot_general(a, b, (((1,), (0,)), ((), ())), preferred_element_type=F32)


def pair_swaps(axis, count):
    first = [(i, i + 1) for i in range(0, count - 1, 2)]
    second = [(i, i + 1) for i in range(1, count - 1, 2)]

    def both(pairs):
        return pairs + [(b, a) for a, b in pairs]

    def run(one, two):
        return lax.ppermute(one, axis, both(first)), lax.ppermute(two, axis, both(second))

    return run


def pack_columns(gas, speed, solid, material, one_ref, two_ref, top_f, top_m, tiles, tile_m, sem):
    size, cols = gas.shape
    fields = (gas, speed, solid)
    ends = (pl.ds(0, LANES), pl.ds(cols - LANES, LANES))
    bands = (pl.ds(0, ROWS), pl.ds(size - ROWS, ROWS))
    tall, flat = [], []
    for e in range(2):
        for f in range(3):
            tall.append(pltpu.make_async_copy(fields[f].at[:, ends[e]], tiles.at[2 * f + e], sem.at[0, 4 * e + f]))
        tall.append(pltpu.make_async_copy(material.at[:, ends[e]], tile_m.at[e], sem.at[0, 4 * e + 3]))
    for e in range(2):
        for f in range(3):
            flat.append(pltpu.make_async_copy(fields[f].at[bands[e], :], top_f.at[2 * f + e], sem.at[1, 4 * e + f]))
        flat.append(pltpu.make_async_copy(material.at[bands[e], :], top_m.at[e], sem.at[1, 4 * e + 3]))
    for copy in tall + flat:
        copy.start()
    for copy in tall:
        copy.wait()
    lane = iota((size, LANES), 1)
    head = jnp.where(
        lane < 4,
        tiles[4],
        jnp.where(
            lane < 8,
            pltpu.roll(base_conductivity(tile_m[0]), 4, 1),
            jnp.where(lane < 10, pltpu.roll(tiles[0], 8, 1), pltpu.roll(tiles[2], 10, 1)),
        ),
    )
    tail = jnp.where(
        lane >= 124,
        tiles[5],
        jnp.where(
            lane >= 120,
            pltpu.roll(base_conductivity(tile_m[1]), 124, 1),
            jnp.where(lane >= 118, pltpu.roll(tiles[1], 120, 1), pltpu.roll(tiles[3], 118, 1)),
        ),
    )
    head = head.T[0:16]
    tail = tail.T[112:128]
    is_even = even("tile")
    one_ref[...] = jnp.where(is_even, tail, head)
    two_ref[...] = jnp.where(is_even, head, tail)
    for copy in flat:
        copy.wait()


def halo_tiles(w):
    lane = iota(w.shape, 1)
    zero = jnp.zeros_like(w)
    solid = jnp.where((lane < 4) | (lane >= 124), w, zero)
    conduct = jnp.where(
        lane < 4, pltpu.roll(w, 124, 1), jnp.where(lane >= 124, pltpu.roll(w, 4, 1), zero)
    )
    return solid, conduct


def gas_halo_tiles(w):
    lane = iota(w.shape, 1)
    zero = jnp.zeros_like(w)
    gas = jnp.where(
        lane < 2, pltpu.roll(w, 120, 1), jnp.where(lane >= 126, pltpu.roll(w, 8, 1), zero)
    )
    speed = jnp.where(
        lane < 1, pltpu.roll(w, 118, 1), jnp.where(lane >= 127, pltpu.roll(w, 10, 1), zero)
    )
    return gas, speed


def pack_rows(one, two, edges, edge_m, w_ref, a_ref, b_ref, wt):
    is_even = even("tile")
    wt[...] = jnp.zeros_like(wt)
    wt[0:16, :] = jnp.where(is_even, one[...], two[...])
    wt[112:128, :] = jnp.where(is_even, two[...], one[...])
    w = wt[...].T
    w_ref[...] = w
    size = w.shape[0]
    wide = edges.shape[2] + LANES

    def rows(e, part, step):
        g, s, u, m = edges.at[e], edges.at[2 + e], edges.at[4 + e], edge_m.at[e]
        uh, kh = halo_tiles(part)
        gh, sh = gas_halo_tiles(part)
        g = jnp.concatenate([g[...], gh], axis=1)
        s = jnp.concatenate([s[...], sh], axis=1)
        u = jnp.concatenate([u[...], uh], axis=1)
        k = jnp.concatenate([base_conductivity(m[...]), kh], axis=1)
        before = pltpu.roll(g, 1, 1)
        after = pltpu.roll(g, wide - 1, 1)
        inner = pltpu.roll(g, step, 0)
        partial = g - s * (g - before) + DIFFUSE * (inner + before + after - 4.0 * g)
        return g, partial, u, k

    row = iota((ROWS, wide), 0)
    zero = jnp.zeros((ROWS, wide), F32)
    g, partial, u, k = rows(0, w[0:ROWS], ROWS - 1)

    def first_two(x, y):
        return jnp.where(row == 0, x, jnp.where(row == 1, pltpu.roll(y, 1, 0), zero))

    up = (first_two(g, u), first_two(partial, k))
    g, partial, u, k = rows(1, w[size - ROWS : size], 1)

    def last_rows(x, y):
        return jnp.where(row == 0, pltpu.roll(x, 1, 0), y)

    down = (last_rows(g, u), last_rows(partial, k))
    is_even = even("passage")
    for half in range(2):
        a_ref[half * ROWS : (half + 1) * ROWS, :] = jnp.where(is_even, down[half], up[half])
        b_ref[half * ROWS : (half + 1) * ROWS, :] = jnp.where(is_even, up[half], down[half])


def find_slots(devices, per_owner, rows, cols, owner, surface, cell, slot_ref, row_ref, idx_ref, held, lhs, rhs):
    blocks = owner.shape[0]
    owners = iota((devices, LANES), 0)
    for b in range(blocks):
        held[b * devices : (b + 1) * devices, :] = jnp.where(owner[b : b + 1, :] == owners, 1.0, 0.0).astype(BF16)
    r, c = iota((LANES, 2 * LANES), 0), iota((LANES, 2 * LANES), 1)
    before = jnp.where((r < c) | (c >= LANES), 1.0, 0.0).astype(BF16)
    counts = dot(held[...], before)
    high = slot_ref.shape[0]
    table = idx_ref.shape[0]
    start = jnp.zeros((devices, LANES), F32)
    highs, lows = iota((table, LANES), 0), iota((LANES, LANES), 0)
    for b in range(blocks):
        own = counts[b * devices : (b + 1) * devices]
        mine = owner[b : b + 1, :]
        rank = jnp.sum(
            jnp.where(mine == owners, own[:, :LANES] + start, 0.0), axis=0, keepdims=True
        ).astype(jnp.int32)
        start = start + own[:, LANES:]
        hi = mine * per_owner + lax.shift_right_logical(rank, 7)
        lo = rank & (LANES - 1)
        slot_ref[b : b + 1, :] = hi * LANES + lo
        value = surface[b : b + 1, :]
        coarse = (value & ~255).astype(F32)
        fine = (value & 255).astype(F32)
        at = slice(b * LANES, (b + 1) * LANES)
        lhs[0:table, at] = jnp.where(highs == hi, coarse, 0.0).astype(BF16)
        lhs[table : 2 * table, at] = jnp.where(highs == hi, fine, 0.0).astype(BF16)
        rhs[:, at] = jnp.where(lows == lo, 1.0, 0.0).astype(BF16)
    both = dot_lanes(lhs[...], rhs[...])
    idx_ref[...] = both[0:table] + both[table : 2 * table]
    place = cell[...]
    row_ref[...] = lax.div(lax.rem(place, cols), LANES) * rows + lax.div(place, cols)


def shifted(tiles, lane):
    count = len(tiles)
    left = [pltpu.roll(x, LANES - 1, 1) for x in tiles]
    right = [pltpu.roll(x, 1, 1) for x in tiles]
    after = [jnp.where(lane == LANES - 1, left[(i + 1) % count], left[i]) for i in range(count)]
    before = [jnp.where(lane == 0, right[i - 1], right[i]) for i in range(count)]
    return after, before


def gas_kernel(
    tiles_across, per_owner, gas, speed, w, ra, rb, rowidx, cell, owner, surface, slot, film, wall, idx,
    out, route, gx, sx, sh, s1, tab, final, stage, lhs, rhs, sums, sem,
):
    rows, cols = gas.shape
    nt = cols // LANES
    devices = route.shape[0]
    blocks = owner.shape[0]
    table = idx.shape[0]
    copies = [pltpu.make_async_copy(speed, sx, sem.at[1, 0])]
    for ct in range(nt):
        at = pl.ds(ct * LANES, LANES)
        copies.append(pltpu.make_async_copy(gas.at[:, at], gx.at[ct, pl.ds(ROWS, rows)], sem.at[0, ct]))
    for copy in copies:
        copy.start()
    gh, speed_halo = gas_halo_tiles(w[...])
    gx[nt, ROWS : ROWS + rows, :] = gh
    sh[...] = speed_halo
    is_even = even("passage")
    place = lax.axis_index("passage")
    in_top = jnp.where(place > 0, 1.0, 0.0)
    in_bottom = jnp.where(place < lax.axis_size("passage") - 1, 1.0, 0.0)

    def top(row, ct):
        at = slice(ct * LANES, (ct + 1) * LANES)
        return jnp.where(is_even, rb[row : row + 1, at], ra[row : row + 1, at])

    def bottom(row, ct):
        at = slice(ct * LANES, (ct + 1) * LANES)
        return jnp.where(is_even, ra[row : row + 1, at], rb[row : row + 1, at])

    for ct in range(nt + 1):
        gx[ct, ROWS - 1 : ROWS, :] = top(0, ct)
        gx[ct, ROWS + rows : ROWS + rows + 1, :] = bottom(0, ct)
    for copy in copies:
        copy.wait()
    for ct in range(nt):
        s1[ct, ROWS - 1 : ROWS, :] = in_top * (top(8, ct) + DIFFUSE * gx[ct, ROWS : ROWS + 1, :])
        s1[ct, ROWS + rows : ROWS + rows + 1, :] = in_bottom * (
            bottom(8, ct) + DIFFUSE * gx[ct, ROWS + rows - 1 : ROWS + rows, :]
        )
    lane = iota((ROWS, LANES), 1)

    def tendency(v, north, south, after, before, s):
        return DIFFUSE * (south + north + after + before - 4.0 * v) - s * (v - before)

    def first(i, carry):
        r0 = pl.multiple_of(i * ROWS, ROWS)
        v = [gx[ct, pl.ds(ROWS + r0, ROWS), :] for ct in range(nt + 1)]
        after, before = shifted(v, lane)
        for ct in range(nt + 1):
            north = gx[ct, pl.ds(ROWS - 1 + r0, ROWS), :]
            south = gx[ct, pl.ds(ROWS + 1 + r0, ROWS), :]
            s = sh[pl.ds(r0, ROWS), :] if ct == nt else sx[pl.ds(r0, ROWS), ct * LANES : (ct + 1) * LANES]
            new = v[ct] + tendency(v[ct], north, south, after[ct], before[ct], s)
            if ct == nt:
                new = jnp.where(s > 0, new, 0.0)
            s1[ct, pl.ds(ROWS + r0, ROWS), :] = new
        return carry

    lax.fori_loop(0, rows // ROWS, first, 0, unroll=4)

    def second(i, carry):
        r0 = pl.multiple_of(i * ROWS, ROWS)
        v = [s1[ct, pl.ds(ROWS + r0, ROWS), :] for ct in range(nt + 1)]
        after, before = shifted(v, lane)
        for ct in range(nt):
            north = s1[ct, pl.ds(ROWS - 1 + r0, ROWS), :]
            south = s1[ct, pl.ds(ROWS + 1 + r0, ROWS), :]
            at = slice(ct * LANES, (ct + 1) * LANES)
            s = sx[pl.ds(r0, ROWS), at]
            g = gx[ct, pl.ds(ROWS + r0, ROWS), :]
            new = 0.5 * (g + v[ct] + tendency(v[ct], north, south, after[ct], before[ct], s))
            tab[pl.ds(ct * rows + r0, ROWS), :] = new
            final[pl.ds(r0, ROWS), at] = new
        return carry

    lax.fori_loop(0, rows // ROWS, second, 0, unroll=4)
    put = pltpu.make_async_copy(final, out, sem.at[1, 0])
    put.start()
    sub = iota((ROWS, LANES), 0)
    unroll = 8

    def gather(i, carry):
        base = pl.multiple_of(i * (ROWS * unroll), ROWS * unroll)
        for g in range(unroll):
            acc = jnp.broadcast_to(tab[pl.ds(rowidx[base + g * ROWS], 1), :], (ROWS, LANES))
            for j in range(1, ROWS):
                row = tab[pl.ds(rowidx[base + g * ROWS + j], 1), :]
                acc = jnp.where(sub == j, jnp.broadcast_to(row, (ROWS, LANES)), acc)
            stage[pl.ds(base + g * ROWS, ROWS), :] = acc
        return carry

    lax.fori_loop(0, stage.shape[0] // (ROWS * unroll), gather, 0)
    lanes_down = iota((LANES, LANES), 0)
    highs = iota((table, LANES), 0)
    owners = iota((devices, LANES), 0)
    part = table + devices
    for b in range(blocks):
        at = slice(b * LANES, (b + 1) * LANES)
        picked = jnp.where(lanes_down == (cell[b : b + 1, :] & (LANES - 1)), stage[at, :].T, 0.0)
        face = jnp.sum(picked, axis=0, keepdims=True)
        heat = split3(film[b : b + 1, :] * (face - wall[b : b + 1, :]))
        place_of = slot[b : b + 1, :]
        hi = lax.shift_right_logical(place_of, 7)
        lo = place_of & (LANES - 1)
        mine = owner[b : b + 1, :]
        voxel = surface[b : b + 1, :]
        line = lax.div(voxel, cols)
        col = lax.rem(voxel, cols)
        tile = lax.rem(mine, tiles_across)
        to_right = (col >= cols - EDGE) & (tile < tiles_across - 1)
        to_left = (col < EDGE) & (tile > 0)
        dest = jnp.where(to_right, mine + 1, jnp.where(to_left, mine - 1, -1))
        code = jnp.where(to_right, col - (cols - EDGE), 16 + col) + 8 * line
        for k in range(3):
            lhs[k * part : k * part + table, at] = jnp.where(highs == hi, heat[k], 0.0).astype(BF16)
            lhs[k * part + table : (k + 1) * part, at] = jnp.where(owners == dest, heat[k], 0.0).astype(BF16)
        rhs[0:LANES, at] = jnp.where(lanes_down == lo, 1.0, 0.0).astype(BF16)
        rhs[LANES : LANES + 32, at] = jnp.where(iota((32, LANES), 0) == code, 1.0, 0.0).astype(BF16)
    three = dot_lanes(lhs[...], rhs[...])
    sums[...] = three[0:part] + three[part : 2 * part] + three[2 * part : 3 * part]
    route[...] = jnp.zeros_like(route)
    for o in range(devices):
        own = slice(o * per_owner, (o + 1) * per_owner)
        route[o, 0:per_owner, :] = sums[own, 0:LANES]
        route[o, per_owner : 2 * per_owner, :] = idx[own, :]
        route[o, 2 * per_owner : 2 * per_owner + 1, 0:32] = sums[table + o : table + o + 1, LANES : LANES + 32]
    put.wait()


def strip_kernel(
    per_owner, recv, ra, rb, w, solid, material, token, top_ref, up_ref, ret_ref, lhs, rhs, dep, src, tabu, su, sm, sem
):
    devices = recv.shape[0]
    cols = solid.shape[1]
    nt = cols // LANES
    wide = cols + LANES
    high = 2 * nt
    copies = [
        pltpu.make_async_copy(solid.at[pl.ds(0, 2 * ROWS)], su, sem.at[0]),
        pltpu.make_async_copy(material.at[pl.ds(0, 2 * ROWS)], sm, sem.at[1]),
    ]
    for copy in copies:
        copy.start()
    highs = iota((high, LANES), 0)
    lanes_down = iota((LANES, LANES), 0)
    for d in range(devices):
        for q in range(per_owner):
            at = slice((d * per_owner + q) * LANES, (d * per_owner + q + 1) * LANES)
            heat = split3(recv[d, q : q + 1, :])
            where = recv[d, per_owner + q : per_owner + q + 1, :].astype(jnp.int32)
            hi = lax.shift_right_logical(where, 7)
            for k in range(3):
                lhs[k * high : (k + 1) * high, at] = jnp.where(highs == hi, heat[k], 0.0).astype(BF16)
            rhs[:, at] = jnp.where(lanes_down == (where & (LANES - 1)), 1.0, 0.0).astype(BF16)
    three = dot_lanes(lhs[...], rhs[...])
    dep[...] = three[0:high] + three[high : 2 * high] + three[2 * high : 3 * high]
    edges = recv[0, 2 * per_owner : 2 * per_owner + 1, :]
    for d in range(1, devices):
        edges = edges + recv[d, 2 * per_owner : 2 * per_owner + 1, :]
    src[...] = jnp.zeros_like(src)
    lane = iota((1, LANES), 1)
    for line in range(2):
        for ct in range(nt):
            src[line : line + 1, ct * LANES : (ct + 1) * LANES] = dep[line * nt + ct : line * nt + ct + 1, :]
        left = pltpu.roll(edges, LANES - EDGE - 8 * line, 1)
        right = pltpu.roll(edges, LANES - 16 - 8 * line, 1)
        src[line : line + 1, cols:wide] = jnp.where(
            lane >= LANES - EDGE, left, jnp.where(lane < EDGE, right, 0.0)
        )
    is_even = even("passage")
    row8 = iota((ROWS, wide), 0)

    def above(at):
        return jnp.where(row8 > 0, jnp.where(is_even, rb[at : at + ROWS, :], ra[at : at + ROWS, :]), 0.0)

    uh, kh = halo_tiles(w[0 : 2 * ROWS, :])
    for copy in copies:
        copy.wait()
    u = jnp.concatenate([above(0), jnp.concatenate([su[...], uh], axis=1)], axis=0)
    k0 = jnp.concatenate([above(8), jnp.concatenate([base_conductivity(sm[...]), kh], axis=1)], axis=0)
    inside = jnp.where(k0 > 0, 0.5 * SOLID_STEP, 0.0)
    source = jnp.concatenate(
        [jnp.zeros((ROWS, wide), F32), 2.0 * src[...], jnp.zeros((ROWS, wide), F32)], axis=0
    )
    high_rows = 3 * ROWS
    for _ in range(SUBSTEPS):
        k = k0 * jnp.exp(SOFTEN * u)
        across = (k + pltpu.roll(k, wide - 1, 1)) * (pltpu.roll(u, wide - 1, 1) - u)
        down = (k + pltpu.roll(k, high_rows - 1, 0)) * (pltpu.roll(u, high_rows - 1, 0) - u)
        flux = across - pltpu.roll(across, 1, 1) + down - pltpu.roll(down, 1, 0)
        u = u + inside * (flux + source)
    for j in range(EDGE):
        for ct in range(nt):
            row = ROWS - EDGE + j
            up_ref[j, ct : ct + 1, :] = u[row : row + 1, ct * LANES : (ct + 1) * LANES]
    top_ref[...] = u[ROWS : 2 * ROWS, 0:cols]
    for line in range(2):
        for ct in range(nt):
            tabu[line * nt + ct : line * nt + ct + 1, :] = top_ref[line : line + 1, ct * LANES : (ct + 1) * LANES]
    parts = jnp.concatenate(split3(tabu[...]), axis=0).astype(BF16)
    for d in range(devices):
        for q in range(per_owner):
            at = slice((d * per_owner + q) * LANES, (d * per_owner + q + 1) * LANES)
            x = dot(parts, rhs[:, at])
            x = x[0:high] + x[high : 2 * high] + x[2 * high : 3 * high]
            where = recv[d, per_owner + q : per_owner + q + 1, :].astype(jnp.int32)
            hi = lax.shift_right_logical(where, 7)
            ret_ref[d, q : q + 1, :] = jnp.sum(jnp.where(highs == hi, x, 0.0), axis=0, keepdims=True)


def bulk_kernel(last_half, start, count, groups, solid, material, w, *refs):
    if last_half:
        ra, rb, top, so_far, out, low_ref, u0, m0, ua, ub, ka, kb, k0, k1, fin, sem = refs
    else:
        out, token, u0, m0, ua, ub, ka, kb, k0, k1, fin, sem = refs
    cols = solid.shape[1]
    nt = cols // LANES
    size = count // groups
    blocks = size // ROWS
    copies = []
    for g in range(groups):
        here, there = pl.ds(start + g * size, size), pl.ds(g * size, size)
        copies.append(pltpu.make_async_copy(solid.at[here], u0.at[there], sem.at[0, g]))
        copies.append(pltpu.make_async_copy(material.at[here], m0.at[there], sem.at[1, g]))
    for copy in copies:
        copy.start()
    if last_half:
        put = pltpu.make_async_copy(top, out.at[pl.ds(0, ROWS)], sem.at[2, 0])
        put.start()
    uh, kh = halo_tiles(w[start : start + count, :])
    ua[nt, ROWS : ROWS + count, :] = SCALE * uh
    k0[nt] = SHARE * kh
    zero = jnp.zeros((ROWS, LANES), F32)
    for ct in range(nt + 1):
        at = slice(ct * LANES, (ct + 1) * LANES)
        if last_half:
            is_even = even("passage")
            below = SCALE * jnp.where(is_even, ra[1:2, at], rb[1:2, at])
            below_k = SHARE * jnp.where(is_even, ra[9:10, at], rb[9:10, at]) * jnp.exp2(below)
        for u, k in ((ua, ka), (ub, kb)):
            u[ct, 0:ROWS, :] = zero
            k[ct, 0:ROWS, :] = zero
            if last_half:
                u[ct, ROWS + count : ROWS + count + 1, :] = below
                k[ct, ROWS + count : ROWS + count + 1, :] = below_k
            else:
                u[ct, ROWS + count : 2 * ROWS + count, :] = zero
                k[ct, ROWS + count : 2 * ROWS + count, :] = zero
    if not last_half:
        token[...] = zero
    lane = iota((ROWS, LANES), 1)
    edge = lane == LANES - 1

    def begin(i, carry):
        r0 = pl.multiple_of(i * ROWS, ROWS)
        bases = []
        for ct in range(nt + 1):
            if ct < nt:
                at = slice(ct * LANES, (ct + 1) * LANES)
                here = SCALE * u0[pl.ds(r0, ROWS), at]
                base = base_conductivity(m0[pl.ds(r0, ROWS), at], SHARE)
                ua[ct, pl.ds(ROWS + r0, ROWS), :] = here
                k0[ct, pl.ds(r0, ROWS), :] = base
            else:
                here = ua[ct, pl.ds(ROWS + r0, ROWS), :]
                base = k0[ct, pl.ds(r0, ROWS), :]
            ka[ct, pl.ds(ROWS + r0, ROWS), :] = base * jnp.exp2(here)
            bases.append(base)
        turned = [pltpu.roll(x, LANES - 1, 1) for x in bases]
        for ct in range(nt + 1):
            k1[ct, pl.ds(r0, ROWS), :] = jnp.where(edge, turned[(ct + 1) % (nt + 1)], turned[ct])
        return carry

    for g in range(groups):
        copies[2 * g].wait()
        copies[2 * g + 1].wait()
        lax.fori_loop(g * blocks, (g + 1) * blocks, begin, 0, unroll=True)

    def substep(u, k, nu, nk, final):
        def body(i, carry):
            r0 = pl.multiple_of(i * ROWS, ROWS)
            at = pl.ds(ROWS + r0, ROWS)
            north, south = pl.ds(ROWS - 1 + r0, ROWS), pl.ds(ROWS + 1 + r0, ROWS)
            here = [u[ct, at, :] for ct in range(nt + 1)]
            cond = [k[ct, at, :] for ct in range(nt + 1)]
            turned = [pltpu.roll(x, LANES - 1, 1) for x in here]
            across = []
            for ct in range(nt + 1):
                nearby = jnp.where(edge, turned[(ct + 1) % (nt + 1)], turned[ct])
                nearby_k = k1[ct, pl.ds(r0, ROWS), :] * jnp.exp2(nearby)
                across.append((cond[ct] + nearby_k) * (nearby - here[ct]))
            back = [pltpu.roll(x, 1, 1) for x in across]
            for ct in range(nt if final else nt + 1):
                flux = across[ct] - jnp.where(lane == 0, back[ct - 1], back[ct])
                flux = flux + (cond[ct] + k[ct, north, :]) * (u[ct, north, :] - here[ct])
                flux = flux + (cond[ct] + k[ct, south, :]) * (u[ct, south, :] - here[ct])
                if ct == nt:
                    flux = jnp.where(k0[ct, pl.ds(r0, ROWS), :] > 0, flux, 0.0)
                new = here[ct] + flux
                if final:
                    fin[pl.ds(r0, ROWS), ct * LANES : (ct + 1) * LANES] = new * (1.0 / SCALE)
                else:
                    nu[ct, at, :] = new
                    nk[ct, at, :] = k0[ct, pl.ds(r0, ROWS), :] * jnp.exp2(new)
            return carry

        return body

    for step in range(SUBSTEPS - 1):
        u, k, nu, nk = (ua, ka, ub, kb) if step % 2 == 0 else (ub, kb, ua, ka)
        lax.fori_loop(0, count // ROWS, substep(u, k, nu, nk, False), 0, unroll=blocks)
    last = (ua, ka, ub, kb) if SUBSTEPS % 2 == 1 else (ub, kb, ua, ka)
    outs = []
    for g in range(groups):
        lax.fori_loop(g * blocks, (g + 1) * blocks, substep(*last, True), 0, unroll=True)
        first = g * size + (ROWS if last_half and g == 0 else 0)
        end = (g + 1) * size - (ROWS if not last_half and g == groups - 1 else 0)
        outs.append(
            pltpu.make_async_copy(
                fin.at[pl.ds(first, end - first)], out.at[pl.ds(start + first, end - first)], sem.at[0, g]
            )
        )
        outs[-1].start()
    if last_half:
        low_ref[...] = fin[count - ROWS : count, :]
        put.wait()
    for copy in outs:
        copy.wait()


def finish_kernel(recv, slot, below, low, solid, wall_ref, out, tabl, edge, sem):
    devices, per_owner = recv.shape[0], recv.shape[1]
    rows = solid.shape[0]
    nt = below.shape[1]
    last = lax.axis_index("passage") == lax.axis_size("passage") - 1
    edge[...] = low[...]
    for j in range(EDGE):
        row = ROWS - EDGE + j
        for ct in range(nt):
            at = slice(ct * LANES, (ct + 1) * LANES)
            edge[row : row + 1, at] = jnp.where(last, low[row : row + 1, at], below[j, ct : ct + 1, :])
    store = pltpu.make_async_copy(edge, out.at[pl.ds(rows - ROWS, ROWS)], sem.at[0])
    store.start()
    for d in range(devices):
        tabl[d * per_owner : (d + 1) * per_owner, :] = recv[d]
    table = tabl.shape[0]
    parts = jnp.concatenate(split3(tabl[...]), axis=0).astype(BF16)
    highs, lanes_down = iota((table, LANES), 0), iota((LANES, LANES), 0)
    for b in range(slot.shape[0]):
        place = slot[b : b + 1, :]
        lows = jnp.where(lanes_down == (place & (LANES - 1)), 1.0, 0.0).astype(BF16)
        x = dot(parts, lows)
        x = x[0:table] + x[table : 2 * table] + x[2 * table : 3 * table]
        hi = lax.shift_right_logical(place, 7)
        wall_ref[b : b + 1, :] = jnp.sum(jnp.where(highs == hi, x, 0.0), axis=0, keepdims=True)
    store.wait()


def shards(gas, gas_speed, solid, material, face_cell, face_owner, face_surface, film, wall_previous):
    passages = lax.axis_size("passage")
    tiles = lax.axis_size("tile")
    devices = passages * tiles
    rows, cols = solid.shape
    nt = cols // LANES
    faces = face_cell.shape[0]
    blocks = faces // LANES
    cap = 2 * faces // devices
    per_owner = max(1, cap // LANES)
    table = devices * per_owner
    wide = cols + LANES

    def shape(dims, kind=F32):
        return jax.ShapeDtypeStruct(dims, kind)

    def cost(flops, moved, hard=0):
        return pl.CostEstimate(flops=flops, bytes_accessed=moved, transcendentals=hard)

    one, two, edges, edge_m = pl.pallas_call(
        pack_columns,
        in_specs=[whole(pltpu.HBM)] * 4,
        out_specs=[whole()] * 4,
        out_shape=[shape((16, rows))] * 2 + [shape((6, ROWS, cols)), shape((2, ROWS, cols), jnp.int32)],
        scratch_shapes=[
            VMEM((6, rows, LANES), F32),
            VMEM((2, rows, LANES), jnp.int32),
            pltpu.SemaphoreType.DMA((2, 8)),
        ],
        compiler_params=params(52),
        name="pack_columns",
        cost_estimate=cost(1000000, 8 * rows * LANES * 4),
    )(gas, gas_speed, solid, material)
    one, two = pair_swaps("tile", tiles)(one, two)

    w, ra, rb = pl.pallas_call(
        pack_rows,
        in_specs=[whole()] * 4,
        out_specs=[whole()] * 3,
        out_shape=[shape((rows, LANES)), shape((16, wide)), shape((16, wide))],
        scratch_shapes=[VMEM((LANES, rows), F32)],
        compiler_params=params(8),
        name="pack_rows",
        cost_estimate=cost(1000000, 8 * ROWS * cols * 4),
    )(one, two, edges, edge_m)
    ra, rb = pair_swaps("passage", passages)(ra, rb)

    def folded(x):
        return x.reshape(blocks, LANES)

    owner, surface, cell = folded(face_owner), folded(face_surface), folded(face_cell)
    slot, rowidx, idx = pl.pallas_call(
        functools.partial(find_slots, devices, per_owner, rows, cols),
        in_specs=[whole()] * 3,
        out_specs=[whole()] * 3,
        out_shape=[shape((blocks, LANES), jnp.int32), shape((blocks, LANES), jnp.int32), shape((table, LANES))],
        scratch_shapes=[
            VMEM((blocks * devices, LANES), BF16),
            VMEM((2 * table, faces), BF16),
            VMEM((LANES, faces), BF16),
        ],
        compiler_params=params(24),
        name="find_slots",
        cost_estimate=cost(20000000, 1000000),
    )(owner, surface, cell)

    part = table + devices
    gas_next, route = pl.pallas_call(
        functools.partial(gas_kernel, tiles, per_owner),
        in_specs=[whole(pltpu.HBM)] * 2 + [whole()] * 3 + [whole(pltpu.SMEM)] + [whole()] * 7,
        out_specs=[whole(pltpu.HBM), whole()],
        out_shape=[shape((rows, cols)), shape((devices, ROUTE_ROWS, LANES))],
        scratch_shapes=[
            VMEM((nt + 1, rows + 2 * ROWS, LANES), F32),
            VMEM((rows, cols), F32),
            VMEM((rows, LANES), F32),
            VMEM((nt + 1, rows + 2 * ROWS, LANES), F32),
            VMEM((nt * rows, LANES), F32),
            VMEM((rows, cols), F32),
            VMEM((faces, LANES), F32),
            VMEM((3 * part, faces), BF16),
            VMEM((LANES + 32, faces), BF16),
            VMEM((part, LANES + 32), F32),
            pltpu.SemaphoreType.DMA((2, nt)),
        ],
        compiler_params=params(24),
        name="gas_and_heat",
        cost_estimate=cost(60000000, 40000000),
    )(
        gas, gas_speed, w, ra, rb, rowidx.reshape(faces), cell, owner, surface, slot,
        folded(film), folded(wall_previous), idx,
    )
    recv = lax.all_to_all(route, ("passage", "tile"), 0, 0, tiled=True)

    blocks_here = rows // ROWS
    ahead = blocks_here // 2 // 4 * 4

    def bulk_half(last_half, start, count, groups, *more):
        return pl.pallas_call(
            functools.partial(bulk_kernel, last_half, start, count, groups),
            in_specs=[whole(pltpu.HBM)] * 2 + [whole()] + ([whole()] * 3 + [whole(pltpu.HBM)] if last_half else []),
            out_specs=[whole(pltpu.HBM), whole()],
            out_shape=[shape((rows, cols)), shape((ROWS, cols if last_half else LANES))],
            input_output_aliases={6: 0} if last_half else {},
            scratch_shapes=[VMEM((count, cols), F32), VMEM((count, cols), jnp.int32)]
            + [VMEM((nt + 1, count + 2 * ROWS, LANES), F32)] * 4
            + [VMEM((nt + 1, count, LANES), F32)] * 2
            + [VMEM((count, cols), F32), pltpu.SemaphoreType.DMA((3, groups))],
            compiler_params=params(52),
            name="solid_bulk",
            cost_estimate=cost(60000000, 30000000),
        )(solid, material, w, *more)

    bulk, token = bulk_half(False, 0, ahead * ROWS, 4)

    slots = table * LANES
    top, up, ret = pl.pallas_call(
        functools.partial(strip_kernel, per_owner),
        in_specs=[whole()] * 4 + [whole(pltpu.HBM)] * 2 + [whole()],
        out_specs=[whole()] * 3,
        out_shape=[shape((ROWS, cols)), shape((EDGE, nt, LANES)), shape((devices, per_owner, LANES))],
        scratch_shapes=[
            VMEM((6 * nt, slots), BF16),
            VMEM((LANES, slots), BF16),
            VMEM((2 * nt, LANES), F32),
            VMEM((ROWS, wide), F32),
            VMEM((2 * nt, LANES), F32),
            VMEM((2 * ROWS, cols), F32),
            VMEM((2 * ROWS, cols), jnp.int32),
            pltpu.SemaphoreType.DMA((2,)),
        ],
        compiler_params=params(52),
        name="solid_strip",
        cost_estimate=cost(20000000, 4000000),
    )(recv, ra, rb, w, solid, material, token)
    ret = lax.all_to_all(ret, ("passage", "tile"), 0, 0, tiled=True)
    below = lax.ppermute(up, "passage", [(i + 1, i) for i in range(passages - 1)])

    behind = (ahead - 2) * ROWS
    bulk, low = bulk_half(True, behind, rows - behind, 3, ra, rb, top, bulk)
    wall, solid_next = pl.pallas_call(
        finish_kernel,
        in_specs=[whole()] * 4 + [whole(pltpu.HBM)],
        out_specs=[whole(), whole(pltpu.HBM)],
        out_shape=[shape((blocks, LANES)), shape((rows, cols))],
        input_output_aliases={4: 1},
        scratch_shapes=[
            VMEM((table, LANES), F32),
            VMEM((ROWS, cols), F32),
            pltpu.SemaphoreType.DMA((1,)),
        ],
        compiler_params=params(24),
        name="wall_temperatures",
        cost_estimate=cost(20000000, 4000000),
    )(ret, slot, below, low, bulk)
    return gas_next, solid_next, wall.reshape(faces)


def solution(mesh):
    in_specs = (
        P("passage", "tile"),
        P("passage", "tile"),
        P("passage", "tile"),
        P("passage", "tile"),
        P(("passage", "tile")),
        P(("passage", "tile"), None),
        P(("passage", "tile")),
        P(("passage", "tile")),
        P(("passage", "tile")),
    )
    out_specs = (P("passage", "tile"), P("passage", "tile"), P(("passage", "tile")))
    return jax.shard_map(shards, mesh=mesh, in_specs=in_specs, out_specs=out_specs, check_vma=False)
```

```python
import functools

import jax
import jax.numpy as jnp
from jax import lax
from jax.experimental import pallas as pl
from jax.experimental.pallas import tpu as pltpu
from jax.sharding import PartitionSpec as P

SUBSTEPS = 4
DIFFUSE = 0.05
SOLID_STEP = 0.1
SOFTEN = 0.08
SCALE = SOFTEN * 1.4426950408889634
SHARE = 0.5 * SOLID_STEP
LANES = 128
ROWS = 8
TALL = 64
ROUTE_ROWS = 8
EDGE = SUBSTEPS - 1
F32 = jnp.float32
BF16 = jnp.bfloat16
VMEM = pltpu.VMEM
MIB = 2**20


def params(mib):
    return pltpu.CompilerParams(vmem_limit_bytes=int(mib * MIB))


def whole(space=pltpu.VMEM):
    return pl.BlockSpec(memory_space=space)


def iota(shape, dim):
    return lax.broadcasted_iota(jnp.int32, shape, dim)


def base_conductivity(material, share=1.0):
    return jnp.where(
        material == 0,
        jnp.float32(share),
        jnp.where(material == 1, jnp.float32(0.3 * share), jnp.float32(0.08 * share)),
    )


def even(axis):
    return lax.rem(lax.axis_index(axis), 2) == 0


def split3(x):
    one = x.astype(BF16).astype(F32)
    rest = x - one
    two = rest.astype(BF16).astype(F32)
    return one, two, (rest - two).astype(BF16).astype(F32)


def dot_lanes(a, b):
    return lax.dot_general(a, b, (((1,), (1,)), ((), ())), preferred_element_type=F32)


def dot(a, b):
    return lax.dot_general(a, b, (((1,), (0,)), ((), ())), preferred_element_type=F32)


def pair_swaps(axis, count):
    first = [(i, i + 1) for i in range(0, count - 1, 2)]
    second = [(i, i + 1) for i in range(1, count - 1, 2)]

    def both(pairs):
        return pairs + [(b, a) for a, b in pairs]

    def run(one, two):
        return lax.ppermute(one, axis, both(first)), lax.ppermute(two, axis, both(second))

    return run


def pack_columns(gas, speed, solid, material, one_ref, two_ref, top_f, top_m, tiles, tile_m, sem):
    size, cols = gas.shape
    fields = (gas, speed, solid)
    ends = (pl.ds(0, LANES), pl.ds(cols - LANES, LANES))
    bands = (pl.ds(0, ROWS), pl.ds(size - ROWS, ROWS))
    tall, flat = [], []
    for e in range(2):
        for f in range(3):
            tall.append(pltpu.make_async_copy(fields[f].at[:, ends[e]], tiles.at[2 * f + e], sem.at[0, 4 * e + f]))
        tall.append(pltpu.make_async_copy(material.at[:, ends[e]], tile_m.at[e], sem.at[0, 4 * e + 3]))
    for e in range(2):
        for f in range(3):
            flat.append(pltpu.make_async_copy(fields[f].at[bands[e], :], top_f.at[2 * f + e], sem.at[1, 4 * e + f]))
        flat.append(pltpu.make_async_copy(material.at[bands[e], :], top_m.at[e], sem.at[1, 4 * e + 3]))
    for copy in tall + flat:
        copy.start()
    for copy in tall:
        copy.wait()
    lane = iota((size, LANES), 1)
    head = jnp.where(
        lane < 4,
        tiles[4],
        jnp.where(
            lane < 8,
            pltpu.roll(base_conductivity(tile_m[0]), 4, 1),
            jnp.where(lane < 10, pltpu.roll(tiles[0], 8, 1), pltpu.roll(tiles[2], 10, 1)),
        ),
    )
    tail = jnp.where(
        lane >= 124,
        tiles[5],
        jnp.where(
            lane >= 120,
            pltpu.roll(base_conductivity(tile_m[1]), 124, 1),
            jnp.where(lane >= 118, pltpu.roll(tiles[1], 120, 1), pltpu.roll(tiles[3], 118, 1)),
        ),
    )
    head = head.T[0:16]
    tail = tail.T[112:128]
    is_even = even("tile")
    one_ref[...] = jnp.where(is_even, tail, head)
    two_ref[...] = jnp.where(is_even, head, tail)
    for copy in flat:
        copy.wait()


def halo_tiles(w):
    lane = iota(w.shape, 1)
    zero = jnp.zeros_like(w)
    solid = jnp.where((lane < 4) | (lane >= 124), w, zero)
    conduct = jnp.where(
        lane < 4, pltpu.roll(w, 124, 1), jnp.where(lane >= 124, pltpu.roll(w, 4, 1), zero)
    )
    return solid, conduct


def gas_halo_tiles(w):
    lane = iota(w.shape, 1)
    zero = jnp.zeros_like(w)
    gas = jnp.where(
        lane < 2, pltpu.roll(w, 120, 1), jnp.where(lane >= 126, pltpu.roll(w, 8, 1), zero)
    )
    speed = jnp.where(
        lane < 1, pltpu.roll(w, 118, 1), jnp.where(lane >= 127, pltpu.roll(w, 10, 1), zero)
    )
    return gas, speed


def pack_rows(one, two, edges, edge_m, token, w_ref, a_ref, b_ref, wt):
    is_even = even("tile")
    wt[...] = jnp.zeros_like(wt)
    wt[0:16, :] = jnp.where(is_even, one[...], two[...])
    wt[112:128, :] = jnp.where(is_even, two[...], one[...])
    w = wt[...].T
    w_ref[...] = w
    size = w.shape[0]
    wide = edges.shape[2] + LANES

    def rows(e, part, step):
        g, s, u, m = edges.at[e], edges.at[2 + e], edges.at[4 + e], edge_m.at[e]
        uh, kh = halo_tiles(part)
        gh, sh = gas_halo_tiles(part)
        g = jnp.concatenate([g[...], gh], axis=1)
        s = jnp.concatenate([s[...], sh], axis=1)
        u = jnp.concatenate([u[...], uh], axis=1)
        k = jnp.concatenate([base_conductivity(m[...]), kh], axis=1)
        before = pltpu.roll(g, 1, 1)
        after = pltpu.roll(g, wide - 1, 1)
        inner = pltpu.roll(g, step, 0)
        partial = g - s * (g - before) + DIFFUSE * (inner + before + after - 4.0 * g)
        return g, partial, u, k

    row = iota((ROWS, wide), 0)
    zero = jnp.zeros((ROWS, wide), F32)
    g, partial, u, k = rows(0, w[0:ROWS], ROWS - 1)

    def first_two(x, y):
        return jnp.where(row == 0, x, jnp.where(row == 1, pltpu.roll(y, 1, 0), zero))

    up = (first_two(g, u), first_two(partial, k))
    g, partial, u, k = rows(1, w[size - ROWS : size], 1)

    def last_rows(x, y):
        return jnp.where(row == 0, pltpu.roll(x, 1, 0), y)

    down = (last_rows(g, u), last_rows(partial, k))
    is_even = even("passage")
    for half in range(2):
        a_ref[half * ROWS : (half + 1) * ROWS, :] = jnp.where(is_even, down[half], up[half])
        b_ref[half * ROWS : (half + 1) * ROWS, :] = jnp.where(is_even, up[half], down[half])


def find_slots(devices, per_owner, rows, cols, owner, surface, cell, slot_ref, row_ref, idx_ref, held, lhs, rhs):
    blocks = owner.shape[0]
    owners = iota((devices, LANES), 0)
    for b in range(blocks):
        held[b * devices : (b + 1) * devices, :] = jnp.where(owner[b : b + 1, :] == owners, 1.0, 0.0).astype(BF16)
    r, c = iota((LANES, 2 * LANES), 0), iota((LANES, 2 * LANES), 1)
    before = jnp.where((r < c) | (c >= LANES), 1.0, 0.0).astype(BF16)
    counts = dot(held[...], before)
    high = slot_ref.shape[0]
    table = idx_ref.shape[0]
    start = jnp.zeros((devices, LANES), F32)
    highs, lows = iota((table, LANES), 0), iota((LANES, LANES), 0)
    for b in range(blocks):
        own = counts[b * devices : (b + 1) * devices]
        mine = owner[b : b + 1, :]
        rank = jnp.sum(
            jnp.where(mine == owners, own[:, :LANES] + start, 0.0), axis=0, keepdims=True
        ).astype(jnp.int32)
        start = start + own[:, LANES:]
        hi = mine * per_owner + lax.shift_right_logical(rank, 7)
        lo = rank & (LANES - 1)
        slot_ref[b : b + 1, :] = hi * LANES + lo
        value = surface[b : b + 1, :]
        coarse = (value & ~255).astype(F32)
        fine = (value & 255).astype(F32)
        at = slice(b * LANES, (b + 1) * LANES)
        lhs[0:table, at] = jnp.where(highs == hi, coarse, 0.0).astype(BF16)
        lhs[table : 2 * table, at] = jnp.where(highs == hi, fine, 0.0).astype(BF16)
        rhs[:, at] = jnp.where(lows == lo, 1.0, 0.0).astype(BF16)
    both = dot_lanes(lhs[...], rhs[...])
    idx_ref[...] = both[0:table] + both[table : 2 * table]
    place = cell[...]
    row_ref[...] = lax.div(lax.rem(place, cols), LANES) * rows + lax.div(place, cols)


def shifted(tiles, lane):
    count = len(tiles)
    left = [pltpu.roll(x, LANES - 1, 1) for x in tiles]
    right = [pltpu.roll(x, 1, 1) for x in tiles]
    after = [jnp.where(lane == LANES - 1, left[(i + 1) % count], left[i]) for i in range(count)]
    before = [jnp.where(lane == 0, right[i - 1], right[i]) for i in range(count)]
    return after, before


def fetch(gas, speed, g0, s0, token, sem):
    copies = [pltpu.make_async_copy(gas, g0, sem.at[0]), pltpu.make_async_copy(speed, s0, sem.at[1])]
    for copy in copies:
        copy.start()
    token[...] = jnp.zeros_like(token)
    for copy in copies:
        copy.wait()


def tendency(v, north, south, after, before, s):
    return DIFFUSE * (south + north + after + before - 4.0 * v) - s * (v - before)


def first_section(gas, speed, w, s1, gx, sh):
    rows, cols = gas.shape
    nt = cols // LANES
    gh, speed_halo = gas_halo_tiles(w[...])
    gx[nt, ROWS : ROWS + rows, :] = gh
    sh[...] = speed_halo
    zero = jnp.zeros((ROWS, LANES), F32)
    for ct in range(nt + 1):
        gx[ct, 0:ROWS, :] = zero
        gx[ct, ROWS + rows : 2 * ROWS + rows, :] = zero
        s1[ct, 0:ROWS, :] = zero
        s1[ct, ROWS + rows : 2 * ROWS + rows, :] = zero

    def spread(i, carry):
        r0 = i * rows
        for ct in range(nt):
            gx[ct, pl.ds(ROWS + r0, rows), :] = gas[pl.ds(r0, rows), ct * LANES : (ct + 1) * LANES]
        return carry

    spread(0, 0)
    lane = iota((rows, LANES), 1)

    def body(i, carry):
        r0 = i * rows
        v = [gx[ct, pl.ds(ROWS + r0, rows), :] for ct in range(nt + 1)]
        after, before = shifted(v, lane)
        for ct in range(nt + 1):
            north = gx[ct, pl.ds(ROWS - 1 + r0, rows), :]
            south = gx[ct, pl.ds(ROWS + 1 + r0, rows), :]
            s = sh[pl.ds(r0, rows), :] if ct == nt else speed[pl.ds(r0, rows), ct * LANES : (ct + 1) * LANES]
            new = v[ct] + tendency(v[ct], north, south, after[ct], before[ct], s)
            if ct == nt:
                new = jnp.where(s > 0, new, 0.0)
            s1[ct, pl.ds(ROWS + r0, rows), :] = new
        return carry

    body(0, 0)


def gas_kernel(
    tiles_across, per_owner, gas, speed, sone, w, ra, rb, where_at, cell, owner, surface, slot, film, wall, idx,
    out, route, s1, tab, final, stage, lhs, rhs, sums, rowidx, sem,
):
    rows, cols = gas.shape
    nt = cols // LANES
    devices = route.shape[0]
    blocks = owner.shape[0]
    table = idx.shape[0]
    rows_in = pltpu.make_async_copy(where_at, rowidx, sem.at[1])
    rows_in.start()
    is_even = even("passage")
    place = lax.axis_index("passage")
    in_top = jnp.where(place > 0, 1.0, 0.0)
    in_bottom = jnp.where(place < lax.axis_size("passage") - 1, 1.0, 0.0)

    def top(row, ct):
        at = slice(ct * LANES, (ct + 1) * LANES)
        return jnp.where(is_even, rb[row : row + 1, at], ra[row : row + 1, at])

    def bottom(row, ct):
        at = slice(ct * LANES, (ct + 1) * LANES)
        return jnp.where(is_even, ra[row : row + 1, at], rb[row : row + 1, at])

    speed_halo = gas_halo_tiles(w[...])[1]
    for ct in range(nt + 1):
        up, down = DIFFUSE * top(0, ct), DIFFUSE * bottom(0, ct)
        if ct == nt:
            up = jnp.where(speed_halo[0:1] > 0, up, 0.0)
            down = jnp.where(speed_halo[rows - 1 : rows] > 0, down, 0.0)
        s1[ct, ROWS : ROWS + 1, :] = s1[ct, ROWS : ROWS + 1, :] + up
        s1[ct, ROWS + rows - 1 : ROWS + rows, :] = s1[ct, ROWS + rows - 1 : ROWS + rows, :] + down
    for ct in range(nt):
        at = slice(ct * LANES, (ct + 1) * LANES)
        s1[ct, ROWS - 1 : ROWS, :] = in_top * (top(8, ct) + DIFFUSE * gas[0:1, at])
        s1[ct, ROWS + rows : ROWS + rows + 1, :] = in_bottom * (bottom(8, ct) + DIFFUSE * gas[rows - 1 : rows, at])
    lane = iota((rows, LANES), 1)

    def second(i, carry):
        r0 = i * rows
        v = [s1[ct, pl.ds(ROWS + r0, rows), :] for ct in range(nt + 1)]
        after, before = shifted(v, lane)
        for ct in range(nt):
            north = s1[ct, pl.ds(ROWS - 1 + r0, rows), :]
            south = s1[ct, pl.ds(ROWS + 1 + r0, rows), :]
            at = slice(ct * LANES, (ct + 1) * LANES)
            g = gas[pl.ds(r0, rows), at]
            s = speed[pl.ds(r0, rows), at]
            new = 0.5 * (g + v[ct] + tendency(v[ct], north, south, after[ct], before[ct], s))
            tab[pl.ds(ct * rows + r0, rows), :] = new
            final[pl.ds(r0, rows), at] = new
        return carry

    second(0, 0)
    put = pltpu.make_async_copy(final, out, sem.at[0])
    put.start()
    rows_in.wait()
    sub = iota((ROWS, LANES), 0)
    unroll = 8

    def gather(i, carry):
        base = pl.multiple_of(i * (ROWS * unroll), ROWS * unroll)
        for g in range(unroll):
            acc = jnp.broadcast_to(tab[pl.ds(rowidx[base + g * ROWS], 1), :], (ROWS, LANES))
            for j in range(1, ROWS):
                row = tab[pl.ds(rowidx[base + g * ROWS + j], 1), :]
                acc = jnp.where(sub == j, jnp.broadcast_to(row, (ROWS, LANES)), acc)
            stage[pl.ds(base + g * ROWS, ROWS), :] = acc
        return carry

    lax.fori_loop(0, stage.shape[0] // (ROWS * unroll), gather, 0)
    lanes_down = iota((LANES, LANES), 0)
    highs = iota((table, LANES), 0)
    owners = iota((devices, LANES), 0)
    part = table + devices
    for b in range(blocks):
        at = slice(b * LANES, (b + 1) * LANES)
        picked = jnp.where(lanes_down == (cell[b : b + 1, :] & (LANES - 1)), stage[at, :].T, 0.0)
        face = jnp.sum(picked, axis=0, keepdims=True)
        heat = split3(film[b : b + 1, :] * (face - wall[b : b + 1, :]))
        place_of = slot[b : b + 1, :]
        hi = lax.shift_right_logical(place_of, 7)
        lo = place_of & (LANES - 1)
        mine = owner[b : b + 1, :]
        voxel = surface[b : b + 1, :]
        line = lax.div(voxel, cols)
        col = lax.rem(voxel, cols)
        tile = lax.rem(mine, tiles_across)
        to_right = (col >= cols - EDGE) & (tile < tiles_across - 1)
        to_left = (col < EDGE) & (tile > 0)
        dest = jnp.where(to_right, mine + 1, jnp.where(to_left, mine - 1, -1))
        code = jnp.where(to_right, col - (cols - EDGE), 16 + col) + 8 * line
        for k in range(3):
            lhs[k * part : k * part + table, at] = jnp.where(highs == hi, heat[k], 0.0).astype(BF16)
            lhs[k * part + table : (k + 1) * part, at] = jnp.where(owners == dest, heat[k], 0.0).astype(BF16)
        rhs[0:LANES, at] = jnp.where(lanes_down == lo, 1.0, 0.0).astype(BF16)
        rhs[LANES : LANES + 32, at] = jnp.where(iota((32, LANES), 0) == code, 1.0, 0.0).astype(BF16)
    three = dot_lanes(lhs[...], rhs[...])
    sums[...] = three[0:part] + three[part : 2 * part] + three[2 * part : 3 * part]
    route[...] = jnp.zeros_like(route)
    for o in range(devices):
        own = slice(o * per_owner, (o + 1) * per_owner)
        route[o, 0:per_owner, :] = sums[own, 0:LANES]
        route[o, per_owner : 2 * per_owner, :] = idx[own, :]
        route[o, 2 * per_owner : 2 * per_owner + 1, 0:32] = sums[table + o : table + o + 1, LANES : LANES + 32]
    put.wait()


def strip_kernel(
    per_owner, recv, ra, rb, w, solid, material, token, top_ref, up_ref, ret_ref, lhs, rhs, dep, src, tabu, su, sm, sem
):
    devices = recv.shape[0]
    cols = solid.shape[1]
    nt = cols // LANES
    wide = cols + LANES
    high = 2 * nt
    copies = [
        pltpu.make_async_copy(solid.at[pl.ds(0, 2 * ROWS)], su, sem.at[0]),
        pltpu.make_async_copy(material.at[pl.ds(0, 2 * ROWS)], sm, sem.at[1]),
    ]
    for copy in copies:
        copy.start()
    highs = iota((high, LANES), 0)
    lanes_down = iota((LANES, LANES), 0)
    for d in range(devices):
        for q in range(per_owner):
            at = slice((d * per_owner + q) * LANES, (d * per_owner + q + 1) * LANES)
            heat = split3(recv[d, q : q + 1, :])
            where = recv[d, per_owner + q : per_owner + q + 1, :].astype(jnp.int32)
            hi = lax.shift_right_logical(where, 7)
            for k in range(3):
                lhs[k * high : (k + 1) * high, at] = jnp.where(highs == hi, heat[k], 0.0).astype(BF16)
            rhs[:, at] = jnp.where(lanes_down == (where & (LANES - 1)), 1.0, 0.0).astype(BF16)
    three = dot_lanes(lhs[...], rhs[...])
    dep[...] = three[0:high] + three[high : 2 * high] + three[2 * high : 3 * high]
    edges = recv[0, 2 * per_owner : 2 * per_owner + 1, :]
    for d in range(1, devices):
        edges = edges + recv[d, 2 * per_owner : 2 * per_owner + 1, :]
    src[...] = jnp.zeros_like(src)
    lane = iota((1, LANES), 1)
    for line in range(2):
        for ct in range(nt):
            src[line : line + 1, ct * LANES : (ct + 1) * LANES] = dep[line * nt + ct : line * nt + ct + 1, :]
        left = pltpu.roll(edges, LANES - EDGE - 8 * line, 1)
        right = pltpu.roll(edges, LANES - 16 - 8 * line, 1)
        src[line : line + 1, cols:wide] = jnp.where(
            lane >= LANES - EDGE, left, jnp.where(lane < EDGE, right, 0.0)
        )
    is_even = even("passage")
    row8 = iota((ROWS, wide), 0)

    def above(at):
        return jnp.where(row8 > 0, jnp.where(is_even, rb[at : at + ROWS, :], ra[at : at + ROWS, :]), 0.0)

    uh, kh = halo_tiles(w[0 : 2 * ROWS, :])
    for copy in copies:
        copy.wait()
    u = jnp.concatenate([above(0), jnp.concatenate([su[...], uh], axis=1)], axis=0)
    k0 = jnp.concatenate([above(8), jnp.concatenate([base_conductivity(sm[...]), kh], axis=1)], axis=0)
    inside = jnp.where(k0 > 0, 0.5 * SOLID_STEP, 0.0)
    source = jnp.concatenate(
        [jnp.zeros((ROWS, wide), F32), 2.0 * src[...], jnp.zeros((ROWS, wide), F32)], axis=0
    )
    high_rows = 3 * ROWS
    for _ in range(SUBSTEPS):
        k = k0 * jnp.exp(SOFTEN * u)
        across = (k + pltpu.roll(k, wide - 1, 1)) * (pltpu.roll(u, wide - 1, 1) - u)
        down = (k + pltpu.roll(k, high_rows - 1, 0)) * (pltpu.roll(u, high_rows - 1, 0) - u)
        flux = across - pltpu.roll(across, 1, 1) + down - pltpu.roll(down, 1, 0)
        u = u + inside * (flux + source)
    for j in range(EDGE):
        for ct in range(nt):
            row = ROWS - EDGE + j
            up_ref[j, ct : ct + 1, :] = u[row : row + 1, ct * LANES : (ct + 1) * LANES]
    top_ref[...] = u[ROWS : 2 * ROWS, 0:cols]
    for line in range(2):
        for ct in range(nt):
            tabu[line * nt + ct : line * nt + ct + 1, :] = top_ref[line : line + 1, ct * LANES : (ct + 1) * LANES]
    parts = jnp.concatenate(split3(tabu[...]), axis=0).astype(BF16)
    for d in range(devices):
        for q in range(per_owner):
            at = slice((d * per_owner + q) * LANES, (d * per_owner + q + 1) * LANES)
            x = dot(parts, rhs[:, at])
            x = x[0:high] + x[high : 2 * high] + x[2 * high : 3 * high]
            where = recv[d, per_owner + q : per_owner + q + 1, :].astype(jnp.int32)
            hi = lax.shift_right_logical(where, 7)
            ret_ref[d, q : q + 1, :] = jnp.sum(jnp.where(highs == hi, x, 0.0), axis=0, keepdims=True)


def bulk_kernel(solid, material, w, ra, rb, out, low_ref, u0, m0, ua, ub, ka, kb, k0, k1, fin, sem):
    count, cols = solid.shape
    nt = cols // LANES
    groups = sem.shape[1]
    size = count // groups
    blocks = size // TALL
    copies = []
    for g in range(groups):
        at = pl.ds(g * size, size)
        copies.append(pltpu.make_async_copy(solid.at[at], u0.at[at], sem.at[0, g]))
        copies.append(pltpu.make_async_copy(material.at[at], m0.at[at], sem.at[1, g]))
    for copy in copies:
        copy.start()
    uh, kh = halo_tiles(w[...])
    ua[nt, ROWS : ROWS + count, :] = SCALE * uh
    k0[nt] = SHARE * kh
    zero = jnp.zeros((ROWS, LANES), F32)
    for ct in range(nt + 1):
        at = slice(ct * LANES, (ct + 1) * LANES)
        is_even = even("passage")
        below = SCALE * jnp.where(is_even, ra[1:2, at], rb[1:2, at])
        below_k = SHARE * jnp.where(is_even, ra[9:10, at], rb[9:10, at]) * jnp.exp2(below)
        for u, k in ((ua, ka), (ub, kb)):
            u[ct, 0:ROWS, :] = zero
            k[ct, 0:ROWS, :] = zero
            u[ct, ROWS + count : ROWS + count + 1, :] = below
            k[ct, ROWS + count : ROWS + count + 1, :] = below_k
    lane = iota((TALL, LANES), 1)
    edge = lane == LANES - 1

    def begin(i, carry):
        r0 = i * TALL
        bases = []
        for ct in range(nt + 1):
            if ct < nt:
                at = slice(ct * LANES, (ct + 1) * LANES)
                here = SCALE * u0[pl.ds(r0, TALL), at]
                base = base_conductivity(m0[pl.ds(r0, TALL), at], SHARE)
                ua[ct, pl.ds(ROWS + r0, TALL), :] = here
                k0[ct, pl.ds(r0, TALL), :] = base
            else:
                here = ua[ct, pl.ds(ROWS + r0, TALL), :]
                base = k0[ct, pl.ds(r0, TALL), :]
            ka[ct, pl.ds(ROWS + r0, TALL), :] = base * jnp.exp2(here)
            bases.append(base)
        turned = [pltpu.roll(x, LANES - 1, 1) for x in bases]
        for ct in range(nt + 1):
            k1[ct, pl.ds(r0, TALL), :] = jnp.where(edge, turned[(ct + 1) % (nt + 1)], turned[ct])
        return carry

    for g in range(groups):
        copies[2 * g].wait()
        copies[2 * g + 1].wait()
        for i in range(g * blocks, (g + 1) * blocks):
            begin(i, 0)

    def substep(u, k, nu, nk, final):
        tall = TALL if final else count
        lane = iota((tall, LANES), 1)
        edge = lane == LANES - 1

        def body(i, carry):
            r0 = i * tall
            at = pl.ds(ROWS + r0, tall)
            north, south = pl.ds(ROWS - 1 + r0, tall), pl.ds(ROWS + 1 + r0, tall)
            here = [u[ct, at, :] for ct in range(nt + 1)]
            cond = [k[ct, at, :] for ct in range(nt + 1)]
            turned = [pltpu.roll(x, LANES - 1, 1) for x in here]
            across = []
            for ct in range(nt + 1):
                nearby = jnp.where(edge, turned[(ct + 1) % (nt + 1)], turned[ct])
                nearby_k = k1[ct, pl.ds(r0, tall), :] * jnp.exp2(nearby)
                across.append((cond[ct] + nearby_k) * (nearby - here[ct]))
            back = [pltpu.roll(x, 1, 1) for x in across]
            for ct in range(nt if final else nt + 1):
                flux = across[ct] - jnp.where(lane == 0, back[ct - 1], back[ct])
                flux = flux + (cond[ct] + k[ct, north, :]) * (u[ct, north, :] - here[ct])
                flux = flux + (cond[ct] + k[ct, south, :]) * (u[ct, south, :] - here[ct])
                if ct == nt:
                    flux = jnp.where(k0[ct, pl.ds(r0, tall), :] > 0, flux, 0.0)
                new = here[ct] + flux
                if final:
                    fin[pl.ds(r0, tall), ct * LANES : (ct + 1) * LANES] = new * (1.0 / SCALE)
                else:
                    nu[ct, at, :] = new
                    nk[ct, at, :] = k0[ct, pl.ds(r0, tall), :] * jnp.exp2(new)
            return carry

        return body

    for step in range(SUBSTEPS - 1):
        u, k, nu, nk = (ua, ka, ub, kb) if step % 2 == 0 else (ub, kb, ua, ka)
        substep(u, k, nu, nk, False)(0, 0)
    last = (ua, ka, ub, kb) if SUBSTEPS % 2 == 1 else (ub, kb, ua, ka)
    outs = []
    for g in range(groups):
        for i in range(g * blocks, (g + 1) * blocks):
            substep(*last, True)(i, 0)
        at = pl.ds(g * size, size)
        outs.append(pltpu.make_async_copy(fin.at[at], out.at[at], sem.at[0, g]))
        outs[-1].start()
    low_ref[...] = fin[count - ROWS : count, :]
    for copy in outs:
        copy.wait()


def finish_kernel(recv, slot, below, low, top, solid, wall_ref, out, tabl, edge, sem):
    devices, per_owner = recv.shape[0], recv.shape[1]
    rows = solid.shape[0]
    nt = below.shape[1]
    last = lax.axis_index("passage") == lax.axis_size("passage") - 1
    put = pltpu.make_async_copy(top, out.at[pl.ds(0, ROWS)], sem.at[1])
    put.start()
    edge[...] = low[...]
    for j in range(EDGE):
        row = ROWS - EDGE + j
        for ct in range(nt):
            at = slice(ct * LANES, (ct + 1) * LANES)
            edge[row : row + 1, at] = jnp.where(last, low[row : row + 1, at], below[j, ct : ct + 1, :])
    store = pltpu.make_async_copy(edge, out.at[pl.ds(rows - ROWS, ROWS)], sem.at[0])
    store.start()
    for d in range(devices):
        tabl[d * per_owner : (d + 1) * per_owner, :] = recv[d]
    table = tabl.shape[0]
    parts = jnp.concatenate(split3(tabl[...]), axis=0).astype(BF16)
    highs, lanes_down = iota((table, LANES), 0), iota((LANES, LANES), 0)
    for b in range(slot.shape[0]):
        place = slot[b : b + 1, :]
        lows = jnp.where(lanes_down == (place & (LANES - 1)), 1.0, 0.0).astype(BF16)
        x = dot(parts, lows)
        x = x[0:table] + x[table : 2 * table] + x[2 * table : 3 * table]
        hi = lax.shift_right_logical(place, 7)
        wall_ref[b : b + 1, :] = jnp.sum(jnp.where(highs == hi, x, 0.0), axis=0, keepdims=True)
    put.wait()
    store.wait()


def shards(gas, gas_speed, solid, material, face_cell, face_owner, face_surface, film, wall_previous):
    passages = lax.axis_size("passage")
    tiles = lax.axis_size("tile")
    devices = passages * tiles
    rows, cols = solid.shape
    nt = cols // LANES
    faces = face_cell.shape[0]
    blocks = faces // LANES
    cap = 2 * faces // devices
    per_owner = max(1, cap // LANES)
    table = devices * per_owner
    wide = cols + LANES

    def shape(dims, kind=F32):
        return jax.ShapeDtypeStruct(dims, kind)

    def cost(flops, moved, hard=0):
        return pl.CostEstimate(flops=flops, bytes_accessed=moved, transcendentals=hard)

    one, two, edges, edge_m = pl.pallas_call(
        pack_columns,
        in_specs=[whole(pltpu.HBM)] * 4,
        out_specs=[whole()] * 4,
        out_shape=[shape((16, rows))] * 2 + [shape((6, ROWS, cols)), shape((2, ROWS, cols), jnp.int32)],
        scratch_shapes=[
            VMEM((6, rows, LANES), F32),
            VMEM((2, rows, LANES), jnp.int32),
            pltpu.SemaphoreType.DMA((2, 8)),
        ],
        compiler_params=params(52),
        name="pack_columns",
        cost_estimate=cost(1000000, 8 * rows * LANES * 4),
    )(gas, gas_speed, solid, material)
    one, two = pair_swaps("tile", tiles)(one, two)

    g0, s0, token = pl.pallas_call(
        fetch,
        in_specs=[whole(pltpu.HBM)] * 2,
        out_specs=[whole()] * 3,
        out_shape=[shape((rows, cols))] * 2 + [shape((ROWS, LANES))],
        scratch_shapes=[pltpu.SemaphoreType.DMA((2,))],
        compiler_params=params(48),
        name="fetch",
        cost_estimate=cost(0, 16 * rows * cols),
    )(gas, gas_speed)
    w, ra, rb = pl.pallas_call(
        pack_rows,
        in_specs=[whole()] * 5,
        out_specs=[whole()] * 3,
        out_shape=[shape((rows, LANES)), shape((16, wide)), shape((16, wide))],
        scratch_shapes=[VMEM((LANES, rows), F32)],
        compiler_params=params(8),
        name="pack_rows",
        cost_estimate=cost(1000000, 8 * ROWS * cols * 4),
    )(one, two, edges, edge_m, token)
    ra, rb = pair_swaps("passage", passages)(ra, rb)

    def folded(x):
        return x.reshape(blocks, LANES)

    owner, surface, cell = folded(face_owner), folded(face_surface), folded(face_cell)
    slot, rowidx, idx = pl.pallas_call(
        functools.partial(find_slots, devices, per_owner, rows, cols),
        in_specs=[whole()] * 3,
        out_specs=[whole()] * 3,
        out_shape=[shape((blocks, LANES), jnp.int32), shape((blocks, LANES), jnp.int32), shape((table, LANES))],
        scratch_shapes=[
            VMEM((blocks * devices, LANES), BF16),
            VMEM((2 * table, faces), BF16),
            VMEM((LANES, faces), BF16),
        ],
        compiler_params=params(24),
        name="find_slots",
        cost_estimate=cost(20000000, 1000000),
    )(owner, surface, cell)

    part = table + devices
    ringed = (nt + 1, rows + 2 * ROWS, LANES)
    sone = pl.pallas_call(
        first_section,
        in_specs=[whole()] * 3,
        out_specs=whole(),
        out_shape=shape(ringed),
        scratch_shapes=[VMEM(ringed, F32), VMEM((rows, LANES), F32)],
        compiler_params=params(12),
        name="first_section",
        cost_estimate=cost(8000000, 6000000),
    )(g0, s0, w)
    gas_next, route, _ = pl.pallas_call(
        functools.partial(gas_kernel, tiles, per_owner),
        in_specs=[whole()] * 6 + [whole(pl.ANY)] + [whole()] * 7,
        out_specs=[whole(pltpu.HBM), whole(), whole()],
        out_shape=[shape((rows, cols)), shape((devices, ROUTE_ROWS, LANES)), shape(ringed)],
        input_output_aliases={2: 2},
        scratch_shapes=[
            VMEM((nt * rows, LANES), F32),
            VMEM((rows, cols), F32),
            VMEM((faces, LANES), F32),
            VMEM((3 * part, faces), BF16),
            VMEM((LANES + 32, faces), BF16),
            VMEM((part, LANES + 32), F32),
            pltpu.SMEM((faces,), jnp.int32),
            pltpu.SemaphoreType.DMA((2,)),
        ],
        compiler_params=params(20),
        name="gas_and_heat",
        cost_estimate=cost(60000000, 40000000),
    )(
        g0, s0, sone, w, ra, rb, rowidx.reshape(faces), cell, owner, surface, slot,
        folded(film), folded(wall_previous), idx,
    )
    recv = lax.all_to_all(route, ("passage", "tile"), 0, 0, tiled=True)

    bulk, low = pl.pallas_call(
        bulk_kernel,
        in_specs=[whole(pltpu.HBM)] * 2 + [whole()] * 3,
        out_specs=[whole(pltpu.HBM), whole()],
        out_shape=[shape((rows, cols)), shape((ROWS, cols))],
        scratch_shapes=[VMEM((rows, cols), F32), VMEM((rows, cols), jnp.int32)]
        + [VMEM(ringed, F32)] * 4
        + [VMEM((nt + 1, rows, LANES), F32)] * 2
        + [VMEM((rows, cols), F32), pltpu.SemaphoreType.DMA((2, 4))],
        compiler_params=params(52),
        name="solid_bulk",
        cost_estimate=cost(60000000, 30000000),
    )(solid, material, w, ra, rb)

    slots = table * LANES
    top, up, ret = pl.pallas_call(
        functools.partial(strip_kernel, per_owner),
        in_specs=[whole()] * 4 + [whole(pltpu.HBM)] * 2 + [whole()],
        out_specs=[whole()] * 3,
        out_shape=[shape((ROWS, cols)), shape((EDGE, nt, LANES)), shape((devices, per_owner, LANES))],
        scratch_shapes=[
            VMEM((6 * nt, slots), BF16),
            VMEM((LANES, slots), BF16),
            VMEM((2 * nt, LANES), F32),
            VMEM((ROWS, wide), F32),
            VMEM((2 * nt, LANES), F32),
            VMEM((2 * ROWS, cols), F32),
            VMEM((2 * ROWS, cols), jnp.int32),
            pltpu.SemaphoreType.DMA((2,)),
        ],
        compiler_params=params(52),
        name="solid_strip",
        cost_estimate=cost(20000000, 4000000),
    )(recv, ra, rb, w, solid, material, low)
    ret = lax.all_to_all(ret, ("passage", "tile"), 0, 0, tiled=True)
    below = lax.ppermute(up, "passage", [(i + 1, i) for i in range(passages - 1)])

    wall, solid_next = pl.pallas_call(
        finish_kernel,
        in_specs=[whole()] * 5 + [whole(pltpu.HBM)],
        out_specs=[whole(), whole(pltpu.HBM)],
        out_shape=[shape((blocks, LANES)), shape((rows, cols))],
        input_output_aliases={5: 1},
        scratch_shapes=[
            VMEM((table, LANES), F32),
            VMEM((ROWS, cols), F32),
            pltpu.SemaphoreType.DMA((2,)),
        ],
        compiler_params=params(24),
        name="wall_temperatures",
        cost_estimate=cost(20000000, 4000000),
    )(ret, slot, below, low, top, bulk)
    return gas_next, solid_next, wall.reshape(faces)


def solution(mesh):
    in_specs = (
        P("passage", "tile"),
        P("passage", "tile"),
        P("passage", "tile"),
        P("passage", "tile"),
        P(("passage", "tile")),
        P(("passage", "tile"), None),
        P(("passage", "tile")),
        P(("passage", "tile")),
        P(("passage", "tile")),
    )
    out_specs = (P("passage", "tile"), P("passage", "tile"), P(("passage", "tile")))
    return jax.shard_map(shards, mesh=mesh, in_specs=in_specs, out_specs=out_specs, check_vma=False)
```

```python
import functools

import jax
import jax.numpy as jnp
from jax import lax
from jax.experimental import pallas as pl
from jax.experimental.pallas import tpu as pltpu
from jax.sharding import PartitionSpec as P

SUBSTEPS = 4
DIFFUSE = 0.05
SOLID_STEP = 0.1
SOFTEN = 0.08
SCALE = SOFTEN * 1.4426950408889634
SHARE = 0.5 * SOLID_STEP
LANES = 128
ROWS = 8
ROUTE_ROWS = 8
EDGE = SUBSTEPS - 1
F32 = jnp.float32
BF16 = jnp.bfloat16
VMEM = pltpu.VMEM
MIB = 2**20


def params(mib):
    return pltpu.CompilerParams(vmem_limit_bytes=int(mib * MIB))


def whole(space=pltpu.VMEM):
    return pl.BlockSpec(memory_space=space)


def iota(shape, dim):
    return lax.broadcasted_iota(jnp.int32, shape, dim)


def base_conductivity(material, share=1.0):
    return jnp.where(
        material == 0,
        jnp.float32(share),
        jnp.where(material == 1, jnp.float32(0.3 * share), jnp.float32(0.08 * share)),
    )


def even(axis):
    return lax.rem(lax.axis_index(axis), 2) == 0


def split3(x):
    one = x.astype(BF16).astype(F32)
    rest = x - one
    two = rest.astype(BF16).astype(F32)
    return one, two, (rest - two).astype(BF16).astype(F32)


def dot_lanes(a, b):
    return lax.dot_general(a, b, (((1,), (1,)), ((), ())), preferred_element_type=F32)


def dot(a, b):
    return lax.dot_general(a, b, (((1,), (0,)), ((), ())), preferred_element_type=F32)


def pair_swaps(axis, count):
    first = [(i, i + 1) for i in range(0, count - 1, 2)]
    second = [(i, i + 1) for i in range(1, count - 1, 2)]

    def both(pairs):
        return pairs + [(b, a) for a, b in pairs]

    def run(one, two):
        return lax.ppermute(one, axis, both(first)), lax.ppermute(two, axis, both(second))

    return run


def pack_columns(gas, speed, solid, material, one_ref, two_ref, top_f, top_m, tiles, tile_m, sem):
    size, cols = gas.shape
    fields = (gas, speed, solid)
    ends = (pl.ds(0, LANES), pl.ds(cols - LANES, LANES))
    bands = (pl.ds(0, ROWS), pl.ds(size - ROWS, ROWS))
    tall, flat = [], []
    for e in range(2):
        for f in range(3):
            tall.append(pltpu.make_async_copy(fields[f].at[:, ends[e]], tiles.at[2 * f + e], sem.at[0, 4 * e + f]))
        tall.append(pltpu.make_async_copy(material.at[:, ends[e]], tile_m.at[e], sem.at[0, 4 * e + 3]))
    for e in range(2):
        for f in range(3):
            flat.append(pltpu.make_async_copy(fields[f].at[bands[e], :], top_f.at[2 * f + e], sem.at[1, 4 * e + f]))
        flat.append(pltpu.make_async_copy(material.at[bands[e], :], top_m.at[e], sem.at[1, 4 * e + 3]))
    for copy in tall + flat:
        copy.start()
    for copy in tall:
        copy.wait()
    lane = iota((size, LANES), 1)
    head = jnp.where(
        lane < 4,
        tiles[4],
        jnp.where(
            lane < 8,
            pltpu.roll(base_conductivity(tile_m[0]), 4, 1),
            jnp.where(lane < 10, pltpu.roll(tiles[0], 8, 1), pltpu.roll(tiles[2], 10, 1)),
        ),
    )
    tail = jnp.where(
        lane >= 124,
        tiles[5],
        jnp.where(
            lane >= 120,
            pltpu.roll(base_conductivity(tile_m[1]), 124, 1),
            jnp.where(lane >= 118, pltpu.roll(tiles[1], 120, 1), pltpu.roll(tiles[3], 118, 1)),
        ),
    )
    head = head.T[0:16]
    tail = tail.T[112:128]
    is_even = even("tile")
    one_ref[...] = jnp.where(is_even, tail, head)
    two_ref[...] = jnp.where(is_even, head, tail)
    for copy in flat:
        copy.wait()


def halo_tiles(w):
    lane = iota(w.shape, 1)
    zero = jnp.zeros_like(w)
    solid = jnp.where((lane < 4) | (lane >= 124), w, zero)
    conduct = jnp.where(
        lane < 4, pltpu.roll(w, 124, 1), jnp.where(lane >= 124, pltpu.roll(w, 4, 1), zero)
    )
    return solid, conduct


def gas_halo_tiles(w):
    lane = iota(w.shape, 1)
    zero = jnp.zeros_like(w)
    gas = jnp.where(
        lane < 2, pltpu.roll(w, 120, 1), jnp.where(lane >= 126, pltpu.roll(w, 8, 1), zero)
    )
    speed = jnp.where(
        lane < 1, pltpu.roll(w, 118, 1), jnp.where(lane >= 127, pltpu.roll(w, 10, 1), zero)
    )
    return gas, speed


def pack_rows(one, two, edges, edge_m, token, w_ref, a_ref, b_ref, wt):
    is_even = even("tile")
    wt[...] = jnp.zeros_like(wt)
    wt[0:16, :] = jnp.where(is_even, one[...], two[...])
    wt[112:128, :] = jnp.where(is_even, two[...], one[...])
    w = wt[...].T
    w_ref[...] = w
    size = w.shape[0]
    wide = edges.shape[2] + LANES

    def rows(e, part, step):
        g, s, u, m = edges.at[e], edges.at[2 + e], edges.at[4 + e], edge_m.at[e]
        uh, kh = halo_tiles(part)
        gh, sh = gas_halo_tiles(part)
        g = jnp.concatenate([g[...], gh], axis=1)
        s = jnp.concatenate([s[...], sh], axis=1)
        u = jnp.concatenate([u[...], uh], axis=1)
        k = jnp.concatenate([base_conductivity(m[...]), kh], axis=1)
        before = pltpu.roll(g, 1, 1)
        after = pltpu.roll(g, wide - 1, 1)
        inner = pltpu.roll(g, step, 0)
        partial = g - s * (g - before) + DIFFUSE * (inner + before + after - 4.0 * g)
        return g, partial, u, k

    row = iota((ROWS, wide), 0)
    zero = jnp.zeros((ROWS, wide), F32)
    g, partial, u, k = rows(0, w[0:ROWS], ROWS - 1)

    def first_two(x, y):
        return jnp.where(row == 0, x, jnp.where(row == 1, pltpu.roll(y, 1, 0), zero))

    up = (first_two(g, u), first_two(partial, k))
    g, partial, u, k = rows(1, w[size - ROWS : size], 1)

    def last_rows(x, y):
        return jnp.where(row == 0, pltpu.roll(x, 1, 0), y)

    down = (last_rows(g, u), last_rows(partial, k))
    is_even = even("passage")
    for half in range(2):
        a_ref[half * ROWS : (half + 1) * ROWS, :] = jnp.where(is_even, down[half], up[half])
        b_ref[half * ROWS : (half + 1) * ROWS, :] = jnp.where(is_even, up[half], down[half])


def find_slots(devices, per_owner, rows, cols, owner, surface, cell, slot_ref, row_ref, idx_ref, held, lhs, rhs):
    blocks = owner.shape[0]
    owners = iota((devices, LANES), 0)
    for b in range(blocks):
        held[b * devices : (b + 1) * devices, :] = jnp.where(owner[b : b + 1, :] == owners, 1.0, 0.0).astype(BF16)
    r, c = iota((LANES, 2 * LANES), 0), iota((LANES, 2 * LANES), 1)
    before = jnp.where((r < c) | (c >= LANES), 1.0, 0.0).astype(BF16)
    counts = dot(held[...], before)
    high = slot_ref.shape[0]
    table = idx_ref.shape[0]
    start = jnp.zeros((devices, LANES), F32)
    highs, lows = iota((table, LANES), 0), iota((LANES, LANES), 0)
    for b in range(blocks):
        own = counts[b * devices : (b + 1) * devices]
        mine = owner[b : b + 1, :]
        rank = jnp.sum(
            jnp.where(mine == owners, own[:, :LANES] + start, 0.0), axis=0, keepdims=True
        ).astype(jnp.int32)
        start = start + own[:, LANES:]
        hi = mine * per_owner + lax.shift_right_logical(rank, 7)
        lo = rank & (LANES - 1)
        slot_ref[b : b + 1, :] = hi * LANES + lo
        value = surface[b : b + 1, :]
        coarse = (value & ~255).astype(F32)
        fine = (value & 255).astype(F32)
        at = slice(b * LANES, (b + 1) * LANES)
        lhs[0:table, at] = jnp.where(highs == hi, coarse, 0.0).astype(BF16)
        lhs[table : 2 * table, at] = jnp.where(highs == hi, fine, 0.0).astype(BF16)
        rhs[:, at] = jnp.where(lows == lo, 1.0, 0.0).astype(BF16)
    both = dot_lanes(lhs[...], rhs[...])
    idx_ref[...] = both[0:table] + both[table : 2 * table]
    place = cell[...]
    row_ref[...] = lax.div(lax.rem(place, cols), LANES) * rows + lax.div(place, cols)


def shifted(tiles, lane):
    count = len(tiles)
    left = [pltpu.roll(x, LANES - 1, 1) for x in tiles]
    right = [pltpu.roll(x, 1, 1) for x in tiles]
    after = [jnp.where(lane == LANES - 1, left[(i + 1) % count], left[i]) for i in range(count)]
    before = [jnp.where(lane == 0, right[i - 1], right[i]) for i in range(count)]
    return after, before


def fetch(gas, speed, g0, s0, token, sem):
    copies = [pltpu.make_async_copy(gas, g0, sem.at[0]), pltpu.make_async_copy(speed, s0, sem.at[1])]
    for copy in copies:
        copy.start()
    token[...] = jnp.zeros_like(token)
    for copy in copies:
        copy.wait()


def tendency(v, north, south, after, before, s):
    return DIFFUSE * (south + north + after + before - 4.0 * v) - s * (v - before)


def first_section(gas, speed, w, s1, gx, sh):
    rows, cols = gas.shape
    nt = cols // LANES
    gh, speed_halo = gas_halo_tiles(w[...])
    gx[nt, ROWS : ROWS + rows, :] = gh
    sh[...] = speed_halo
    zero = jnp.zeros((ROWS, LANES), F32)
    for ct in range(nt + 1):
        gx[ct, 0:ROWS, :] = zero
        gx[ct, ROWS + rows : 2 * ROWS + rows, :] = zero
        s1[ct, 0:ROWS, :] = zero
        s1[ct, ROWS + rows : 2 * ROWS + rows, :] = zero

    def spread(i, carry):
        r0 = i * rows
        for ct in range(nt):
            gx[ct, pl.ds(ROWS + r0, rows), :] = gas[pl.ds(r0, rows), ct * LANES : (ct + 1) * LANES]
        return carry

    spread(0, 0)
    lane = iota((rows, LANES), 1)

    def body(i, carry):
        r0 = i * rows
        v = [gx[ct, pl.ds(ROWS + r0, rows), :] for ct in range(nt + 1)]
        after, before = shifted(v, lane)
        for ct in range(nt + 1):
            north = gx[ct, pl.ds(ROWS - 1 + r0, rows), :]
            south = gx[ct, pl.ds(ROWS + 1 + r0, rows), :]
            s = sh[pl.ds(r0, rows), :] if ct == nt else speed[pl.ds(r0, rows), ct * LANES : (ct + 1) * LANES]
            new = v[ct] + tendency(v[ct], north, south, after[ct], before[ct], s)
            if ct == nt:
                new = jnp.where(s > 0, new, 0.0)
            s1[ct, pl.ds(ROWS + r0, rows), :] = new
        return carry

    body(0, 0)


def gas_kernel(
    tiles_across, per_owner, gas, speed, sone, w, ra, rb, where_at, cell, owner, surface, slot, film, wall, idx,
    out, route, s1, tab, final, stage, lhs, rhs, sums, rowidx, sem,
):
    rows, cols = gas.shape
    nt = cols // LANES
    devices = route.shape[0]
    blocks = owner.shape[0]
    table = idx.shape[0]
    rows_in = pltpu.make_async_copy(where_at, rowidx, sem.at[1])
    rows_in.start()
    is_even = even("passage")
    place = lax.axis_index("passage")
    in_top = jnp.where(place > 0, 1.0, 0.0)
    in_bottom = jnp.where(place < lax.axis_size("passage") - 1, 1.0, 0.0)

    def top(row, ct):
        at = slice(ct * LANES, (ct + 1) * LANES)
        return jnp.where(is_even, rb[row : row + 1, at], ra[row : row + 1, at])

    def bottom(row, ct):
        at = slice(ct * LANES, (ct + 1) * LANES)
        return jnp.where(is_even, ra[row : row + 1, at], rb[row : row + 1, at])

    speed_halo = gas_halo_tiles(w[...])[1]
    for ct in range(nt + 1):
        up, down = DIFFUSE * top(0, ct), DIFFUSE * bottom(0, ct)
        if ct == nt:
            up = jnp.where(speed_halo[0:1] > 0, up, 0.0)
            down = jnp.where(speed_halo[rows - 1 : rows] > 0, down, 0.0)
        s1[ct, ROWS : ROWS + 1, :] = s1[ct, ROWS : ROWS + 1, :] + up
        s1[ct, ROWS + rows - 1 : ROWS + rows, :] = s1[ct, ROWS + rows - 1 : ROWS + rows, :] + down
    for ct in range(nt):
        at = slice(ct * LANES, (ct + 1) * LANES)
        s1[ct, ROWS - 1 : ROWS, :] = in_top * (top(8, ct) + DIFFUSE * gas[0:1, at])
        s1[ct, ROWS + rows : ROWS + rows + 1, :] = in_bottom * (bottom(8, ct) + DIFFUSE * gas[rows - 1 : rows, at])
    lane = iota((rows, LANES), 1)

    def second(i, carry):
        r0 = i * rows
        v = [s1[ct, pl.ds(ROWS + r0, rows), :] for ct in range(nt + 1)]
        after, before = shifted(v, lane)
        for ct in range(nt):
            north = s1[ct, pl.ds(ROWS - 1 + r0, rows), :]
            south = s1[ct, pl.ds(ROWS + 1 + r0, rows), :]
            at = slice(ct * LANES, (ct + 1) * LANES)
            g = gas[pl.ds(r0, rows), at]
            s = speed[pl.ds(r0, rows), at]
            new = 0.5 * (g + v[ct] + tendency(v[ct], north, south, after[ct], before[ct], s))
            tab[pl.ds(ct * rows + r0, rows), :] = new
            final[pl.ds(r0, rows), at] = new
        return carry

    second(0, 0)
    put = pltpu.make_async_copy(final, out, sem.at[0])
    put.start()
    rows_in.wait()
    sub = iota((ROWS, LANES), 0)
    lanes_down = iota((LANES, LANES), 0)
    highs = iota((table, LANES), 0)
    owners = iota((devices, LANES), 0)
    part = table + devices

    def gather(b):
        base = pl.multiple_of(b * LANES, LANES)
        for g in range(LANES // ROWS):
            acc = jnp.broadcast_to(tab[pl.ds(rowidx[base + g * ROWS], 1), :], (ROWS, LANES))
            for j in range(1, ROWS):
                row = tab[pl.ds(rowidx[base + g * ROWS + j], 1), :]
                acc = jnp.where(sub == j, jnp.broadcast_to(row, (ROWS, LANES)), acc)
            stage[pl.ds(base + g * ROWS, ROWS), :] = acc

    def place_heat(b):
        at = pl.ds(pl.multiple_of(b * LANES, LANES), LANES)
        one = pl.ds(b, 1)
        picked = jnp.where(lanes_down == (cell[one, :] & (LANES - 1)), stage[at, :].T, 0.0)
        face = jnp.sum(picked, axis=0, keepdims=True)
        heat = split3(film[one, :] * (face - wall[one, :]))
        place_of = slot[one, :]
        hi = lax.shift_right_logical(place_of, 7)
        lo = place_of & (LANES - 1)
        mine = owner[one, :]
        voxel = surface[one, :]
        line = lax.div(voxel, cols)
        col = lax.rem(voxel, cols)
        tile = lax.rem(mine, tiles_across)
        to_right = (col >= cols - EDGE) & (tile < tiles_across - 1)
        to_left = (col < EDGE) & (tile > 0)
        dest = jnp.where(to_right, mine + 1, jnp.where(to_left, mine - 1, -1))
        code = jnp.where(to_right, col - (cols - EDGE), 16 + col) + 8 * line
        for k in range(3):
            lhs[k * part : k * part + table, at] = jnp.where(highs == hi, heat[k], 0.0).astype(BF16)
            lhs[k * part + table : (k + 1) * part, at] = jnp.where(owners == dest, heat[k], 0.0).astype(BF16)
        rhs[0:LANES, at] = jnp.where(lanes_down == lo, 1.0, 0.0).astype(BF16)
        rhs[LANES : LANES + 32, at] = jnp.where(iota((32, LANES), 0) == code, 1.0, 0.0).astype(BF16)

    def both(b, carry):
        place_heat(b - 1)
        gather(b)
        return carry

    gather(0)
    lax.fori_loop(1, blocks, both, 0)
    place_heat(blocks - 1)
    three = dot_lanes(lhs[...], rhs[...])
    sums[...] = three[0:part] + three[part : 2 * part] + three[2 * part : 3 * part]
    route[...] = jnp.zeros_like(route)
    for o in range(devices):
        own = slice(o * per_owner, (o + 1) * per_owner)
        route[o, 0:per_owner, :] = sums[own, 0:LANES]
        route[o, per_owner : 2 * per_owner, :] = idx[own, :]
        route[o, 2 * per_owner : 2 * per_owner + 1, 0:32] = sums[table + o : table + o + 1, LANES : LANES + 32]
    put.wait()


def strip_kernel(
    per_owner, recv, ra, rb, w, solid, material, token, top_ref, up_ref, ret_ref, lhs, rhs, dep, src, tabu, su, sm, sem
):
    devices = recv.shape[0]
    cols = solid.shape[1]
    nt = cols // LANES
    wide = cols + LANES
    high = 2 * nt
    copies = [
        pltpu.make_async_copy(solid.at[pl.ds(0, 2 * ROWS)], su, sem.at[0]),
        pltpu.make_async_copy(material.at[pl.ds(0, 2 * ROWS)], sm, sem.at[1]),
    ]
    for copy in copies:
        copy.start()
    highs = iota((high, LANES), 0)
    lanes_down = iota((LANES, LANES), 0)
    for d in range(devices):
        for q in range(per_owner):
            at = slice((d * per_owner + q) * LANES, (d * per_owner + q + 1) * LANES)
            heat = split3(recv[d, q : q + 1, :])
            where = recv[d, per_owner + q : per_owner + q + 1, :].astype(jnp.int32)
            hi = lax.shift_right_logical(where, 7)
            for k in range(3):
                lhs[k * high : (k + 1) * high, at] = jnp.where(highs == hi, heat[k], 0.0).astype(BF16)
            rhs[:, at] = jnp.where(lanes_down == (where & (LANES - 1)), 1.0, 0.0).astype(BF16)
    three = dot_lanes(lhs[...], rhs[...])
    dep[...] = three[0:high] + three[high : 2 * high] + three[2 * high : 3 * high]
    edges = recv[0, 2 * per_owner : 2 * per_owner + 1, :]
    for d in range(1, devices):
        edges = edges + recv[d, 2 * per_owner : 2 * per_owner + 1, :]
    src[...] = jnp.zeros_like(src)
    lane = iota((1, LANES), 1)
    for line in range(2):
        for ct in range(nt):
            src[line : line + 1, ct * LANES : (ct + 1) * LANES] = dep[line * nt + ct : line * nt + ct + 1, :]
        left = pltpu.roll(edges, LANES - EDGE - 8 * line, 1)
        right = pltpu.roll(edges, LANES - 16 - 8 * line, 1)
        src[line : line + 1, cols:wide] = jnp.where(
            lane >= LANES - EDGE, left, jnp.where(lane < EDGE, right, 0.0)
        )
    is_even = even("passage")
    row8 = iota((ROWS, wide), 0)

    def above(at):
        return jnp.where(row8 > 0, jnp.where(is_even, rb[at : at + ROWS, :], ra[at : at + ROWS, :]), 0.0)

    uh, kh = halo_tiles(w[0 : 2 * ROWS, :])
    for copy in copies:
        copy.wait()
    u = jnp.concatenate([above(0), jnp.concatenate([su[...], uh], axis=1)], axis=0)
    k0 = jnp.concatenate([above(8), jnp.concatenate([base_conductivity(sm[...]), kh], axis=1)], axis=0)
    inside = jnp.where(k0 > 0, 0.5 * SOLID_STEP, 0.0)
    source = jnp.concatenate(
        [jnp.zeros((ROWS, wide), F32), 2.0 * src[...], jnp.zeros((ROWS, wide), F32)], axis=0
    )
    high_rows = 3 * ROWS
    for _ in range(SUBSTEPS):
        k = k0 * jnp.exp(SOFTEN * u)
        across = (k + pltpu.roll(k, wide - 1, 1)) * (pltpu.roll(u, wide - 1, 1) - u)
        down = (k + pltpu.roll(k, high_rows - 1, 0)) * (pltpu.roll(u, high_rows - 1, 0) - u)
        flux = across - pltpu.roll(across, 1, 1) + down - pltpu.roll(down, 1, 0)
        u = u + inside * (flux + source)
    for j in range(EDGE):
        for ct in range(nt):
            row = ROWS - EDGE + j
            up_ref[j, ct : ct + 1, :] = u[row : row + 1, ct * LANES : (ct + 1) * LANES]
    top_ref[...] = u[ROWS : 2 * ROWS, 0:cols]
    for line in range(2):
        for ct in range(nt):
            tabu[line * nt + ct : line * nt + ct + 1, :] = top_ref[line : line + 1, ct * LANES : (ct + 1) * LANES]
    parts = jnp.concatenate(split3(tabu[...]), axis=0).astype(BF16)
    for d in range(devices):
        for q in range(per_owner):
            at = slice((d * per_owner + q) * LANES, (d * per_owner + q + 1) * LANES)
            x = dot(parts, rhs[:, at])
            x = x[0:high] + x[high : 2 * high] + x[2 * high : 3 * high]
            where = recv[d, per_owner + q : per_owner + q + 1, :].astype(jnp.int32)
            hi = lax.shift_right_logical(where, 7)
            ret_ref[d, q : q + 1, :] = jnp.sum(jnp.where(highs == hi, x, 0.0), axis=0, keepdims=True)


def bulk_kernel(is_back, start, chunk, solid, material, w, *refs):
    if is_back:
        ra, rb, _, fin, u0, m0, ua, ub, ka, kb, k0, k1, sem = refs
    else:
        out, token, u0, m0, ua, ub, ka, kb, k0, k1, fin, sem = refs
    count, cols = u0.shape
    nt = cols // LANES
    skip = ROWS if is_back else 0
    copies = []
    for g in range(count // chunk):
        here, there = pl.ds(start + g * chunk, chunk), pl.ds(g * chunk, chunk)
        copies.append(pltpu.make_async_copy(solid.at[here], u0.at[there], sem.at[0, g]))
        copies.append(pltpu.make_async_copy(material.at[here], m0.at[there], sem.at[1, g]))
    for copy in copies:
        copy.start()
    uh, kh = halo_tiles(w[start : start + count, :])
    ua[nt, ROWS : ROWS + count, :] = SCALE * uh
    k0[nt] = SHARE * kh
    zero = jnp.zeros((ROWS, LANES), F32)
    for ct in range(nt + 1):
        at = slice(ct * LANES, (ct + 1) * LANES)
        if is_back:
            is_even = even("passage")
            below = SCALE * jnp.where(is_even, ra[1:2, at], rb[1:2, at])
            below_k = SHARE * jnp.where(is_even, ra[9:10, at], rb[9:10, at]) * jnp.exp2(below)
        for u, k in ((ua, ka), (ub, kb)):
            u[ct, 0:ROWS, :] = zero
            k[ct, 0:ROWS, :] = zero
            u[ct, ROWS + count : 2 * ROWS + count, :] = zero
            k[ct, ROWS + count : 2 * ROWS + count, :] = zero
            if is_back:
                u[ct, ROWS + count : ROWS + count + 1, :] = below
                k[ct, ROWS + count : ROWS + count + 1, :] = below_k
    if not is_back:
        token[...] = zero
    edge = iota((chunk, LANES), 1) == LANES - 1

    def begin(r0):
        bases = []
        for ct in range(nt + 1):
            if ct < nt:
                at = slice(ct * LANES, (ct + 1) * LANES)
                here = SCALE * u0[pl.ds(r0, chunk), at]
                base = base_conductivity(m0[pl.ds(r0, chunk), at], SHARE)
                ua[ct, pl.ds(ROWS + r0, chunk), :] = here
                k0[ct, pl.ds(r0, chunk), :] = base
            else:
                here = ua[ct, pl.ds(ROWS + r0, chunk), :]
                base = k0[ct, pl.ds(r0, chunk), :]
            ka[ct, pl.ds(ROWS + r0, chunk), :] = base * jnp.exp2(here)
            bases.append(base)
        turned = [pltpu.roll(x, LANES - 1, 1) for x in bases]
        for ct in range(nt + 1):
            k1[ct, pl.ds(r0, chunk), :] = jnp.where(edge, turned[(ct + 1) % (nt + 1)], turned[ct])

    for g in range(count // chunk):
        copies[2 * g].wait()
        copies[2 * g + 1].wait()
        begin(g * chunk)

    def substep(u, k, nu, nk, r0, tall, final):
        lane = iota((tall, LANES), 1)
        edge = lane == LANES - 1
        at = pl.ds(ROWS + r0, tall)
        north, south = pl.ds(ROWS - 1 + r0, tall), pl.ds(ROWS + 1 + r0, tall)
        here = [u[ct, at, :] for ct in range(nt + 1)]
        cond = [k[ct, at, :] for ct in range(nt + 1)]
        turned = [pltpu.roll(x, LANES - 1, 1) for x in here]
        across = []
        for ct in range(nt + 1):
            nearby = jnp.where(edge, turned[(ct + 1) % (nt + 1)], turned[ct])
            nearby_k = k1[ct, pl.ds(r0, tall), :] * jnp.exp2(nearby)
            across.append((cond[ct] + nearby_k) * (nearby - here[ct]))
        back = [pltpu.roll(x, 1, 1) for x in across]
        for ct in range(nt if final else nt + 1):
            flux = across[ct] - jnp.where(lane == 0, back[ct - 1], back[ct])
            flux = flux + (cond[ct] + k[ct, north, :]) * (u[ct, north, :] - here[ct])
            flux = flux + (cond[ct] + k[ct, south, :]) * (u[ct, south, :] - here[ct])
            if ct == nt:
                flux = jnp.where(k0[ct, pl.ds(r0, tall), :] > 0, flux, 0.0)
            new = here[ct] + flux
            if final:
                fin[pl.ds(r0 - skip, tall), ct * LANES : (ct + 1) * LANES] = new * (1.0 / SCALE)
            else:
                nu[ct, at, :] = new
                nk[ct, at, :] = k0[ct, pl.ds(r0, tall), :] * jnp.exp2(new)

    for step in range(SUBSTEPS - 1):
        u, k, nu, nk = (ua, ka, ub, kb) if step % 2 == 0 else (ub, kb, ua, ka)
        substep(u, k, nu, nk, 0, count, False)
    last = (ua, ka, ub, kb) if SUBSTEPS % 2 == 1 else (ub, kb, ua, ka)
    if is_back:
        substep(*last, skip, count - skip, True)
        return
    outs = []
    for g in range(count // chunk):
        tall = chunk - (ROWS if (g + 1) * chunk == count else 0)
        substep(*last, g * chunk, tall, True)
        at = pl.ds(g * chunk, tall)
        outs.append(pltpu.make_async_copy(fin.at[at], out.at[at], sem.at[0, g]))
        outs[-1].start()
    for copy in outs:
        copy.wait()


def finish_kernel(recv, slot, below, back, top, solid, wall_ref, out, tabl, edge, sem):
    devices, per_owner = recv.shape[0], recv.shape[1]
    rows = solid.shape[0]
    nt = below.shape[1]
    most = back.shape[0] - ROWS
    stores = [
        pltpu.make_async_copy(top, out.at[pl.ds(0, ROWS)], sem.at[0]),
        pltpu.make_async_copy(back.at[pl.ds(0, most)], out.at[pl.ds(rows - ROWS - most, most)], sem.at[1]),
        pltpu.make_async_copy(edge, out.at[pl.ds(rows - ROWS, ROWS)], sem.at[2]),
    ]
    for store in stores[:2]:
        store.start()
    last = lax.axis_index("passage") == lax.axis_size("passage") - 1
    edge[...] = back[most : most + ROWS, :]
    for j in range(EDGE):
        row = ROWS - EDGE + j
        for ct in range(nt):
            at = slice(ct * LANES, (ct + 1) * LANES)
            edge[row : row + 1, at] = jnp.where(last, edge[row : row + 1, at], below[j, ct : ct + 1, :])
    stores[2].start()
    for d in range(devices):
        tabl[d * per_owner : (d + 1) * per_owner, :] = recv[d]
    table = tabl.shape[0]
    parts = jnp.concatenate(split3(tabl[...]), axis=0).astype(BF16)
    highs, lanes_down = iota((table, LANES), 0), iota((LANES, LANES), 0)
    for b in range(slot.shape[0]):
        place = slot[b : b + 1, :]
        lows = jnp.where(lanes_down == (place & (LANES - 1)), 1.0, 0.0).astype(BF16)
        x = dot(parts, lows)
        x = x[0:table] + x[table : 2 * table] + x[2 * table : 3 * table]
        hi = lax.shift_right_logical(place, 7)
        wall_ref[b : b + 1, :] = jnp.sum(jnp.where(highs == hi, x, 0.0), axis=0, keepdims=True)
    for store in stores:
        store.wait()


def shards(gas, gas_speed, solid, material, face_cell, face_owner, face_surface, film, wall_previous):
    passages = lax.axis_size("passage")
    tiles = lax.axis_size("tile")
    devices = passages * tiles
    rows, cols = solid.shape
    nt = cols // LANES
    faces = face_cell.shape[0]
    blocks = faces // LANES
    cap = 2 * faces // devices
    per_owner = max(1, cap // LANES)
    table = devices * per_owner
    wide = cols + LANES

    def shape(dims, kind=F32):
        return jax.ShapeDtypeStruct(dims, kind)

    def cost(flops, moved, hard=0):
        return pl.CostEstimate(flops=flops, bytes_accessed=moved, transcendentals=hard)

    one, two, edges, edge_m = pl.pallas_call(
        pack_columns,
        in_specs=[whole(pltpu.HBM)] * 4,
        out_specs=[whole()] * 4,
        out_shape=[shape((16, rows))] * 2 + [shape((6, ROWS, cols)), shape((2, ROWS, cols), jnp.int32)],
        scratch_shapes=[
            VMEM((6, rows, LANES), F32),
            VMEM((2, rows, LANES), jnp.int32),
            pltpu.SemaphoreType.DMA((2, 8)),
        ],
        compiler_params=params(52),
        name="pack_columns",
        cost_estimate=cost(1000000, 8 * rows * LANES * 4),
    )(gas, gas_speed, solid, material)
    one, two = pair_swaps("tile", tiles)(one, two)

    g0, s0, token = pl.pallas_call(
        fetch,
        in_specs=[whole(pltpu.HBM)] * 2,
        out_specs=[whole()] * 3,
        out_shape=[shape((rows, cols))] * 2 + [shape((ROWS, LANES))],
        scratch_shapes=[pltpu.SemaphoreType.DMA((2,))],
        compiler_params=params(48),
        name="fetch",
        cost_estimate=cost(0, 16 * rows * cols),
    )(gas, gas_speed)
    w, ra, rb = pl.pallas_call(
        pack_rows,
        in_specs=[whole()] * 5,
        out_specs=[whole()] * 3,
        out_shape=[shape((rows, LANES)), shape((16, wide)), shape((16, wide))],
        scratch_shapes=[VMEM((LANES, rows), F32)],
        compiler_params=params(8),
        name="pack_rows",
        cost_estimate=cost(1000000, 8 * ROWS * cols * 4),
    )(one, two, edges, edge_m, token)
    ra, rb = pair_swaps("passage", passages)(ra, rb)

    def folded(x):
        return x.reshape(blocks, LANES)

    owner, surface, cell = folded(face_owner), folded(face_surface), folded(face_cell)
    slot, rowidx, idx = pl.pallas_call(
        functools.partial(find_slots, devices, per_owner, rows, cols),
        in_specs=[whole()] * 3,
        out_specs=[whole()] * 3,
        out_shape=[shape((blocks, LANES), jnp.int32), shape((blocks, LANES), jnp.int32), shape((table, LANES))],
        scratch_shapes=[
            VMEM((blocks * devices, LANES), BF16),
            VMEM((2 * table, faces), BF16),
            VMEM((LANES, faces), BF16),
        ],
        compiler_params=params(24),
        name="find_slots",
        cost_estimate=cost(20000000, 1000000),
    )(owner, surface, cell)

    part = table + devices
    ringed = (nt + 1, rows + 2 * ROWS, LANES)
    sone = pl.pallas_call(
        first_section,
        in_specs=[whole()] * 3,
        out_specs=whole(),
        out_shape=shape(ringed),
        scratch_shapes=[VMEM(ringed, F32), VMEM((rows, LANES), F32)],
        compiler_params=params(12),
        name="first_section",
        cost_estimate=cost(8000000, 6000000),
    )(g0, s0, w)
    gas_next, route, _ = pl.pallas_call(
        functools.partial(gas_kernel, tiles, per_owner),
        in_specs=[whole()] * 6 + [whole(pl.ANY)] + [whole()] * 7,
        out_specs=[whole(pltpu.HBM), whole(), whole()],
        out_shape=[shape((rows, cols)), shape((devices, ROUTE_ROWS, LANES)), shape(ringed)],
        input_output_aliases={2: 2},
        scratch_shapes=[
            VMEM((nt * rows, LANES), F32),
            VMEM((rows, cols), F32),
            VMEM((faces, LANES), F32),
            VMEM((3 * part, faces), BF16),
            VMEM((LANES + 32, faces), BF16),
            VMEM((part, LANES + 32), F32),
            pltpu.SMEM((faces,), jnp.int32),
            pltpu.SemaphoreType.DMA((2,)),
        ],
        compiler_params=params(20),
        name="gas_and_heat",
        cost_estimate=cost(60000000, 40000000),
    )(
        g0, s0, sone, w, ra, rb, rowidx.reshape(faces), cell, owner, surface, slot,
        folded(film), folded(wall_previous), idx,
    )
    recv = lax.all_to_all(route, ("passage", "tile"), 0, 0, tiled=True)

    behind = rows * 3 // 8 // ROWS * ROWS
    front = rows - behind + ROWS
    chunk = front // 3 if front % (3 * ROWS) == 0 else ROWS

    def bulk_part(is_back, start, count, chunk, outs, specs, *more):
        kept = [] if is_back else [VMEM((count, cols), F32)]
        return pl.pallas_call(
            functools.partial(bulk_kernel, is_back, start, chunk),
            in_specs=[whole(pltpu.HBM)] * 2 + [whole()] * (1 + len(more)),
            out_specs=specs,
            out_shape=outs,
            scratch_shapes=[VMEM((count, cols), F32), VMEM((count, cols), jnp.int32)]
            + [VMEM((nt + 1, count + 2 * ROWS, LANES), F32)] * 4
            + [VMEM((nt + 1, count, LANES), F32)] * 2
            + kept
            + [pltpu.SemaphoreType.DMA((2, count // chunk))],
            compiler_params=params(52),
            name="solid_bulk",
            cost_estimate=cost(60000000, 30000000),
        )(solid, material, w, *more)

    bulk, token = bulk_part(
        False, 0, front, chunk, [shape((rows, cols)), shape((ROWS, LANES))], [whole(pltpu.HBM), whole()]
    )

    slots = table * LANES
    top, up, ret = pl.pallas_call(
        functools.partial(strip_kernel, per_owner),
        in_specs=[whole()] * 4 + [whole(pltpu.HBM)] * 2 + [whole()],
        out_specs=[whole()] * 3,
        out_shape=[shape((ROWS, cols)), shape((EDGE, nt, LANES)), shape((devices, per_owner, LANES))],
        scratch_shapes=[
            VMEM((6 * nt, slots), BF16),
            VMEM((LANES, slots), BF16),
            VMEM((2 * nt, LANES), F32),
            VMEM((ROWS, wide), F32),
            VMEM((2 * nt, LANES), F32),
            VMEM((2 * ROWS, cols), F32),
            VMEM((2 * ROWS, cols), jnp.int32),
            pltpu.SemaphoreType.DMA((2,)),
        ],
        compiler_params=params(52),
        name="solid_strip",
        cost_estimate=cost(20000000, 4000000),
    )(recv, ra, rb, w, solid, material, token)
    ret = lax.all_to_all(ret, ("passage", "tile"), 0, 0, tiled=True)
    below = lax.ppermute(up, "passage", [(i + 1, i) for i in range(passages - 1)])

    (back,) = bulk_part(
        True, rows - behind - ROWS, behind + ROWS, behind + ROWS, [shape((behind, cols))], [whole()], ra, rb, top
    )
    wall, solid_next = pl.pallas_call(
        finish_kernel,
        in_specs=[whole()] * 5 + [whole(pltpu.HBM)],
        out_specs=[whole(), whole(pltpu.HBM)],
        out_shape=[shape((blocks, LANES)), shape((rows, cols))],
        input_output_aliases={5: 1},
        scratch_shapes=[
            VMEM((table, LANES), F32),
            VMEM((ROWS, cols), F32),
            pltpu.SemaphoreType.DMA((3,)),
        ],
        compiler_params=params(24),
        name="wall_temperatures",
        cost_estimate=cost(20000000, 4000000),
    )(ret, slot, below, back, top, bulk)
    return gas_next, solid_next, wall.reshape(faces)


def solution(mesh):
    in_specs = (
        P("passage", "tile"),
        P("passage", "tile"),
        P("passage", "tile"),
        P("passage", "tile"),
        P(("passage", "tile")),
        P(("passage", "tile"), None),
        P(("passage", "tile")),
        P(("passage", "tile")),
        P(("passage", "tile")),
    )
    out_specs = (P("passage", "tile"), P("passage", "tile"), P(("passage", "tile")))
    return jax.shard_map(shards, mesh=mesh, in_specs=in_specs, out_specs=out_specs, check_vma=False)
```

```python
import functools

import jax
import jax.numpy as jnp
from jax import lax
from jax.experimental import pallas as pl
from jax.experimental.pallas import tpu as pltpu
from jax.sharding import PartitionSpec as P

SUBSTEPS = 4
DIFFUSE = 0.05
SOLID_STEP = 0.1
SOFTEN = 0.08
SCALE = SOFTEN * 1.4426950408889634
SHARE = 0.5 * SOLID_STEP
LANES = 128
ROWS = 8
ROUTE_ROWS = 8
EDGE = SUBSTEPS - 1
F32 = jnp.float32
BF16 = jnp.bfloat16
VMEM = pltpu.VMEM
MIB = 2**20


def params(mib):
    return pltpu.CompilerParams(vmem_limit_bytes=int(mib * MIB))


def whole(space=pltpu.VMEM):
    return pl.BlockSpec(memory_space=space)


def iota(shape, dim):
    return lax.broadcasted_iota(jnp.int32, shape, dim)


def base_conductivity(material, share=1.0):
    return jnp.where(
        material == 0,
        jnp.float32(share),
        jnp.where(material == 1, jnp.float32(0.3 * share), jnp.float32(0.08 * share)),
    )


def even(axis):
    return lax.rem(lax.axis_index(axis), 2) == 0


def split3(x):
    one = x.astype(BF16).astype(F32)
    rest = x - one
    two = rest.astype(BF16).astype(F32)
    return one, two, (rest - two).astype(BF16).astype(F32)


def dot_lanes(a, b):
    return lax.dot_general(a, b, (((1,), (1,)), ((), ())), preferred_element_type=F32)


def dot(a, b):
    return lax.dot_general(a, b, (((1,), (0,)), ((), ())), preferred_element_type=F32)


def pair_swaps(axis, count):
    first = [(i, i + 1) for i in range(0, count - 1, 2)]
    second = [(i, i + 1) for i in range(1, count - 1, 2)]

    def both(pairs):
        return pairs + [(b, a) for a, b in pairs]

    def run(one, two):
        return lax.ppermute(one, axis, both(first)), lax.ppermute(two, axis, both(second))

    return run


def pack_columns(gas, speed, solid, material, one_ref, two_ref, top_f, top_m, tiles, tile_m, sem):
    size, cols = gas.shape
    fields = (gas, speed, solid)
    ends = (pl.ds(0, LANES), pl.ds(cols - LANES, LANES))
    bands = (pl.ds(0, ROWS), pl.ds(size - ROWS, ROWS))
    tall, flat = [], []
    for e in range(2):
        for f in range(3):
            tall.append(pltpu.make_async_copy(fields[f].at[:, ends[e]], tiles.at[2 * f + e], sem.at[0, 4 * e + f]))
        tall.append(pltpu.make_async_copy(material.at[:, ends[e]], tile_m.at[e], sem.at[0, 4 * e + 3]))
    for e in range(2):
        for f in range(3):
            flat.append(pltpu.make_async_copy(fields[f].at[bands[e], :], top_f.at[2 * f + e], sem.at[1, 4 * e + f]))
        flat.append(pltpu.make_async_copy(material.at[bands[e], :], top_m.at[e], sem.at[1, 4 * e + 3]))
    for copy in tall + flat:
        copy.start()
    for copy in tall:
        copy.wait()
    lane = iota((size, LANES), 1)
    head = jnp.where(
        lane < 4,
        tiles[4],
        jnp.where(
            lane < 8,
            pltpu.roll(base_conductivity(tile_m[0]), 4, 1),
            jnp.where(lane < 10, pltpu.roll(tiles[0], 8, 1), pltpu.roll(tiles[2], 10, 1)),
        ),
    )
    tail = jnp.where(
        lane >= 124,
        tiles[5],
        jnp.where(
            lane >= 120,
            pltpu.roll(base_conductivity(tile_m[1]), 124, 1),
            jnp.where(lane >= 118, pltpu.roll(tiles[1], 120, 1), pltpu.roll(tiles[3], 118, 1)),
        ),
    )
    head = head.T[0:16]
    tail = tail.T[112:128]
    is_even = even("tile")
    one_ref[...] = jnp.where(is_even, tail, head)
    two_ref[...] = jnp.where(is_even, head, tail)
    for copy in flat:
        copy.wait()


def halo_tiles(w):
    lane = iota(w.shape, 1)
    zero = jnp.zeros_like(w)
    solid = jnp.where((lane < 4) | (lane >= 124), w, zero)
    conduct = jnp.where(
        lane < 4, pltpu.roll(w, 124, 1), jnp.where(lane >= 124, pltpu.roll(w, 4, 1), zero)
    )
    return solid, conduct


def gas_halo_tiles(w):
    lane = iota(w.shape, 1)
    zero = jnp.zeros_like(w)
    gas = jnp.where(
        lane < 2, pltpu.roll(w, 120, 1), jnp.where(lane >= 126, pltpu.roll(w, 8, 1), zero)
    )
    speed = jnp.where(
        lane < 1, pltpu.roll(w, 118, 1), jnp.where(lane >= 127, pltpu.roll(w, 10, 1), zero)
    )
    return gas, speed


def pack_rows(one, two, edges, edge_m, token, w_ref, a_ref, b_ref, wt):
    is_even = even("tile")
    wt[...] = jnp.zeros_like(wt)
    wt[0:16, :] = jnp.where(is_even, one[...], two[...])
    wt[112:128, :] = jnp.where(is_even, two[...], one[...])
    w = wt[...].T
    w_ref[...] = w
    size = w.shape[0]
    wide = edges.shape[2] + LANES

    def rows(e, part, step):
        g, s, u, m = edges.at[e], edges.at[2 + e], edges.at[4 + e], edge_m.at[e]
        uh, kh = halo_tiles(part)
        gh, sh = gas_halo_tiles(part)
        g = jnp.concatenate([g[...], gh], axis=1)
        s = jnp.concatenate([s[...], sh], axis=1)
        u = jnp.concatenate([u[...], uh], axis=1)
        k = jnp.concatenate([base_conductivity(m[...]), kh], axis=1)
        before = pltpu.roll(g, 1, 1)
        after = pltpu.roll(g, wide - 1, 1)
        inner = pltpu.roll(g, step, 0)
        partial = g - s * (g - before) + DIFFUSE * (inner + before + after - 4.0 * g)
        return g, partial, u, k

    row = iota((ROWS, wide), 0)
    zero = jnp.zeros((ROWS, wide), F32)
    g, partial, u, k = rows(0, w[0:ROWS], ROWS - 1)

    def first_two(x, y):
        return jnp.where(row == 0, x, jnp.where(row == 1, pltpu.roll(y, 1, 0), zero))

    up = (first_two(g, u), first_two(partial, k))
    g, partial, u, k = rows(1, w[size - ROWS : size], 1)

    def last_rows(x, y):
        return jnp.where(row == 0, pltpu.roll(x, 1, 0), y)

    down = (last_rows(g, u), last_rows(partial, k))
    is_even = even("passage")
    for half in range(2):
        a_ref[half * ROWS : (half + 1) * ROWS, :] = jnp.where(is_even, down[half], up[half])
        b_ref[half * ROWS : (half + 1) * ROWS, :] = jnp.where(is_even, up[half], down[half])


def find_slots(devices, per_owner, rows, cols, owner, surface, cell, slot_ref, row_ref, idx_ref, rhs, held, lhs):
    blocks = owner.shape[0]
    owners = iota((devices, LANES), 0)
    for b in range(blocks):
        held[b * devices : (b + 1) * devices, :] = jnp.where(owner[b : b + 1, :] == owners, 1.0, 0.0).astype(BF16)
    r, c = iota((LANES, 2 * LANES), 0), iota((LANES, 2 * LANES), 1)
    before = jnp.where((r < c) | (c >= LANES), 1.0, 0.0).astype(BF16)
    counts = dot(held[...], before)
    high = slot_ref.shape[0]
    table = idx_ref.shape[0]
    start = jnp.zeros((devices, LANES), F32)
    highs, lows = iota((table, LANES), 0), iota((LANES, LANES), 0)
    for b in range(blocks):
        own = counts[b * devices : (b + 1) * devices]
        mine = owner[b : b + 1, :]
        rank = jnp.sum(
            jnp.where(mine == owners, own[:, :LANES] + start, 0.0), axis=0, keepdims=True
        ).astype(jnp.int32)
        start = start + own[:, LANES:]
        hi = mine * per_owner + lax.shift_right_logical(rank, 7)
        lo = rank & (LANES - 1)
        slot_ref[b : b + 1, :] = hi * LANES + lo
        value = surface[b : b + 1, :]
        coarse = (value & ~255).astype(F32)
        fine = (value & 255).astype(F32)
        at = slice(b * LANES, (b + 1) * LANES)
        lhs[0:table, at] = jnp.where(highs == hi, coarse, 0.0).astype(BF16)
        lhs[table : 2 * table, at] = jnp.where(highs == hi, fine, 0.0).astype(BF16)
        line, col = lax.div(value, cols), lax.rem(value, cols)
        code = jnp.where(col >= cols - EDGE, col - (cols - EDGE), 16 + col) + 8 * line
        rhs[0:LANES, at] = jnp.where(lows == lo, 1.0, 0.0).astype(BF16)
        rhs[LANES : LANES + 32, at] = jnp.where(iota((32, LANES), 0) == code, 1.0, 0.0).astype(BF16)
    both = dot_lanes(lhs[...], rhs[0:LANES, :])
    idx_ref[...] = both[0:table] + both[table : 2 * table]
    place = cell[...]
    row_ref[...] = lax.div(lax.rem(place, cols), LANES) * rows + lax.div(place, cols)


def shifted(tiles, lane):
    count = len(tiles)
    left = [pltpu.roll(x, LANES - 1, 1) for x in tiles]
    right = [pltpu.roll(x, 1, 1) for x in tiles]
    after = [jnp.where(lane == LANES - 1, left[(i + 1) % count], left[i]) for i in range(count)]
    before = [jnp.where(lane == 0, right[i - 1], right[i]) for i in range(count)]
    return after, before


def fetch(gas, speed, g0, s0, token, sem):
    copies = [pltpu.make_async_copy(gas, g0, sem.at[0]), pltpu.make_async_copy(speed, s0, sem.at[1])]
    for copy in copies:
        copy.start()
    token[...] = jnp.zeros_like(token)
    for copy in copies:
        copy.wait()


def tendency(v, north, south, after, before, s):
    return DIFFUSE * (south + north + after + before - 4.0 * v) - s * (v - before)


def first_section(gas, speed, w, s1, gx, sh):
    rows, cols = gas.shape
    nt = cols // LANES
    gh, speed_halo = gas_halo_tiles(w[...])
    gx[nt, ROWS : ROWS + rows, :] = gh
    sh[...] = speed_halo
    zero = jnp.zeros((ROWS, LANES), F32)
    for ct in range(nt + 1):
        gx[ct, 0:ROWS, :] = zero
        gx[ct, ROWS + rows : 2 * ROWS + rows, :] = zero
        s1[ct, 0:ROWS, :] = zero
        s1[ct, ROWS + rows : 2 * ROWS + rows, :] = zero

    def spread(i, carry):
        r0 = i * rows
        for ct in range(nt):
            gx[ct, pl.ds(ROWS + r0, rows), :] = gas[pl.ds(r0, rows), ct * LANES : (ct + 1) * LANES]
        return carry

    spread(0, 0)
    lane = iota((rows, LANES), 1)

    def body(i, carry):
        r0 = i * rows
        v = [gx[ct, pl.ds(ROWS + r0, rows), :] for ct in range(nt + 1)]
        after, before = shifted(v, lane)
        for ct in range(nt + 1):
            north = gx[ct, pl.ds(ROWS - 1 + r0, rows), :]
            south = gx[ct, pl.ds(ROWS + 1 + r0, rows), :]
            s = sh[pl.ds(r0, rows), :] if ct == nt else speed[pl.ds(r0, rows), ct * LANES : (ct + 1) * LANES]
            new = v[ct] + tendency(v[ct], north, south, after[ct], before[ct], s)
            if ct == nt:
                new = jnp.where(s > 0, new, 0.0)
            s1[ct, pl.ds(ROWS + r0, rows), :] = new
        return carry

    body(0, 0)


def gas_kernel(
    tiles_across, per_owner, gas, speed, sone, w, ra, rb, where_at, cell, owner, surface, slot, film, wall, idx, rhs,
    out, route, s1, tab, final, stage, lhs, sums, rowidx, sem,
):
    rows, cols = gas.shape
    nt = cols // LANES
    devices = route.shape[0]
    blocks = owner.shape[0]
    table = idx.shape[0]
    rows_in = pltpu.make_async_copy(where_at, rowidx, sem.at[1])
    rows_in.start()
    is_even = even("passage")
    place = lax.axis_index("passage")
    in_top = jnp.where(place > 0, 1.0, 0.0)
    in_bottom = jnp.where(place < lax.axis_size("passage") - 1, 1.0, 0.0)

    def top(row, ct):
        at = slice(ct * LANES, (ct + 1) * LANES)
        return jnp.where(is_even, rb[row : row + 1, at], ra[row : row + 1, at])

    def bottom(row, ct):
        at = slice(ct * LANES, (ct + 1) * LANES)
        return jnp.where(is_even, ra[row : row + 1, at], rb[row : row + 1, at])

    speed_halo = gas_halo_tiles(w[...])[1]
    for ct in range(nt + 1):
        up, down = DIFFUSE * top(0, ct), DIFFUSE * bottom(0, ct)
        if ct == nt:
            up = jnp.where(speed_halo[0:1] > 0, up, 0.0)
            down = jnp.where(speed_halo[rows - 1 : rows] > 0, down, 0.0)
        s1[ct, ROWS : ROWS + 1, :] = s1[ct, ROWS : ROWS + 1, :] + up
        s1[ct, ROWS + rows - 1 : ROWS + rows, :] = s1[ct, ROWS + rows - 1 : ROWS + rows, :] + down
    for ct in range(nt):
        at = slice(ct * LANES, (ct + 1) * LANES)
        s1[ct, ROWS - 1 : ROWS, :] = in_top * (top(8, ct) + DIFFUSE * gas[0:1, at])
        s1[ct, ROWS + rows : ROWS + rows + 1, :] = in_bottom * (bottom(8, ct) + DIFFUSE * gas[rows - 1 : rows, at])
    lane = iota((rows, LANES), 1)

    def second(i, carry):
        r0 = i * rows
        v = [s1[ct, pl.ds(ROWS + r0, rows), :] for ct in range(nt + 1)]
        after, before = shifted(v, lane)
        for ct in range(nt):
            north = s1[ct, pl.ds(ROWS - 1 + r0, rows), :]
            south = s1[ct, pl.ds(ROWS + 1 + r0, rows), :]
            at = slice(ct * LANES, (ct + 1) * LANES)
            g = gas[pl.ds(r0, rows), at]
            s = speed[pl.ds(r0, rows), at]
            new = 0.5 * (g + v[ct] + tendency(v[ct], north, south, after[ct], before[ct], s))
            tab[pl.ds(ct * rows + r0, rows), :] = new
            final[pl.ds(r0, rows), at] = new
        return carry

    second(0, 0)
    put = pltpu.make_async_copy(final, out, sem.at[0])
    put.start()
    rows_in.wait()
    sub = iota((ROWS, LANES), 0)
    lanes_down = iota((LANES, LANES), 0)
    highs = iota((table, LANES), 0)
    owners = iota((devices, LANES), 0)
    part = table + devices

    def gather(b):
        base = pl.multiple_of(b * LANES, LANES)
        for g in range(LANES // ROWS):
            acc = jnp.broadcast_to(tab[pl.ds(rowidx[base + g * ROWS], 1), :], (ROWS, LANES))
            for j in range(1, ROWS):
                row = tab[pl.ds(rowidx[base + g * ROWS + j], 1), :]
                acc = jnp.where(sub == j, jnp.broadcast_to(row, (ROWS, LANES)), acc)
            stage[pl.ds(base + g * ROWS, ROWS), :] = acc

    def place_heat(b):
        at = pl.ds(pl.multiple_of(b * LANES, LANES), LANES)
        one = pl.ds(b, 1)
        picked = jnp.where(lanes_down == (cell[one, :] & (LANES - 1)), stage[at, :].T, 0.0)
        face = jnp.sum(picked, axis=0, keepdims=True)
        heat = split3(film[one, :] * (face - wall[one, :]))
        place_of = slot[one, :]
        hi = lax.shift_right_logical(place_of, 7)
        mine = owner[one, :]
        voxel = surface[one, :]
        col = lax.rem(voxel, cols)
        tile = lax.rem(mine, tiles_across)
        to_right = (col >= cols - EDGE) & (tile < tiles_across - 1)
        to_left = (col < EDGE) & (tile > 0)
        dest = jnp.where(to_right, mine + 1, jnp.where(to_left, mine - 1, -1))
        for k in range(3):
            lhs[k * part : k * part + table, at] = jnp.where(highs == hi, heat[k], 0.0).astype(BF16)
            lhs[k * part + table : (k + 1) * part, at] = jnp.where(owners == dest, heat[k], 0.0).astype(BF16)

    several = 8

    def both(i, carry):
        for j in range(several):
            place_heat((i - 1) * several + j)
        for j in range(several):
            gather(i * several + j)
        return carry

    for j in range(several):
        gather(j)
    lax.fori_loop(1, blocks // several, both, 0)
    for j in range(several):
        place_heat(blocks - several + j)
    three = dot_lanes(lhs[...], rhs[...])
    sums[...] = three[0:part] + three[part : 2 * part] + three[2 * part : 3 * part]
    route[...] = jnp.zeros_like(route)
    for o in range(devices):
        own = slice(o * per_owner, (o + 1) * per_owner)
        route[o, 0:per_owner, :] = sums[own, 0:LANES]
        route[o, per_owner : 2 * per_owner, :] = idx[own, :]
        route[o, 2 * per_owner : 2 * per_owner + 1, 0:32] = sums[table + o : table + o + 1, LANES : LANES + 32]
    put.wait()


def strip_kernel(
    per_owner, recv, ra, rb, w, solid, material, token, top_ref, up_ref, ret_ref, lhs, rhs, dep, src, tabu, su, sm, sem
):
    devices = recv.shape[0]
    cols = solid.shape[1]
    nt = cols // LANES
    wide = cols + LANES
    high = 2 * nt
    copies = [
        pltpu.make_async_copy(solid.at[pl.ds(0, 2 * ROWS)], su, sem.at[0]),
        pltpu.make_async_copy(material.at[pl.ds(0, 2 * ROWS)], sm, sem.at[1]),
    ]
    for copy in copies:
        copy.start()
    highs = iota((high, LANES), 0)
    lanes_down = iota((LANES, LANES), 0)
    for d in range(devices):
        for q in range(per_owner):
            at = slice((d * per_owner + q) * LANES, (d * per_owner + q + 1) * LANES)
            heat = split3(recv[d, q : q + 1, :])
            where = recv[d, per_owner + q : per_owner + q + 1, :].astype(jnp.int32)
            hi = lax.shift_right_logical(where, 7)
            for k in range(3):
                lhs[k * high : (k + 1) * high, at] = jnp.where(highs == hi, heat[k], 0.0).astype(BF16)
            rhs[:, at] = jnp.where(lanes_down == (where & (LANES - 1)), 1.0, 0.0).astype(BF16)
    three = dot_lanes(lhs[...], rhs[...])
    dep[...] = three[0:high] + three[high : 2 * high] + three[2 * high : 3 * high]
    edges = recv[0, 2 * per_owner : 2 * per_owner + 1, :]
    for d in range(1, devices):
        edges = edges + recv[d, 2 * per_owner : 2 * per_owner + 1, :]
    src[...] = jnp.zeros_like(src)
    lane = iota((1, LANES), 1)
    for line in range(2):
        for ct in range(nt):
            src[line : line + 1, ct * LANES : (ct + 1) * LANES] = dep[line * nt + ct : line * nt + ct + 1, :]
        left = pltpu.roll(edges, LANES - EDGE - 8 * line, 1)
        right = pltpu.roll(edges, LANES - 16 - 8 * line, 1)
        src[line : line + 1, cols:wide] = jnp.where(
            lane >= LANES - EDGE, left, jnp.where(lane < EDGE, right, 0.0)
        )
    is_even = even("passage")
    row8 = iota((ROWS, wide), 0)

    def above(at):
        return jnp.where(row8 > 0, jnp.where(is_even, rb[at : at + ROWS, :], ra[at : at + ROWS, :]), 0.0)

    uh, kh = halo_tiles(w[0 : 2 * ROWS, :])
    for copy in copies:
        copy.wait()
    u = jnp.concatenate([above(0), jnp.concatenate([su[...], uh], axis=1)], axis=0)
    k0 = jnp.concatenate([above(8), jnp.concatenate([base_conductivity(sm[...]), kh], axis=1)], axis=0)
    inside = jnp.where(k0 > 0, 0.5 * SOLID_STEP, 0.0)
    source = jnp.concatenate(
        [jnp.zeros((ROWS, wide), F32), 2.0 * src[...], jnp.zeros((ROWS, wide), F32)], axis=0
    )
    high_rows = 3 * ROWS
    for _ in range(SUBSTEPS):
        k = k0 * jnp.exp(SOFTEN * u)
        across = (k + pltpu.roll(k, wide - 1, 1)) * (pltpu.roll(u, wide - 1, 1) - u)
        down = (k + pltpu.roll(k, high_rows - 1, 0)) * (pltpu.roll(u, high_rows - 1, 0) - u)
        flux = across - pltpu.roll(across, 1, 1) + down - pltpu.roll(down, 1, 0)
        u = u + inside * (flux + source)
    for j in range(EDGE):
        for ct in range(nt):
            row = ROWS - EDGE + j
            up_ref[j, ct : ct + 1, :] = u[row : row + 1, ct * LANES : (ct + 1) * LANES]
    top_ref[...] = u[ROWS : 2 * ROWS, 0:cols]
    for line in range(2):
        for ct in range(nt):
            tabu[line * nt + ct : line * nt + ct + 1, :] = top_ref[line : line + 1, ct * LANES : (ct + 1) * LANES]
    parts = jnp.concatenate(split3(tabu[...]), axis=0).astype(BF16)
    for d in range(devices):
        for q in range(per_owner):
            at = slice((d * per_owner + q) * LANES, (d * per_owner + q + 1) * LANES)
            x = dot(parts, rhs[:, at])
            x = x[0:high] + x[high : 2 * high] + x[2 * high : 3 * high]
            where = recv[d, per_owner + q : per_owner + q + 1, :].astype(jnp.int32)
            hi = lax.shift_right_logical(where, 7)
            ret_ref[d, q : q + 1, :] = jnp.sum(jnp.where(highs == hi, x, 0.0), axis=0, keepdims=True)


def bulk_kernel(is_back, start, chunk, solid, material, w, *refs):
    if is_back:
        ra, rb, _, fin, u0, m0, ua, ub, ka, kb, k0, k1, sem = refs
    else:
        out, token, u0, m0, ua, ub, ka, kb, k0, k1, fin, sem = refs
    count, cols = u0.shape
    nt = cols // LANES
    skip = ROWS if is_back else 0
    copies = []
    for g in range(count // chunk):
        here, there = pl.ds(start + g * chunk, chunk), pl.ds(g * chunk, chunk)
        copies.append(pltpu.make_async_copy(solid.at[here], u0.at[there], sem.at[0, g]))
        copies.append(pltpu.make_async_copy(material.at[here], m0.at[there], sem.at[1, g]))
    for copy in copies:
        copy.start()
    uh, kh = halo_tiles(w[start : start + count, :])
    ua[nt, ROWS : ROWS + count, :] = SCALE * uh
    k0[nt] = SHARE * kh
    zero = jnp.zeros((ROWS, LANES), F32)
    for ct in range(nt + 1):
        at = slice(ct * LANES, (ct + 1) * LANES)
        if is_back:
            is_even = even("passage")
            below = SCALE * jnp.where(is_even, ra[1:2, at], rb[1:2, at])
            below_k = SHARE * jnp.where(is_even, ra[9:10, at], rb[9:10, at]) * jnp.exp2(below)
        for u, k in ((ua, ka), (ub, kb)):
            u[ct, 0:ROWS, :] = zero
            k[ct, 0:ROWS, :] = zero
            u[ct, ROWS + count : 2 * ROWS + count, :] = zero
            k[ct, ROWS + count : 2 * ROWS + count, :] = zero
            if is_back:
                u[ct, ROWS + count : ROWS + count + 1, :] = below
                k[ct, ROWS + count : ROWS + count + 1, :] = below_k
    if not is_back:
        token[...] = zero
    edge = iota((chunk, LANES), 1) == LANES - 1

    def begin(r0):
        bases = []
        for ct in range(nt + 1):
            if ct < nt:
                at = slice(ct * LANES, (ct + 1) * LANES)
                here = SCALE * u0[pl.ds(r0, chunk), at]
                base = base_conductivity(m0[pl.ds(r0, chunk), at], SHARE)
                ua[ct, pl.ds(ROWS + r0, chunk), :] = here
                k0[ct, pl.ds(r0, chunk), :] = base
            else:
                here = ua[ct, pl.ds(ROWS + r0, chunk), :]
                base = k0[ct, pl.ds(r0, chunk), :]
            ka[ct, pl.ds(ROWS + r0, chunk), :] = base * jnp.exp2(here)
            bases.append(base)
        turned = [pltpu.roll(x, LANES - 1, 1) for x in bases]
        for ct in range(nt + 1):
            k1[ct, pl.ds(r0, chunk), :] = jnp.where(edge, turned[(ct + 1) % (nt + 1)], turned[ct])

    for g in range(count // chunk):
        copies[2 * g].wait()
        copies[2 * g + 1].wait()
        begin(g * chunk)

    def substep(u, k, nu, nk, r0, tall, final):
        lane = iota((tall, LANES), 1)
        edge = lane == LANES - 1
        at = pl.ds(ROWS + r0, tall)
        north, south = pl.ds(ROWS - 1 + r0, tall), pl.ds(ROWS + 1 + r0, tall)
        here = [u[ct, at, :] for ct in range(nt + 1)]
        cond = [k[ct, at, :] for ct in range(nt + 1)]
        turned = [pltpu.roll(x, LANES - 1, 1) for x in here]
        across = []
        for ct in range(nt + 1):
            nearby = jnp.where(edge, turned[(ct + 1) % (nt + 1)], turned[ct])
            nearby_k = k1[ct, pl.ds(r0, tall), :] * jnp.exp2(nearby)
            across.append((cond[ct] + nearby_k) * (nearby - here[ct]))
        back = [pltpu.roll(x, 1, 1) for x in across]
        for ct in range(nt if final else nt + 1):
            flux = across[ct] - jnp.where(lane == 0, back[ct - 1], back[ct])
            flux = flux + (cond[ct] + k[ct, north, :]) * (u[ct, north, :] - here[ct])
            flux = flux + (cond[ct] + k[ct, south, :]) * (u[ct, south, :] - here[ct])
            if ct == nt:
                flux = jnp.where(k0[ct, pl.ds(r0, tall), :] > 0, flux, 0.0)
            new = here[ct] + flux
            if final:
                fin[pl.ds(r0 - skip, tall), ct * LANES : (ct + 1) * LANES] = new * (1.0 / SCALE)
            else:
                nu[ct, at, :] = new
                nk[ct, at, :] = k0[ct, pl.ds(r0, tall), :] * jnp.exp2(new)

    for step in range(SUBSTEPS - 1):
        u, k, nu, nk = (ua, ka, ub, kb) if step % 2 == 0 else (ub, kb, ua, ka)
        substep(u, k, nu, nk, 0, count, False)
    last = (ua, ka, ub, kb) if SUBSTEPS % 2 == 1 else (ub, kb, ua, ka)
    if is_back:
        substep(*last, skip, count - skip, True)
        return
    outs = []
    for g in range(count // chunk):
        tall = chunk - (ROWS if (g + 1) * chunk == count else 0)
        substep(*last, g * chunk, tall, True)
        at = pl.ds(g * chunk, tall)
        outs.append(pltpu.make_async_copy(fin.at[at], out.at[at], sem.at[0, g]))
        outs[-1].start()
    for copy in outs:
        copy.wait()


def finish_kernel(recv, slot, below, back, top, solid, wall_ref, out, tabl, edge, sem):
    devices, per_owner = recv.shape[0], recv.shape[1]
    rows = solid.shape[0]
    nt = below.shape[1]
    most = back.shape[0] - ROWS
    stores = [
        pltpu.make_async_copy(top, out.at[pl.ds(0, ROWS)], sem.at[0]),
        pltpu.make_async_copy(back.at[pl.ds(0, most)], out.at[pl.ds(rows - ROWS - most, most)], sem.at[1]),
        pltpu.make_async_copy(edge, out.at[pl.ds(rows - ROWS, ROWS)], sem.at[2]),
    ]
    for store in stores[:2]:
        store.start()
    last = lax.axis_index("passage") == lax.axis_size("passage") - 1
    edge[...] = back[most : most + ROWS, :]
    for j in range(EDGE):
        row = ROWS - EDGE + j
        for ct in range(nt):
            at = slice(ct * LANES, (ct + 1) * LANES)
            edge[row : row + 1, at] = jnp.where(last, edge[row : row + 1, at], below[j, ct : ct + 1, :])
    stores[2].start()
    for d in range(devices):
        tabl[d * per_owner : (d + 1) * per_owner, :] = recv[d]
    table = tabl.shape[0]
    parts = jnp.concatenate(split3(tabl[...]), axis=0).astype(BF16)
    highs, lanes_down = iota((table, LANES), 0), iota((LANES, LANES), 0)
    for b in range(slot.shape[0]):
        place = slot[b : b + 1, :]
        lows = jnp.where(lanes_down == (place & (LANES - 1)), 1.0, 0.0).astype(BF16)
        x = dot(parts, lows)
        x = x[0:table] + x[table : 2 * table] + x[2 * table : 3 * table]
        hi = lax.shift_right_logical(place, 7)
        wall_ref[b : b + 1, :] = jnp.sum(jnp.where(highs == hi, x, 0.0), axis=0, keepdims=True)
    for store in stores:
        store.wait()


def shards(gas, gas_speed, solid, material, face_cell, face_owner, face_surface, film, wall_previous):
    passages = lax.axis_size("passage")
    tiles = lax.axis_size("tile")
    devices = passages * tiles
    rows, cols = solid.shape
    nt = cols // LANES
    faces = face_cell.shape[0]
    blocks = faces // LANES
    cap = 2 * faces // devices
    per_owner = max(1, cap // LANES)
    table = devices * per_owner
    wide = cols + LANES

    def shape(dims, kind=F32):
        return jax.ShapeDtypeStruct(dims, kind)

    def cost(flops, moved, hard=0):
        return pl.CostEstimate(flops=flops, bytes_accessed=moved, transcendentals=hard)

    one, two, edges, edge_m = pl.pallas_call(
        pack_columns,
        in_specs=[whole(pltpu.HBM)] * 4,
        out_specs=[whole()] * 4,
        out_shape=[shape((16, rows))] * 2 + [shape((6, ROWS, cols)), shape((2, ROWS, cols), jnp.int32)],
        scratch_shapes=[
            VMEM((6, rows, LANES), F32),
            VMEM((2, rows, LANES), jnp.int32),
            pltpu.SemaphoreType.DMA((2, 8)),
        ],
        compiler_params=params(52),
        name="pack_columns",
        cost_estimate=cost(1000000, 8 * rows * LANES * 4),
    )(gas, gas_speed, solid, material)
    one, two = pair_swaps("tile", tiles)(one, two)

    g0, s0, token = pl.pallas_call(
        fetch,
        in_specs=[whole(pltpu.HBM)] * 2,
        out_specs=[whole()] * 3,
        out_shape=[shape((rows, cols))] * 2 + [shape((ROWS, LANES))],
        scratch_shapes=[pltpu.SemaphoreType.DMA((2,))],
        compiler_params=params(48),
        name="fetch",
        cost_estimate=cost(0, 16 * rows * cols),
    )(gas, gas_speed)
    w, ra, rb = pl.pallas_call(
        pack_rows,
        in_specs=[whole()] * 5,
        out_specs=[whole()] * 3,
        out_shape=[shape((rows, LANES)), shape((16, wide)), shape((16, wide))],
        scratch_shapes=[VMEM((LANES, rows), F32)],
        compiler_params=params(8),
        name="pack_rows",
        cost_estimate=cost(1000000, 8 * ROWS * cols * 4),
    )(one, two, edges, edge_m, token)
    ra, rb = pair_swaps("passage", passages)(ra, rb)

    def folded(x):
        return x.reshape(blocks, LANES)

    owner, surface, cell = folded(face_owner), folded(face_surface), folded(face_cell)
    slot, rowidx, idx, lanes_of = pl.pallas_call(
        functools.partial(find_slots, devices, per_owner, rows, cols),
        in_specs=[whole()] * 3,
        out_specs=[whole()] * 4,
        out_shape=[
            shape((blocks, LANES), jnp.int32),
            shape((blocks, LANES), jnp.int32),
            shape((table, LANES)),
            shape((LANES + 32, faces), BF16),
        ],
        scratch_shapes=[
            VMEM((blocks * devices, LANES), BF16),
            VMEM((2 * table, faces), BF16),
        ],
        compiler_params=params(24),
        name="find_slots",
        cost_estimate=cost(20000000, 1000000),
    )(owner, surface, cell)

    part = table + devices
    ringed = (nt + 1, rows + 2 * ROWS, LANES)
    sone = pl.pallas_call(
        first_section,
        in_specs=[whole()] * 3,
        out_specs=whole(),
        out_shape=shape(ringed),
        scratch_shapes=[VMEM(ringed, F32), VMEM((rows, LANES), F32)],
        compiler_params=params(12),
        name="first_section",
        cost_estimate=cost(8000000, 6000000),
    )(g0, s0, w)
    gas_next, route, _ = pl.pallas_call(
        functools.partial(gas_kernel, tiles, per_owner),
        in_specs=[whole()] * 6 + [whole(pl.ANY)] + [whole()] * 8,
        out_specs=[whole(pltpu.HBM), whole(), whole()],
        out_shape=[shape((rows, cols)), shape((devices, ROUTE_ROWS, LANES)), shape(ringed)],
        input_output_aliases={2: 2},
        scratch_shapes=[
            VMEM((nt * rows, LANES), F32),
            VMEM((rows, cols), F32),
            VMEM((faces, LANES), F32),
            VMEM((3 * part, faces), BF16),
            VMEM((part, LANES + 32), F32),
            pltpu.SMEM((faces,), jnp.int32),
            pltpu.SemaphoreType.DMA((2,)),
        ],
        compiler_params=params(20),
        name="gas_and_heat",
        cost_estimate=cost(60000000, 40000000),
    )(
        g0, s0, sone, w, ra, rb, rowidx.reshape(faces), cell, owner, surface, slot,
        folded(film), folded(wall_previous), idx, lanes_of,
    )
    recv = lax.all_to_all(route, ("passage", "tile"), 0, 0, tiled=True)

    behind = rows * 3 // 8 // ROWS * ROWS
    front = rows - behind + ROWS
    chunk = front // 3 if front % (3 * ROWS) == 0 else ROWS

    def bulk_part(is_back, start, count, chunk, outs, specs, *more):
        kept = [] if is_back else [VMEM((count, cols), F32)]
        return pl.pallas_call(
            functools.partial(bulk_kernel, is_back, start, chunk),
            in_specs=[whole(pltpu.HBM)] * 2 + [whole()] * (1 + len(more)),
            out_specs=specs,
            out_shape=outs,
            scratch_shapes=[VMEM((count, cols), F32), VMEM((count, cols), jnp.int32)]
            + [VMEM((nt + 1, count + 2 * ROWS, LANES), F32)] * 4
            + [VMEM((nt + 1, count, LANES), F32)] * 2
            + kept
            + [pltpu.SemaphoreType.DMA((2, count // chunk))],
            compiler_params=params(52),
            name="solid_bulk",
            cost_estimate=cost(60000000, 30000000),
        )(solid, material, w, *more)

    bulk, token = bulk_part(
        False, 0, front, chunk, [shape((rows, cols)), shape((ROWS, LANES))], [whole(pltpu.HBM), whole()]
    )

    slots = table * LANES
    top, up, ret = pl.pallas_call(
        functools.partial(strip_kernel, per_owner),
        in_specs=[whole()] * 4 + [whole(pltpu.HBM)] * 2 + [whole()],
        out_specs=[whole()] * 3,
        out_shape=[shape((ROWS, cols)), shape((EDGE, nt, LANES)), shape((devices, per_owner, LANES))],
        scratch_shapes=[
            VMEM((6 * nt, slots), BF16),
            VMEM((LANES, slots), BF16),
            VMEM((2 * nt, LANES), F32),
            VMEM((ROWS, wide), F32),
            VMEM((2 * nt, LANES), F32),
            VMEM((2 * ROWS, cols), F32),
            VMEM((2 * ROWS, cols), jnp.int32),
            pltpu.SemaphoreType.DMA((2,)),
        ],
        compiler_params=params(52),
        name="solid_strip",
        cost_estimate=cost(20000000, 4000000),
    )(recv, ra, rb, w, solid, material, token)
    ret = lax.all_to_all(ret, ("passage", "tile"), 0, 0, tiled=True)
    below = lax.ppermute(up, "passage", [(i + 1, i) for i in range(passages - 1)])

    (back,) = bulk_part(
        True, rows - behind - ROWS, behind + ROWS, behind + ROWS, [shape((behind, cols))], [whole()], ra, rb, top
    )
    wall, solid_next = pl.pallas_call(
        finish_kernel,
        in_specs=[whole()] * 5 + [whole(pltpu.HBM)],
        out_specs=[whole(), whole(pltpu.HBM)],
        out_shape=[shape((blocks, LANES)), shape((rows, cols))],
        input_output_aliases={5: 1},
        scratch_shapes=[
            VMEM((table, LANES), F32),
            VMEM((ROWS, cols), F32),
            pltpu.SemaphoreType.DMA((3,)),
        ],
        compiler_params=params(24),
        name="wall_temperatures",
        cost_estimate=cost(20000000, 4000000),
    )(ret, slot, below, back, top, bulk)
    return gas_next, solid_next, wall.reshape(faces)


def solution(mesh):
    in_specs = (
        P("passage", "tile"),
        P("passage", "tile"),
        P("passage", "tile"),
        P("passage", "tile"),
        P(("passage", "tile")),
        P(("passage", "tile"), None),
        P(("passage", "tile")),
        P(("passage", "tile")),
        P(("passage", "tile")),
    )
    out_specs = (P("passage", "tile"), P("passage", "tile"), P(("passage", "tile")))
    return jax.shard_map(shards, mesh=mesh, in_specs=in_specs, out_specs=out_specs, check_vma=False)
```
